32 devices in a mesh: section: 2 (over core), rows: 16 (over z, y, x).
Axes of the slice: x: 2, y: 2, z: 4, core: 2. Of those that a mesh axis runs over, the one named last changes fastest.
Arguments:
- tokens: bfloat16 [4096, 768], P('rows'), may hold values from -6 to 6
- segment_ids: int32 [4096], P('rows'), may hold values from 0 to 127, never falling along the last dimension, each value on 1 to 128 neighbouring positions
- in_proj: bfloat16 [2, 2, 768, 3072], P('section'), may hold values from -0.21875 to 0.21875
- out_proj: bfloat16 [2, 3072, 768], replicated, may hold values from -0.109375 to 0.109375
- front_gain: float32 [2, 2, 768], replicated, may hold values from 0.1 to 1.9
- mixer_gain: float32 [2, 768], replicated, may hold values from 0.1 to 1.9
- feed_gain: float32 [2, 3072], replicated, may hold values from 0.1 to 1.9
- cotangent: bfloat16 [4096, 768], P('rows'), may hold values from -6 to 6
Outputs:
- layer_out: bfloat16 [4096, 768], P('rows')
- input_grad: bfloat16 [4096, 768], P('rows')
- grad_in_proj: float32 [2, 2, 768, 3072], P('section', None, None, 'rows')
- grad_out_proj: float32 [2, 3072, 768], P(None, 'rows', 'section')
- grad_front_gain: float32 [2, 2, 768], replicated
- grad_mixer_gain: float32 [2, 768], replicated
- grad_feed_gain: float32 [2, 3072], replicated
The draws below stay inside these ranges and needn't reach their ends.
All inputs are finite; a program needn't handle non-finite values.
Results may differ from the reference program's by a relative error of at most 0.02.
Values may be sent and summed in bfloat16 or wider, within the bound.
A program may use at most 320 MiB of HBM per device.

```python
import math
import jax
import jax.numpy as jnp
import numpy as np
from jax import lax

D = 768
HEAD_DIM = 64
FF = 3072
LAYERS = 2
SEQ = 128
TOK_DEV = 256
TOKENS = 4096
N_ROWS = 16


def block_scale(own_key, shape, split, low, high):
    def one(dim, blocks):
        steps = jax.random.uniform(jax.random.fold_in(jax.random.fold_in(own_key, 6), dim), (blocks,), jnp.float32, low / len(split), high / len(split))
        return jnp.repeat(jnp.exp(steps), shape[dim] // blocks).reshape((-1,) + (1,) * (len(shape) - dim - 1))

    factor_of = one(*split[0])
    for cut in split[1:]:
        factor_of = factor_of * one(*cut)
    return factor_of


def length_profile(number_of, total, limit, slope):
    loads = [(1 << 20) // math.isqrt(rank ** slope) + 1 for rank in range(2, number_of + 1)]
    surplus, counts = total - limit - (number_of - 1), [1] * (number_of - 1)
    while surplus > 0:
        free = [i for i in range(number_of - 1) if counts[i] < limit]
        mass, left = sum([loads[i] for i in free]), surplus
        for i in free:
            addition = min(limit - counts[i], max(1, left * loads[i] // mass), surplus)
            counts[i] = counts[i] + addition
            surplus = surplus - addition
    return np.array([limit] + counts)


def ragged(key, count, total, limit, lean):
    if count == 2:
        one = jax.random.randint(key, (), max(1, total - limit), min(limit, total - 1) + 1)
        return jnp.stack([one, total - one])
    lengths = jnp.asarray(length_profile(count, total, limit, lean), jnp.int32)
    twos = (count - 1) // 2
    source_of, taker = lengths[1:1 + 2 * twos:2], lengths[2:2 + 2 * twos:2]
    slack = jnp.minimum(source_of - 1, limit - taker)
    shifted = jax.random.randint(jax.random.fold_in(key, 1), (twos,), 0, 1 << 20) % (slack + 1)
    lengths = lengths.at[1:1 + 2 * twos:2].set(source_of - shifted).at[2:2 + 2 * twos:2].set(taker + shifted)
    return lengths[jax.random.permutation(jax.random.fold_in(key, 2), count)]


def centred(stream_key, extent, deviation, limit, split=(), kind=jnp.bfloat16):
    factor_of = block_scale(stream_key, extent, split, -0.22, 0.18) if split else 1.0
    result = jax.random.normal(stream_key, extent, jnp.float32) * deviation * factor_of
    return jnp.minimum(jnp.maximum(result, -limit), limit).astype(kind)


def setup_inputs(seed: int = 0) -> dict:
    streams_of = jax.random.split(jax.random.key(seed), 9)
    return {
        "tokens": centred(streams_of[0], (TOKENS, D), 1.0, 6.0, ((0, 16),)),
        "segment_ids": jnp.searchsorted(jnp.cumsum(ragged(streams_of[1], TOKENS * 4 // SEQ, TOKENS, SEQ, 2)), jnp.arange(TOKENS), side="right").astype(jnp.int32),
        "in_proj": centred(streams_of[2], (2, LAYERS, D, 4 * D), D ** -0.5, 0.21875, ((0, 2),)),
        "out_proj": centred(streams_of[3], (LAYERS, FF, D), FF ** -0.5, 0.109375),
        "front_gain": jnp.clip(1.0 + 0.18 * jax.random.normal(streams_of[4], (LAYERS, 2, D), jnp.float32), 0.1, 1.9),
        "mixer_gain": jnp.clip(1.0 + 0.18 * jax.random.normal(streams_of[5], (LAYERS, D), jnp.float32), 0.1, 1.9),
        "feed_gain": jnp.clip(1.0 + 0.18 * jax.random.normal(streams_of[6], (LAYERS, FF), jnp.float32), 0.1, 1.9),
        "cotangent": centred(streams_of[7], (TOKENS, D), 1.0, 6.0, ((0, 16),)),
    }


PRECISE = lax.Precision.HIGHEST
EPSILON = 1e-05

@jax.custom_vjp
def low(v):
    return lax.optimization_barrier(v.astype(jnp.bfloat16)).astype(jnp.float32)

@jax.custom_vjp
def low_back(v):
    return v

def low_keep(v):
    return (low(v), None)

def low_pass(kept, grad):
    return (grad,)

def back_keep(v):
    return (v, None)

def back_low(kept, grad):
    return (low(grad),)
low.defvjp(low_keep, low_pass)
low_back.defvjp(back_keep, back_low)

def layer_norm(values, gain):
    centered = values - lax.optimization_barrier(jnp.mean(values, axis=-1, keepdims=True))
    spread = lax.optimization_barrier(jnp.mean(centered * centered, axis=-1, keepdims=True))
    return centered * lax.rsqrt(spread + EPSILON) * gain

def gelu_exact(values):
    return jax.nn.gelu(values, approximate=False)

def visible(segment, seq_count):
    segment_grid = segment.reshape(seq_count, SEQ)
    position = jnp.arange(SEQ)
    causal = position[:, None] >= position[None, :]
    same_doc = segment_grid[:, :, None] == segment_grid[:, None, :]
    return jnp.logical_and(causal[None], same_doc)

def attention_branch(stream, segment, weight, gain_in, gain_mid):
    model_width = stream.shape[1]
    seq_count = stream.shape[0] // SEQ
    head_count = model_width // HEAD_DIM
    normed = low(layer_norm(low_back(stream), gain_in))
    projected = low_back(low(jnp.dot(normed, weight[:, :3 * model_width], precision=PRECISE)))
    shaped = projected.reshape(seq_count, SEQ, 3, head_count, HEAD_DIM)
    queries = shaped[:, :, 0]
    key_rows = shaped[:, :, 1]
    value_rows = shaped[:, :, 2]
    scores = jnp.einsum('bqhd,bkhd->bhqk', queries, key_rows, precision=PRECISE) * HEAD_DIM ** (-0.5)
    scores = low_back(scores)
    allowed = visible(segment, seq_count)
    scores = jnp.where(allowed[:, None], scores, -1e+30)
    row_peak = lax.optimization_barrier(jnp.max(scores, axis=-1, keepdims=True))
    weights = jnp.exp(scores - row_peak)
    attention = low(weights / lax.optimization_barrier(jnp.sum(weights, axis=-1, keepdims=True)))
    context = jnp.einsum('bhqk,bkhd->bqhd', attention, value_rows, precision=PRECISE)
    context = low_back(context.reshape(-1, model_width))
    inner_normed = low(layer_norm(context, gain_mid))
    return low(low_back(jnp.dot(inner_normed, weight[:, 3 * model_width:], precision=PRECISE)))

def feed_branch(stream, weight_in, weight_out, gain_in, gain_mid):
    normed = low(layer_norm(low_back(stream), gain_in))
    hidden = low_back(jnp.dot(normed, weight_in, precision=PRECISE))
    inner_normed = low(layer_norm(gelu_exact(hidden), gain_mid))
    return low(low_back(jnp.dot(inner_normed, weight_out, precision=PRECISE)))

def block_forward(stream, segment, in_proj, out_proj, front_gain, mixer_gain, feed_gain):
    for layer_index in range(LAYERS):
        stream = stream + attention_branch(stream, segment, in_proj[0, layer_index], front_gain[layer_index, 0], mixer_gain[layer_index])
        stream = stream + feed_branch(stream, in_proj[1, layer_index], out_proj[layer_index], front_gain[layer_index, 1], feed_gain[layer_index])
    return stream

def reference(tokens, segment_ids, in_proj, out_proj, front_gain, mixer_gain, feed_gain, cotangent):
    params = (in_proj.astype(jnp.float32), out_proj.astype(jnp.float32), front_gain.astype(jnp.float32), mixer_gain.astype(jnp.float32), feed_gain.astype(jnp.float32))
    model_width = tokens.shape[1]
    token_groups = tokens.astype(jnp.float32).reshape(N_ROWS, TOK_DEV, model_width)
    segment_groups = segment_ids.reshape(N_ROWS, TOK_DEV)
    upstream_groups = cotangent.astype(jnp.float32).reshape(N_ROWS, TOK_DEV, model_width)

    def group_step(running, inputs):
        stream, segment, upstream = inputs

        def forward(stream_in, param_set):
            return block_forward(stream_in, segment, *param_set)
        output, pullback = jax.vjp(forward, stream, params)
        stream_grad, param_grads = pullback(upstream)
        running = jax.tree.map(lambda left, right: left + right, running, param_grads)
        return (running, (output.astype(jnp.bfloat16), stream_grad.astype(jnp.bfloat16)))
    zero_grads = jax.tree.map(jnp.zeros_like, params)
    totals, (outputs, stream_grads) = lax.scan(group_step, zero_grads, (token_groups, segment_groups, upstream_groups))
    return (outputs.reshape(-1, model_width), stream_grads.reshape(-1, model_width), totals[0], totals[1], totals[2], totals[3], totals[4])
```

```python
import jax
import jax.numpy as jnp
from jax import lax
from jax.experimental import pallas as pl
from jax.experimental.pallas import tpu as pltpu
from jax.sharding import PartitionSpec as P

HEAD_DIM = 64
SEQ = 128
EPSILON = 1e-05
MESH = pl.DeviceIdType.MESH
BF = jnp.bfloat16
F32 = jnp.float32


def dot(a, b, ca, cb):
    return lax.dot_general(a, b, (((ca,), (cb,)), ((), ())), preferred_element_type=F32)


def fold(v):
    parts = [v[:, i : i + 128] for i in range(0, v.shape[1], 128)]
    total = parts[0]
    for part in parts[1:]:
        total = total + part
    return total


def hat(v):
    centered = v - jnp.mean(v, axis=-1, keepdims=True)
    rs = lax.rsqrt(jnp.mean(centered * centered, axis=-1, keepdims=True) + EPSILON)
    return centered * rs, rs


def hat_back(xh, rs, dxh):
    m1 = jnp.mean(dxh, axis=-1, keepdims=True)
    m2 = jnp.mean(dxh * xh, axis=-1, keepdims=True)
    return rs * (dxh - m1 - xh * m2)


def flip(bit, by):
    return 1 - bit if by else bit


AX, AM, AY, FX, FY, OX, OY = range(7)


def body(
    tok, seg, in_hbm, out_hbm, gf, gm, gff, cot,
    lay_o, inp_o, gi_o, go_o, gain_o,
    W, WO, XS, YS, XR, YR, R2, R3, R4, QKV, PB, CTX, ST, UP, XH, GP, RSB, BIG, HG, QG, DC, OSND, ORCV, GS, GR,
    wsem, wsend, wosem, isend, irecv, s2s, s2r, s3s, s3r, s4s, s4r, gss, gsr, tss, tsr,
):
    s = lax.axis_index("section")
    r = lax.axis_index("rows")
    x = lax.rem(r, 2)
    y = lax.rem(r // 2, 2)
    zl = lax.rem(r // 4, 2)
    zh = r // 8
    rx = r + 1 - 2 * x
    ry = r + 2 - 4 * y
    rl = r + 4 - 8 * zl
    rh = r + 8 - 16 * zh
    other = 1 - s
    pending = []

    def remote(src, dst, ssem, rsem, sec, row):
        return pltpu.make_async_remote_copy(
            src_ref=src, dst_ref=dst, send_sem=ssem, recv_sem=rsem, device_id=(sec, row), device_id_type=MESH
        )

    for l in range(2):
        for j in range(4):
            cols = pl.ds(768 * j, 768)
            pltpu.make_async_copy(in_hbm.at[0, l, :, cols], W.at[s, l, :, cols], wsem.at[s, l, j]).start()
    wo0 = pltpu.make_async_copy(out_hbm.at[0], WO, wosem.at[0])
    wo0.start()

    barrier = pltpu.get_barrier_semaphore()
    peers = [(other, r), (0, rx), (1, rx), (0, ry), (1, ry), (0, rl), (1, rl), (s, rh)]
    for peer in peers:
        pl.semaphore_signal(barrier, inc=1, device_id=peer, device_id_type=MESH)
    pl.semaphore_wait(barrier, len(peers))

    for l in range(2):
        for j in range(4):
            cols = pl.ds(768 * j, 768)
            cp = remote(in_hbm.at[0, l, :, cols], W.at[s, l, :, cols], wsend.at[l, j], wsem.at[s, l, j], other, r)
            cp.start()
            pending.append((None, cp))

    def wait_w(sec, l, j):
        cols = pl.ds(768 * j, 768)
        pltpu.make_async_copy(in_hbm.at[0, l, :, cols], W.at[sec, l, :, cols], wsem.at[sec, l, j]).wait()

    def exchange(item, l, own, far, dst, core, nb, bit, keep=None):
        k = 2 * bit + s
        n = 7 * l + item

        def start_own():
            @pl.when(s == core)
            def _():
                pltpu.make_async_copy(own, dst.at[k], irecv.at[n, k]).start()

            @pl.when(s != core)
            def _():
                remote(own, dst.at[k], isend.at[n, 0], irecv.at[n, k], core, r).start()

        def start_far():
            remote(far, dst.at[k], isend.at[n, 1], irecv.at[n, k], core, nb).start()

        cp_own = remote(own, dst.at[k], isend.at[n, 0], irecv.at[n, k], core, r)
        cp_far = remote(far, dst.at[k], isend.at[n, 1], irecv.at[n, k], core, nb)
        if keep is None:
            start_far()
            start_own()
            pending.append((None, cp_far))
            pending.append((s != core, cp_own))
        else:
            pl.when(bit == 0)(start_far)
            pl.when(bit == 1)(start_own)
            pending.append((bit == 0, cp_far))
            pending.append(((bit == 1) & (s != core), cp_own))

    def wait_item(n, dst):
        for k in range(4):
            pltpu.make_async_copy(dst.at[k], dst.at[k], irecv.at[n, k]).wait()

    def x_normed(l):
        return XS.at[l]

    def x_mixer(l):
        return XS.at[2 + l]

    def x_fnormed(l):
        return XS.at[4 + l]

    def x_branch(l):
        return XS.at[6 + l]

    xr_of = (0, 1, 3)

    def y_halves(ys, dim, bit):
        if dim == 0:
            return ys.at[:, bit], ys.at[:, 1 - bit]
        if dim == 1:
            return ys.at[:, :, bit], ys.at[:, :, 1 - bit]
        return ys.at[:, :, :, bit], ys.at[:, :, :, 1 - bit]

    def send_normed(l):
        exchange(AX, l, x_normed(l), x_normed(l), XR.at[xr_of[2 - l]], 0, rl, zl)

    def send_mixer(l):
        exchange(AM, l, x_mixer(l), x_mixer(l), XR.at[xr_of[2 - l] + 1], 0, rl, zl, keep=True)

    def send_ya(l):
        own, far = y_halves(YS.at[0, l], 0, zl)
        exchange(AY, l, own, far, YR.at[2 - l], 0, rl, zl)

    def send_fnormed(l):
        exchange(FX, l, x_fnormed(l), x_fnormed(l), XR.at[xr_of[1 - l]], 1, ry, y)

    def send_yf(l):
        own, far = y_halves(YS.at[1, l], 1, y)
        exchange(FY, l, own, far, YR.at[1 - l], 1, ry, y)

    def send_branch(l):
        slot = 0 if l == 1 else 2
        exchange(OX, l, x_branch(l), x_branch(l), XR.at[xr_of[slot]], 1 - l, rx, x)

    def send_yo(l):
        slot = 0 if l == 1 else 2
        own, far = y_halves(YS.at[2, l], 2, x)
        exchange(OY, l, own, far, YR.at[slot], 1 - l, rx, x)

    def store_y(job, l, c, block):
        turned = block.T
        zhi, zlo, yy = c // 4, lax.rem(c // 2, 2), lax.rem(c, 2)
        YS[job, l, zhi, zlo, yy, 0] = turned[:192]
        YS[job, l, zhi, zlo, yy, 1] = turned[192:]

    lane = lax.broadcasted_iota(jnp.int32, (1, 128), 1)
    mk0 = jnp.where(lane < 64, 1.0, 0.0).astype(BF)
    mk1 = jnp.where(lane < 64, 0.0, 1.0).astype(BF)

    def allowed():
        ids = jnp.broadcast_to(seg[pl.ds(s, 1), :], (128, 128))
        row = lax.broadcasted_iota(jnp.int32, (128, 128), 0)
        col = lax.broadcasted_iota(jnp.int32, (128, 128), 1)
        one = jnp.logical_and(ids == ids.T, row >= col)
        return jnp.concatenate([one, one], axis=0)

    def split0(v):
        return jnp.concatenate([v * mk0, v * mk1], axis=0)

    scale = HEAD_DIM ** (-0.5)

    def attention_forward(l):
        stream = ST[2 * l]
        xh, rs = hat(stream)
        normed = (xh * gf[l, 0:1, :]).astype(BF)
        XS[l] = normed
        send_normed(l)
        for j in range(3):
            wait_w(0, l, j)
            for i in range(2):
                c = 768 * j + 384 * i
                part = dot(XS[l], W[0, l, :, c : c + 384], 1, 0).astype(BF)
                for p in range(3):
                    QKV[l, c // 128 + p] = part[:, 128 * p : 128 * p + 128]
        visible = allowed()

        def pair(p):
            q, k, v = QKV[l, p], QKV[l, 6 + p], QKV[l, 12 + p]
            scores = dot(split0(q), k, 1, 1) * scale
            scores = jnp.where(visible, scores, -1e30)
            e = jnp.exp(scores - jnp.max(scores, axis=-1, keepdims=True))
            probs = e * (1.0 / jnp.sum(e, axis=-1, keepdims=True))
            low = probs.astype(BF)
            PB[l, p] = low
            both = jnp.concatenate([low[:128], low[128:]], axis=1)
            return dot(both, split0(v), 1, 0)

        for p in range(6):
            CTX[l, :, 128 * p : 128 * p + 128] = pair(p)
        xh, rs = hat(CTX[l])
        XS[2 + l] = (xh * gm[l : l + 1, :]).astype(BF)
        send_mixer(l)
        wait_w(0, l, 3)
        branch = dot(XS[2 + l], W[0, l, :, 2304:], 1, 0).astype(BF)
        ST[2 * l + 1] = stream + branch.astype(F32)

    def feed_forward(l):
        stream = ST[2 * l + 1]
        xh, rs = hat(stream)
        XS[4 + l] = (xh * gf[l, 1:2, :]).astype(BF)
        send_fnormed(l)

        def hidden(j, total):
            for i in range(2):
                c = pl.ds(pl.multiple_of(768 * j + 384 * i, 384), 384)
                h = dot(XS[4 + l], W[1, l, :, c], 1, 0)
                phi = 0.5 + 0.5 * lax.erf(h * (0.5**0.5))
                act = h * phi
                BIG[:, c] = act
                GP[l, :, c] = (phi + h * (jnp.exp(-0.5 * h * h) * 0.3989422804014327)).astype(BF)
                total = total + fold(act)
            return total

        total = jnp.zeros((128, 128), F32)
        for j in range(4):
            wait_w(1, l, j)
            total = hidden(j, total)
        width = 3072.0
        mu = jnp.sum(total, axis=-1, keepdims=True) / width

        def spread(c, acc):
            cen = BIG[:, pl.ds(pl.multiple_of(384 * c, 384), 384)] - mu
            return acc + fold(cen * cen)

        acc = lax.fori_loop(0, 8, spread, jnp.zeros((128, 128), F32))
        rs = lax.rsqrt(jnp.sum(acc, axis=-1, keepdims=True) / width + EPSILON)
        RSB[l] = jnp.broadcast_to(rs, (128, 128))

        def scaled(c, carry):
            cols = pl.ds(pl.multiple_of(384 * c, 384), 384)
            xh = (BIG[:, cols] - mu) * rs
            XH[l, :, cols] = xh.astype(BF)
            inner = (xh * gff[l : l + 1, cols]).astype(BF)
            HG[:, cols] = inner
            store_y(2, l, c, inner)
            return carry

        lax.fori_loop(0, 8, scaled, 0)
        send_yo(l)
        if l == 0:
            wo0.wait()
        else:
            wo1.wait()
        for n in range(0, 768, 256):
            branch = dot(HG[...], WO[:, n : n + 256], 1, 0).astype(BF)
            ST[2 * l + 2, :, n : n + 256] = stream[:, n : n + 256] + branch.astype(F32)

    def feed_backward(l):
        def first(c, carry):
            a1, a2 = carry
            for i in range(2):
                at = 384 * (2 * c + i)
                cols = pl.ds(pl.multiple_of(at, 384), 384)
                ig = dot(XS[6 + l], WO[cols, :], 1, 1)
                xh = XH[l, :, cols].astype(F32)
                GS[0, pl.ds(6 + 4 * l + c, 1), 384 * i : 384 * i + 384] = jnp.sum(ig * xh, axis=0, keepdims=True)
                dxh = ig * gff[l : l + 1, cols]
                BIG[:, cols] = dxh
                a1 = a1 + fold(dxh)
                a2 = a2 + fold(dxh * xh)
            return a1, a2

        zero = jnp.zeros((128, 128), F32)
        a1, a2 = lax.fori_loop(0, 4, first, (zero, zero))
        m1 = jnp.sum(a1, axis=-1, keepdims=True) / 3072.0
        m2 = jnp.sum(a2, axis=-1, keepdims=True) / 3072.0
        rs = RSB[l][:, 0:1]

        def second(c, carry):
            cols = pl.ds(pl.multiple_of(384 * c, 384), 384)
            da = rs * (BIG[:, cols] - m1 - XH[l, :, cols].astype(F32) * m2)
            hg = (GP[l, :, cols].astype(F32) * da).astype(BF)
            HG[:, cols] = hg
            store_y(1, l, c, hg)
            return carry

        lax.fori_loop(0, 8, second, 0)
        send_yf(l)
        for n in range(0, 768, 256):
            BIG[:, n : n + 256] = dot(HG[...], W[1, l, n : n + 256, :], 1, 1)
        front_back(l, 1)

    def front_back(l, sub):
        ng = BIG[:, 0:768]
        xh, rs = hat(ST[2 * l + sub])
        GS[0, 2 * l + sub : 2 * l + sub + 1, :] = jnp.sum(ng * xh, axis=0, keepdims=True)
        UP[...] = UP[...] + hat_back(xh, rs, ng * gf[l, sub : sub + 1, :]).astype(BF).astype(F32)

    def attention_backward(l):
        low = UP[...].astype(BF)
        QG[:, 2304:] = low
        for i in range(2):
            store_y(0, l, 6 + i, low[:, 384 * i : 384 * i + 384])
        for n in range(0, 768, 256):
            BIG[:, n : n + 256] = dot(low, W[0, l, n : n + 256, 2304:], 1, 1)
        ig = BIG[:, 0:768]
        xh, rs = hat(CTX[l])
        GS[0, 4 + l : 5 + l, :] = jnp.sum(ig * xh, axis=0, keepdims=True)
        dctx = hat_back(xh, rs, ig * gm[l : l + 1, :]).astype(BF)
        for p in range(6):
            DC[p] = dctx[:, 128 * p : 128 * p + 128]

        def pair(p):
            q, k, v = QKV[l, p], QKV[l, 6 + p], QKV[l, 12 + p]
            probs_low = PB[l, p]
            probs = probs_low.astype(F32)
            dcc = split0(DC[p])
            pg = dot(dcc, v, 1, 1)
            ds = (probs * (pg - jnp.sum(probs * pg, axis=-1, keepdims=True))).astype(BF)
            both = jnp.concatenate([ds[:128], ds[128:]], axis=1)
            dq = dot(both, split0(k), 1, 0) * scale
            dk = dot(ds, split0(q), 0, 0) * scale
            dv = dot(probs_low, dcc, 0, 0)
            return dq.astype(BF), dk.astype(BF), dv.astype(BF)

        def group(g):
            parts = [pair(3 * g + i) for i in range(3)]
            for which in range(3):
                block = jnp.concatenate([part[which] for part in parts], axis=1)
                at = 768 * which + 384 * g
                QG[:, at : at + 384] = block
                store_y(0, l, 2 * which + g, block)

        group(0)
        group(1)
        send_ya(l)
        for n in range(0, 768, 256):
            BIG[:, n : n + 256] = dot(QG[:, 0:2304], W[0, l, n : n + 256, 0:2304], 1, 1)
        front_back(l, 0)

    def g_at(slot, n):
        n = n + 8 if slot == 1 else n
        sec = 1 if slot < 2 else 0
        return W.at[sec, 1, pl.ds(192 * (n // 4), 192), pl.ds(768 * (n % 4), 768)]

    def job_wait(slot):
        if slot == 0:
            nx, ny = jnp.where(s == 0, 7 + OX, 7 + FX), jnp.where(s == 0, 7 + OY, 7 + FY)
        elif slot == 1:
            nx, ny = jnp.where(s == 0, 7 + AX, FX), jnp.where(s == 0, 7 + AY, FY)
        else:
            nx, ny = jnp.where(s == 0, AX, OX), jnp.where(s == 0, AY, OY)
        wait_item(nx, XR.at[xr_of[slot]])
        wait_item(ny, YR.at[slot])
        if slot > 0:

            @pl.when((s == 0) & (zl == 1))
            def _():
                wait_item(7 * (2 - slot) + AM, XR.at[xr_of[slot] + 1])

    d2_row = (jnp.where(s == 0, ry, rx), rx, ry)
    d3_row = (rl, jnp.where(s == 0, ry, rl), jnp.where(s == 0, rx, rl))

    def job_index(slot, r2, r3):
        if slot == 0:
            return flip(zl, r3), flip(jnp.where(s == 0, y, x), r2)
        if slot == 1:
            return flip(jnp.where(s == 0, y, zl), r3), flip(x, r2)
        return (
            jnp.where(s == 0, flip(y, r2), flip(zl, r3)),
            jnp.where(s == 0, flip(x, r3), flip(y, r2)),
        )

    def job(slot):
        job_wait(slot)
        for r2, r4 in ((1, 1), (1, 0), (0, 1), (0, 0)):
            h = flip(zh, r4)
            if slot == 0:
                xi = 0
            else:
                xi = jnp.where(s == 0, zl * h, 0) + xr_of[slot]
            rows = []
            for r3 in (1, 0):
                i1, i2 = job_index(slot, r2, r3)
                rows.append(jnp.concatenate([YR[slot, k, h, i1, i2] for k in range(4)], axis=1))
            lhs = jnp.concatenate(rows, axis=0)
            for n in range(0, 768, 256):
                if slot == 0:
                    rhs = XR[0, :, :, n : n + 256]
                else:
                    rhs = XR[xi, :, :, n : n + 256]
                res = dot(lhs, rhs.reshape(512, 256), 1, 0).astype(BF)
                for q, r3 in enumerate((1, 0)):
                    g_at(slot, 4 * r2 + 2 * r3 + r4)[:, n : n + 256] = res[192 * q : 192 * q + 192]
            if r2 == 1:
                for r3 in (1, 0):
                    at = 2 * r3 + r4
                    cp = remote(
                        g_at(slot, 4 + at), R2.at[slot, at], s2s.at[slot, at], s2r.at[slot, at], s, d2_row[slot]
                    )
                    cp.start()
                    pending.append((None, cp))

    def stage2(slot):
        for r3, r4 in ((1, 1), (1, 0), (0, 1), (0, 0)):
            at = 2 * r3 + r4
            pltpu.make_async_copy(R2.at[slot, at], R2.at[slot, at], s2r.at[slot, at]).wait()
            g = g_at(slot, at)
            g[...] = (g[...].astype(F32) + R2[slot, at].astype(F32)).astype(BF)
            if r3 == 1:
                cp = remote(g, R3.at[slot, r4], s3s.at[slot, r4], s3r.at[slot, r4], s, d3_row[slot])
                cp.start()
                pending.append((None, cp))

    def stage3(slot):
        for r4 in (1, 0):
            pltpu.make_async_copy(R3.at[slot, r4], R3.at[slot, r4], s3r.at[slot, r4]).wait()
            g = g_at(slot, r4)
            g[...] = (g[...].astype(F32) + R3[slot, r4].astype(F32)).astype(BF)
            if r4 == 1:
                cp = remote(g, R4.at[slot], s4s.at[slot], s4r.at[slot], s, rh)
                cp.start()
                pending.append((None, cp))

    def stage4(slot):
        pltpu.make_async_copy(R4.at[slot], R4.at[slot], s4r.at[slot]).wait()
        g = g_at(slot, 0)

        def final(lo, hi):
            return g[:, lo:hi].astype(F32) + R4[slot, :, lo:hi].astype(F32)

        if slot == 1:
            gi_o[1 - s] = final(0, 768)
            return
        core = 0 if slot == 0 else 1
        layer = 1 if slot == 0 else 0

        @pl.when(s == core)
        def _():
            own, away = (0, 384) if core == 0 else (384, 0)
            OSND[...] = final(away, away + 384).astype(BF)
            remote(OSND, ORCV, tss.at[2], tsr.at[2], other, r).start()
            go_o[layer] = final(own, own + 384)

        @pl.when(s != core)
        def _():
            gi_o[layer] = final(0, 768)

    def o_receive():
        cp = remote(OSND, ORCV, tss.at[2], tsr.at[2], other, r)
        cp.wait_recv()
        go_o[s * 0 + (1 - other)] = ORCV[...].astype(F32)
        cp.wait_send()

    def gain_stage(k):
        to = ((other, r), (s, rx), (s, ry), (s, rl), (s, rh))[k]
        return remote(GS.at[k], GR.at[k], gss.at[k], gsr.at[k], *to)

    me = pl.ds(pl.multiple_of(s * 128, 128), 128)
    ST[0] = tok[me, :].astype(F32)
    XS[7] = cot[me, :]
    UP[...] = cot[me, :].astype(F32)
    send_branch(1)
    GS[0, 14:16, :] = jnp.zeros((2, 768), F32)

    wo1 = pltpu.make_async_copy(out_hbm.at[1], WO, wosem.at[1])
    wo2 = pltpu.make_async_copy(out_hbm.at[0], WO, wosem.at[2])

    attention_forward(0)
    feed_forward(0)
    wo1.start()
    attention_forward(1)
    feed_forward(1)
    lay_o[me, :] = ST[4].astype(BF)
    lay_cp = remote(lay_o.at[me, :], lay_o.at[me, :], tss.at[0], tsr.at[0], other, r)
    lay_cp.start()

    feed_backward(1)
    wo2.start()
    attention_backward(1)
    job(0)
    XS[6] = UP[...].astype(BF)
    send_branch(0)
    wo2.wait()
    feed_backward(0)
    pl.when(s == 0)(lambda: None)
    job(1)
    attention_backward(0)
    inp_o[me, :] = UP[...].astype(BF)
    inp_cp = remote(inp_o.at[me, :], inp_o.at[me, :], tss.at[1], tsr.at[1], other, r)
    inp_cp.start()
    gain_stage(0).start()
    stage2(0)
    stage3(0)
    for k in range(2):
        gain_stage(k).wait_recv()
        GS[k + 1] = GS[k] + GR[k]
        gain_stage(k + 1).start()
    stage2(1)
    job(2)
    stage4(0)
    stage3(1)
    for k in range(2, 4):
        gain_stage(k).wait_recv()
        GS[k + 1] = GS[k] + GR[k]
        gain_stage(k + 1).start()
    stage4(1)
    stage2(2)
    stage3(2)
    gain_stage(4).wait_recv()
    gain_o[...] = GS[4] + GR[4]
    stage4(2)
    o_receive()
    for k in range(5):
        gain_stage(k).wait_send()
    other_half = pl.ds(pl.multiple_of(other * 128, 128), 128)
    remote(lay_o.at[other_half, :], lay_o.at[other_half, :], tss.at[0], tsr.at[0], other, r).wait_recv()
    remote(inp_o.at[other_half, :], inp_o.at[other_half, :], tss.at[1], tsr.at[1], other, r).wait_recv()
    lay_cp.wait_send()
    inp_cp.wait_send()
    for cond, cp in pending:
        if cond is None:
            cp.wait_send()
        else:
            pl.when(cond)(cp.wait_send)


def fused(tokens, segment_ids, in_proj, out_proj, front_gain, mixer_gain, feed_gain, cotangent):
    vm = pl.BlockSpec(memory_space=pltpu.VMEM)
    hbm = pl.BlockSpec(memory_space=pl.ANY)
    dma = pltpu.SemaphoreType.DMA
    outs = pl.pallas_call(
        body,
        out_shape=(
            jax.ShapeDtypeStruct((256, 768), BF),
            jax.ShapeDtypeStruct((256, 768), BF),
            jax.ShapeDtypeStruct((2, 192, 768), F32),
            jax.ShapeDtypeStruct((2, 192, 384), F32),
            jax.ShapeDtypeStruct((16, 768), F32),
        ),
        in_specs=[vm, vm, hbm, hbm, vm, vm, vm, vm],
        out_specs=(vm, vm, vm, vm, vm),
        scratch_shapes=[
            pltpu.VMEM((2, 2, 768, 3072), BF),
            pltpu.VMEM((3072, 768), BF),
            pltpu.VMEM((8, 128, 768), BF),
            pltpu.VMEM((3, 2, 2, 2, 2, 2, 192, 128), BF),
            pltpu.VMEM((5, 4, 128, 768), BF),
            pltpu.VMEM((3, 4, 2, 2, 2, 192, 128), BF),
            pltpu.VMEM((3, 4, 192, 768), BF),
            pltpu.VMEM((3, 2, 192, 768), BF),
            pltpu.VMEM((3, 192, 768), BF),
            pltpu.VMEM((2, 18, 128, 128), BF),
            pltpu.VMEM((2, 6, 256, 128), BF),
            pltpu.VMEM((2, 128, 768), F32),
            pltpu.VMEM((5, 128, 768), F32),
            pltpu.VMEM((128, 768), F32),
            pltpu.VMEM((2, 128, 3072), BF),
            pltpu.VMEM((2, 128, 3072), BF),
            pltpu.VMEM((2, 128, 128), F32),
            pltpu.VMEM((128, 3072), F32),
            pltpu.VMEM((128, 3072), BF),
            pltpu.VMEM((128, 3072), BF),
            pltpu.VMEM((6, 128, 128), BF),
            pltpu.VMEM((192, 384), BF),
            pltpu.VMEM((192, 384), BF),
            pltpu.VMEM((5, 16, 768), F32),
            pltpu.VMEM((5, 16, 768), F32),
            dma((2, 2, 4)),
            dma((2, 4)),
            dma((3,)),
            dma((14, 2)),
            dma((14, 4)),
            dma((3, 4)),
            dma((3, 4)),
            dma((3, 2)),
            dma((3, 2)),
            dma((3,)),
            dma((3,)),
            dma((5,)),
            dma((5,)),
            dma((3,)),
            dma((3,)),
        ],
        compiler_params=pltpu.CompilerParams(
            collective_id=0, has_side_effects=True, vmem_limit_bytes=63 * 2**20
        ),
        name="layers",
    )(
        tokens,
        segment_ids.reshape(2, SEQ),
        in_proj,
        out_proj,
        front_gain,
        mixer_gain,
        feed_gain,
        cotangent,
    )
    layer_out, input_grad, in_turned, out_grad, gains = outs
    return (
        layer_out,
        input_grad,
        jnp.swapaxes(in_turned, 1, 2)[None],
        out_grad,
        gains[0:4].reshape(2, 2, 768),
        gains[4:6],
        gains[6:14].reshape(2, 3072),
    )


def passed_along(array, axis, by):
    devices = lax.axis_size(axis)
    pairs = [(i, i + by) for i in range(devices) if 0 <= i + by < devices]
    return lax.ppermute(array, axis, pairs)


def layer_norm(values, gain):
    centered = values - jnp.mean(values, axis=-1, keepdims=True)
    spread = jnp.mean(centered * centered, axis=-1, keepdims=True)
    return centered * lax.rsqrt(spread + EPSILON) * gain


def gelu_exact(values):
    return jax.nn.gelu(values, approximate=False)


def visible(segment, seq_count):
    segment_grid = segment.reshape(seq_count, SEQ)
    position = jnp.arange(SEQ)
    causal = position[:, None] >= position[None, :]
    same_doc = segment_grid[:, :, None] == segment_grid[:, None, :]
    return jnp.logical_and(causal[None], same_doc)


def attention_forward(stream, segment, weight, gain_in, gain_mid):
    model_width = stream.shape[1]
    seq_count = stream.shape[0] // SEQ
    head_count = model_width // HEAD_DIM
    normed = layer_norm(stream, gain_in).astype(jnp.bfloat16)
    projected = jnp.dot(
        normed, weight[:, : 3 * model_width], preferred_element_type=jnp.float32
    ).astype(jnp.bfloat16)
    shaped = projected.reshape(seq_count, SEQ, 3, head_count, HEAD_DIM)
    queries = shaped[:, :, 0]
    key_rows = shaped[:, :, 1]
    value_rows = shaped[:, :, 2]
    scores = jnp.einsum(
        "bqhd,bkhd->bhqk", queries, key_rows, preferred_element_type=jnp.float32
    ) * HEAD_DIM ** (-0.5)
    allowed = visible(segment, seq_count)
    scores = jnp.where(allowed[:, None], scores, -1e30)
    row_peak = jnp.max(scores, axis=-1, keepdims=True)
    weights = jnp.exp(scores - row_peak)
    attention = weights / jnp.sum(weights, axis=-1, keepdims=True)
    attention_low = attention.astype(jnp.bfloat16)
    context = jnp.einsum(
        "bhqk,bkhd->bqhd", attention_low, value_rows, preferred_element_type=jnp.float32
    )
    context = context.reshape(-1, model_width)
    inner_normed = layer_norm(context, gain_mid).astype(jnp.bfloat16)
    branch = jnp.dot(
        inner_normed, weight[:, 3 * model_width :], preferred_element_type=jnp.float32
    ).astype(jnp.bfloat16)
    return (
        branch,
        (normed, queries, key_rows, value_rows, attention, attention_low, context, inner_normed),
    )


def attention_backward(stream, segment, weight, gain_in, gain_mid, upstream):
    model_width = stream.shape[1]
    seq_count = stream.shape[0] // SEQ
    head_count = model_width // HEAD_DIM
    scale = HEAD_DIM ** (-0.5)
    branch, kept = attention_forward(stream, segment, weight, gain_in, gain_mid)
    normed, queries, key_rows, value_rows, attention, attention_low, context, inner_normed = kept
    branch_grad = upstream.astype(jnp.bfloat16)
    out_weight_grad = jnp.einsum(
        "tc,td->cd", inner_normed, branch_grad, preferred_element_type=jnp.float32
    )
    inner_grad = jnp.einsum(
        "td,cd->tc", branch_grad, weight[:, 3 * model_width :], preferred_element_type=jnp.float32
    )
    unused_value, mid_pull = jax.vjp(layer_norm, context, gain_mid)
    context_grad, mid_gain_grad = mid_pull(inner_grad)
    context_low = context_grad.astype(jnp.bfloat16).reshape(seq_count, SEQ, head_count, HEAD_DIM)
    prob_grad = jnp.einsum(
        "bqhd,bkhd->bhqk", context_low, value_rows, preferred_element_type=jnp.float32
    )
    value_grad = jnp.einsum(
        "bhqk,bqhd->bkhd", attention_low, context_low, preferred_element_type=jnp.float32
    )
    score_grad = attention * (prob_grad - jnp.sum(attention * prob_grad, axis=-1, keepdims=True))
    score_low = score_grad.astype(jnp.bfloat16)
    query_grad = (
        jnp.einsum("bhqk,bkhd->bqhd", score_low, key_rows, preferred_element_type=jnp.float32)
        * scale
    )
    key_grad = (
        jnp.einsum("bhqk,bqhd->bkhd", score_low, queries, preferred_element_type=jnp.float32)
        * scale
    )
    projected_grad = jnp.stack([query_grad, key_grad, value_grad], axis=2).astype(jnp.bfloat16)
    projected_grad = projected_grad.reshape(-1, 3 * model_width)
    in_weight_grad = jnp.einsum(
        "tc,td->cd", normed, projected_grad, preferred_element_type=jnp.float32
    )
    normed_grad = jnp.einsum(
        "td,cd->tc",
        projected_grad,
        weight[:, : 3 * model_width],
        preferred_element_type=jnp.float32,
    )
    unused_front, front_pull = jax.vjp(layer_norm, stream, gain_in)
    stream_grad, front_gain_grad = front_pull(normed_grad)
    weight_grad = jnp.concatenate([in_weight_grad, out_weight_grad], axis=1)
    return (stream_grad.astype(jnp.bfloat16), weight_grad, front_gain_grad, mid_gain_grad)


def feed_forward(stream, weight_in, weight_out, gain_in, gain_mid):
    normed = layer_norm(stream, gain_in).astype(jnp.bfloat16)
    hidden = jnp.dot(normed, weight_in, preferred_element_type=jnp.float32)
    activated = gelu_exact(hidden)
    inner_normed = layer_norm(activated, gain_mid).astype(jnp.bfloat16)
    branch = jnp.dot(inner_normed, weight_out, preferred_element_type=jnp.float32).astype(
        jnp.bfloat16
    )
    return (branch, (normed, hidden, activated, inner_normed))


def feed_backward(stream, weight_in, weight_out, gain_in, gain_mid, upstream):
    branch, kept = feed_forward(stream, weight_in, weight_out, gain_in, gain_mid)
    normed, hidden, activated, inner_normed = kept
    branch_grad = upstream.astype(jnp.bfloat16)
    out_weight_grad = jnp.einsum(
        "tc,td->cd", inner_normed, branch_grad, preferred_element_type=jnp.float32
    )
    inner_grad = jnp.einsum(
        "td,cd->tc", branch_grad, weight_out, preferred_element_type=jnp.float32
    )
    unused_value, mid_pull = jax.vjp(layer_norm, activated, gain_mid)
    act_grad, mid_gain_grad = mid_pull(inner_grad)
    unused_act, gelu_pull = jax.vjp(gelu_exact, hidden)
    hidden_grad = gelu_pull(act_grad)[0].astype(jnp.bfloat16)
    in_weight_grad = jnp.einsum(
        "tc,td->cd", normed, hidden_grad, preferred_element_type=jnp.float32
    )
    normed_grad = jnp.einsum(
        "td,cd->tc", hidden_grad, weight_in, preferred_element_type=jnp.float32
    )
    unused_front, front_pull = jax.vjp(layer_norm, stream, gain_in)
    stream_grad, front_gain_grad = front_pull(normed_grad)
    return (
        stream_grad.astype(jnp.bfloat16),
        in_weight_grad,
        out_weight_grad,
        front_gain_grad,
        mid_gain_grad,
    )


def accumulate(store, label, value):
    if label in store:
        store[label] = store[label] + value
    else:
        store[label] = value


def generic(tokens, segment_ids, in_proj, out_proj, front_gain, mixer_gain, feed_gain, cotangent):
    own_section = lax.axis_index("section")
    own_weights = in_proj[0]
    layer_total = own_weights.shape[0]
    model_width = front_gain.shape[2]
    hidden_width = feed_gain.shape[1]
    in_store = {}
    out_store = {}
    front_store = {}
    mixer_store = {}
    feed_store = {}

    def run_forward(sublayer, layer_index, stream, segment):
        if sublayer == 0:
            return attention_forward(
                stream,
                segment,
                own_weights[layer_index],
                front_gain[layer_index, 0],
                mixer_gain[layer_index],
            )[0]
        return feed_forward(
            stream,
            own_weights[layer_index],
            out_proj[layer_index],
            front_gain[layer_index, 1],
            feed_gain[layer_index],
        )[0]

    def resting_grads(stream):
        return (
            jnp.zeros(stream.shape, jnp.bfloat16),
            jnp.zeros(own_weights.shape[1:], jnp.float32),
            jnp.zeros(out_proj.shape[1:], jnp.float32),
            jnp.zeros((model_width,), jnp.float32),
            jnp.zeros((model_width,), jnp.float32),
            jnp.zeros((hidden_width,), jnp.float32),
        )

    def run_backward(sublayer, layer_index, stream, segment, upstream):
        if sublayer == 0:
            stream_grad, weight_grad, front_grad, mid_grad = attention_backward(
                stream,
                segment,
                own_weights[layer_index],
                front_gain[layer_index, 0],
                mixer_gain[layer_index],
                upstream,
            )
            return (
                stream_grad,
                weight_grad,
                jnp.zeros(out_proj.shape[1:], jnp.float32),
                front_grad,
                mid_grad,
                jnp.zeros((hidden_width,), jnp.float32),
            )
        stream_grad, in_grad, out_grad, front_grad, mid_grad = feed_backward(
            stream,
            own_weights[layer_index],
            out_proj[layer_index],
            front_gain[layer_index, 1],
            feed_gain[layer_index],
            upstream,
        )
        return (
            stream_grad,
            in_grad,
            out_grad,
            front_grad,
            jnp.zeros((model_width,), jnp.float32),
            mid_grad,
        )

    stream = tokens.astype(jnp.float32)
    upstream = cotangent.astype(jnp.float32)
    kept_streams = []
    for layer_index in range(layer_total):
        for sublayer in (0, 1):
            kept_streams.append(stream)

            def active_forward(stream_in):
                return run_forward(sublayer, layer_index, stream_in, segment_ids)

            def resting_forward(stream_in):
                return jnp.zeros(stream_in.shape, jnp.bfloat16)

            own_branch = lax.cond(own_section == sublayer, active_forward, resting_forward, stream)
            if sublayer == 0:
                received = passed_along(own_branch, "section", 1)
            else:
                received = passed_along(own_branch, "section", -1)
            stream = stream + jnp.where(own_section == sublayer, own_branch, received).astype(
                jnp.float32
            )
    for position in reversed(range(2 * layer_total)):
        layer_index, sublayer = divmod(position, 2)

        def active_backward(operand):
            return run_backward(sublayer, layer_index, operand[0], segment_ids, operand[1])

        def resting_backward(operand):
            return resting_grads(operand[0])

        grads = lax.cond(
            own_section == sublayer,
            active_backward,
            resting_backward,
            (kept_streams[position], upstream),
        )
        own_grad = grads[0]
        accumulate(in_store, layer_index, grads[1])
        accumulate(out_store, layer_index, grads[2])
        accumulate(front_store, (layer_index, sublayer), grads[3])
        accumulate(mixer_store, layer_index, grads[4])
        accumulate(feed_store, layer_index, grads[5])
        if sublayer == 0:
            received = passed_along(own_grad, "section", 1)
        else:
            received = passed_along(own_grad, "section", -1)
        upstream = upstream + jnp.where(own_section == sublayer, own_grad, received).astype(
            jnp.float32
        )
    in_total = jnp.stack([in_store[layer_index] for layer_index in range(layer_total)])
    out_total = jnp.stack([out_store[layer_index] for layer_index in range(layer_total)])
    front_total = jnp.stack(
        [
            jnp.stack([front_store[layer_index, 0], front_store[layer_index, 1]])
            for layer_index in range(layer_total)
        ]
    )
    mixer_total = jnp.stack([mixer_store[layer_index] for layer_index in range(layer_total)])
    feed_total = jnp.stack([feed_store[layer_index] for layer_index in range(layer_total)])
    first_grad = lax.psum_scatter(in_total[None], "rows", scatter_dimension=3, tiled=True)
    partial_sum = lax.psum_scatter(
        out_total.astype(jnp.bfloat16), "section", scatter_dimension=2, tiled=True
    ).astype(jnp.float32)
    second_grad = lax.psum_scatter(partial_sum, "rows", scatter_dimension=1, tiled=True)
    gain_totals = lax.psum((front_total, mixer_total, feed_total), ("section", "rows"))
    return (
        stream.astype(jnp.bfloat16),
        upstream.astype(jnp.bfloat16),
        first_grad,
        second_grad,
        gain_totals[0],
        gain_totals[1],
        gain_totals[2],
    )


def solution(mesh):
    local = fused if mesh.shape["rows"] == 16 and mesh.shape["section"] == 2 else generic
    return jax.shard_map(
        local,
        mesh=mesh,
        in_specs=(
            P("rows", None),
            P("rows"),
            P("section", None, None, None),
            P(),
            P(),
            P(),
            P(),
            P("rows", None),
        ),
        out_specs=(
            P("rows", None),
            P("rows", None),
            P("section", None, None, "rows"),
            P(None, "rows", "section"),
            P(),
            P(),
            P(),
        ),
        check_vma=False,
    )
```

```python
import jax
import jax.numpy as jnp
from jax import lax
from jax.experimental import pallas as pl
from jax.experimental.pallas import tpu as pltpu
from jax.sharding import PartitionSpec as P

HEAD_DIM = 64
SEQ = 128
EPSILON = 1e-05
MESH = pl.DeviceIdType.MESH
BF = jnp.bfloat16
F32 = jnp.float32


def dot(a, b, ca, cb):
    return lax.dot_general(a, b, (((ca,), (cb,)), ((), ())), preferred_element_type=F32)


def fold(v):
    parts = [v[:, i : i + 128] for i in range(0, v.shape[1], 128)]
    total = parts[0]
    for part in parts[1:]:
        total = total + part
    return total


def hat(v):
    centered = v - jnp.mean(v, axis=-1, keepdims=True)
    rs = lax.rsqrt(jnp.mean(centered * centered, axis=-1, keepdims=True) + EPSILON)
    return centered * rs, rs


def hat_back(xh, rs, dxh):
    m1 = jnp.mean(dxh, axis=-1, keepdims=True)
    m2 = jnp.mean(dxh * xh, axis=-1, keepdims=True)
    return rs * (dxh - m1 - xh * m2)


def flip(bit, by):
    return 1 - bit if by else bit


AX, AM, AY = range(3)


def body(
    tok, seg, in_hbm, out_hbm, gf, gm, gff, cot,
    lay_o, inp_o, gi_o, go_o, gain_o,
    W, WO, XS, YS, XR, YR, R2, R3, R4, FN, BG, SR, FI, FG, RC, RX, RH,
    QKV, PB, CTX, ST, UP, XH, GP, RSB, BIG, HG, ORCV, GS, GR,
    wsem, wsend, wosem, isend, irecv, s2s, s2r, s3s, s3r, s4s, s4r,
    fsend, frecv, f1s, f1r, f2s, f2r, f3s, f3r, gss, gsr, tss, tsr, tksem,
):
    s = lax.axis_index("section")
    r = lax.axis_index("rows")
    x = lax.rem(r, 2)
    y = lax.rem(r // 2, 2)
    zl = lax.rem(r // 4, 2)
    zh = r // 8
    dx, dy, dl, dh = 1 - 2 * x, 2 - 4 * y, 4 - 8 * zl, 8 - 16 * zh
    rx, ry, rl, rh, rd = r + dx, r + dy, r + dl, r + dh, r + dy + dl
    other = 1 - s
    pending = []

    def remote(src, dst, ssem, rsem, sec, row):
        return pltpu.make_async_remote_copy(
            src_ref=src, dst_ref=dst, send_sem=ssem, recv_sem=rsem, device_id=(sec, row), device_id_type=MESH
        )

    me = pl.ds(pl.multiple_of(s * 128, 128), 128)
    kf = 2 * y + zl
    tok_in = pltpu.make_async_copy(tok.at[me, :], XS.at[0, 0], tksem.at[0])
    cot_in = pltpu.make_async_copy(cot.at[me, :], BG.at[1, kf], tksem.at[1])
    tok_in.start()
    cot_in.start()
    for l in range(2):
        for j in range(4):
            cols = pl.ds(768 * j, 768)
            pltpu.make_async_copy(in_hbm.at[0, l, :, cols], W.at[s, l, :, cols], wsem.at[s, l, j]).start()
    wo = [pltpu.make_async_copy(out_hbm.at[l], WO.at[l], wosem.at[l]) for l in range(2)]
    wo[0].start()
    wo[1].start()

    barrier = pltpu.get_barrier_semaphore()
    peers = [(other, r), (0, rx), (1, rx), (s, ry), (s, rl), (s, rd), (s, rh)]
    for peer in peers:
        pl.semaphore_signal(barrier, inc=1, device_id=peer, device_id_type=MESH)
    pl.semaphore_wait(barrier, len(peers))

    for l in range(2):
        for j in range(4):
            cols = pl.ds(768 * j, 768)
            cp = remote(in_hbm.at[0, l, :, cols], W.at[s, l, :, cols], wsend.at[l, j], wsem.at[s, l, j], other, r)
            cp.start()
            pending.append((None, cp))

    def wait_w(sec, l, j):
        cols = pl.ds(768 * j, 768)
        pltpu.make_async_copy(in_hbm.at[0, l, :, cols], W.at[sec, l, :, cols], wsem.at[sec, l, j]).wait()

    ka = 2 * x + s

    def exchange(item, l, own, far, dst):
        @pl.when(s == 0)
        def _():
            pltpu.make_async_copy(own, dst.at[ka], irecv.at[l, item, ka]).start()

        cp_own = remote(own, dst.at[ka], isend.at[l, item, 0], irecv.at[l, item, ka], 0, r)
        cp_far = remote(far, dst.at[ka], isend.at[l, item, 1], irecv.at[l, item, ka], 0, rx)
        cp_far.start()
        pl.when(s == 1)(cp_own.start)
        pending.append((None, cp_far))
        pending.append((s == 1, cp_own))

    def wait_item(l, item, dst):
        for k in range(4):
            pltpu.make_async_copy(dst.at[k], dst.at[k], irecv.at[l, item, k]).wait()

    def send_normed(l):
        exchange(AX, l, XS.at[0, l], XS.at[0, l], XR.at[l, 0])

    def send_mixer(l):
        exchange(AM, l, XS.at[1, l], XS.at[1, l], XR.at[l, 1])

    def send_ya(l):
        exchange(AY, l, YS.at[l, :, :, :, x], YS.at[l, :, :, :, 1 - x], YR.at[l])

    def store_y(l, c, block):
        turned = block.T
        YS[l, c // 4, (c // 2) % 2, c % 2, 0] = turned[:192]
        YS[l, c // 4, (c // 2) % 2, c % 2, 1] = turned[192:]

    group = ((ry, 2 * (1 - y) + zl), (rl, 2 * y + 1 - zl), (rd, 2 * (1 - y) + 1 - zl))

    def share(item, l, buf):
        for p, (row, _) in enumerate(group):
            cp = remote(buf.at[l, kf], buf.at[l, kf], fsend.at[l, item, p], frecv.at[l, item, kf], s, row)
            cp.start()
            pending.append((None, cp))

    def wait_share(item, l, buf):
        for _, k in group:
            pltpu.make_async_copy(buf.at[l, k], buf.at[l, k], frecv.at[l, item, k]).wait()

    lane = lax.broadcasted_iota(jnp.int32, (1, 128), 1)
    mk0 = jnp.where(lane < 64, 1.0, 0.0).astype(BF)
    mk1 = jnp.where(lane < 64, 0.0, 1.0).astype(BF)

    def allowed():
        ids = jnp.broadcast_to(seg[pl.ds(s, 1), :], (128, 128))
        row = lax.broadcasted_iota(jnp.int32, (128, 128), 0)
        col = lax.broadcasted_iota(jnp.int32, (128, 128), 1)
        one = jnp.logical_and(ids == ids.T, row >= col)
        return jnp.concatenate([one, one], axis=0)

    def split0(v):
        return jnp.concatenate([v * mk0, v * mk1], axis=0)

    scale = HEAD_DIM ** (-0.5)
    width = 3072.0

    def attention_forward(l):
        stream = ST[2 * l]
        xh, rs = hat(stream)
        XS[0, l] = (xh * gf[l, 0:1, :]).astype(BF)
        send_normed(l)
        for j in range(3):
            wait_w(0, l, j)
            for i in range(2):
                c = 768 * j + 384 * i
                part = dot(XS[0, l], W[0, l, :, c : c + 384], 1, 0).astype(BF)
                for p in range(3):
                    QKV[l, c // 128 + p] = part[:, 128 * p : 128 * p + 128]
        visible = allowed()

        def pair(p):
            q, k, v = QKV[l, p], QKV[l, 6 + p], QKV[l, 12 + p]
            scores = dot(split0(q), k, 1, 1) * scale
            scores = jnp.where(visible, scores, -1e30)
            e = jnp.exp(scores - jnp.max(scores, axis=-1, keepdims=True))
            probs = e * (1.0 / jnp.sum(e, axis=-1, keepdims=True))
            low = probs.astype(BF)
            PB[l, p] = low
            both = jnp.concatenate([low[:128], low[128:]], axis=1)
            return dot(both, split0(v), 1, 0)

        for p in range(6):
            CTX[l, :, 128 * p : 128 * p + 128] = pair(p)
        xh, rs = hat(CTX[l])
        XS[1, l] = (xh * gm[l : l + 1, :]).astype(BF)
        send_mixer(l)
        wait_w(0, l, 3)
        branch = dot(XS[1, l], W[0, l, :, 2304:], 1, 0).astype(BF)
        ST[2 * l + 1] = stream + branch.astype(F32)

    def feed_forward(l):
        stream = ST[2 * l + 1]
        xh, rs = hat(stream)
        FN[l, kf] = (xh * gf[l, 1:2, :]).astype(BF)
        share(0, l, FN)

        def hidden(j, total):
            for i in range(2):
                c = pl.ds(pl.multiple_of(768 * j + 384 * i, 384), 384)
                h = dot(FN[l, kf], W[1, l, :, c], 1, 0)
                phi = 0.5 + 0.5 * lax.erf(h * (0.5**0.5))
                act = h * phi
                BIG[:, c] = act
                GP[l, :, c] = (phi + h * (jnp.exp(-0.5 * h * h) * 0.3989422804014327)).astype(BF)
                total = total + fold(act)
            return total

        total = jnp.zeros((128, 128), F32)
        for j in range(4):
            wait_w(1, l, j)
            total = hidden(j, total)
        mu = jnp.sum(total, axis=-1, keepdims=True) / width

        def spread(c, acc):
            cen = BIG[:, pl.ds(pl.multiple_of(384 * c, 384), 384)] - mu
            return acc + fold(cen * cen)

        acc = lax.fori_loop(0, 8, spread, jnp.zeros((128, 128), F32))
        rs = lax.rsqrt(jnp.sum(acc, axis=-1, keepdims=True) / width + EPSILON)
        RSB[l] = jnp.where(lane == 0, mu, rs)

        def scaled(c, carry):
            cols = pl.ds(pl.multiple_of(384 * c, 384), 384)
            xh = (BIG[:, cols] - mu) * rs
            XH[l, :, cols] = xh.astype(BF)
            HG[:, cols] = (xh * gff[l : l + 1, cols]).astype(BF)
            return carry

        lax.fori_loop(0, 8, scaled, 0)
        wo[l].wait()
        for n in range(0, 768, 256):
            branch = dot(HG[...], WO[l, :, n : n + 256], 1, 0).astype(BF)
            out = stream[:, n : n + 256] + branch.astype(F32)
            if l == 0:
                ST[2, :, n : n + 256] = out
            else:
                lay_o[me, n : n + 256] = out.astype(BF)

    def feed_backward(l):
        def first(c, carry):
            a1, a2 = carry
            for i in range(2):
                at = 384 * (2 * c + i)
                cols = pl.ds(pl.multiple_of(at, 384), 384)
                ig = dot(BG[l, kf], WO[l, cols, :], 1, 1)
                xh = XH[l, :, cols].astype(F32)
                GS[0, pl.ds(6 + 4 * l + c, 1), 384 * i : 384 * i + 384] = jnp.sum(ig * xh, axis=0, keepdims=True)
                dxh = ig * gff[l : l + 1, cols]
                BIG[:, cols] = dxh
                a1 = a1 + fold(dxh)
                a2 = a2 + fold(dxh * xh)
            return a1, a2

        zero = jnp.zeros((128, 128), F32)
        a1, a2 = lax.fori_loop(0, 4, first, (zero, zero))
        m1 = jnp.sum(a1, axis=-1, keepdims=True) / width
        m2 = jnp.sum(a2, axis=-1, keepdims=True) / width
        kept = RSB[l]
        rs = kept[:, 1:2]
        stats = jnp.where(lane < 2, kept, jnp.where(lane == 2, m1, m2))
        SR[l, kf] = stats.T[0:8]
        share(2, l, SR)

        def second(c, carry):
            cols = pl.ds(pl.multiple_of(384 * c, 384), 384)
            da = rs * (BIG[:, cols] - m1 - XH[l, :, cols].astype(F32) * m2)
            HG[:, cols] = (GP[l, :, cols].astype(F32) * da).astype(BF)
            return carry

        lax.fori_loop(0, 8, second, 0)
        for n in range(0, 768, 256):
            BIG[:, n : n + 256] = dot(HG[...], W[1, l, n : n + 256, :], 1, 1)
        front_back(l, 1)

    def front_back(l, sub):
        ng = BIG[:, 0:768]
        xh, rs = hat(ST[2 * l + sub])
        GS[0, 2 * l + sub : 2 * l + sub + 1, :] = jnp.sum(ng * xh, axis=0, keepdims=True)
        UP[...] = UP[...] + hat_back(xh, rs, ng * gf[l, sub : sub + 1, :]).astype(BF).astype(F32)

    def attention_backward(l):
        low = UP[...].astype(BF)
        for i in range(2):
            store_y(l, 6 + i, low[:, 384 * i : 384 * i + 384])
        for n in range(0, 768, 256):
            BIG[:, n : n + 256] = dot(low, W[0, l, n : n + 256, 2304:], 1, 1)
        ig = BIG[:, 0:768]
        xh, rs = hat(CTX[l])
        GS[0, 4 + l : 5 + l, :] = jnp.sum(ig * xh, axis=0, keepdims=True)
        dctx = hat_back(xh, rs, ig * gm[l : l + 1, :]).astype(BF)
        HG[:, 2304:] = dctx

        def pair(p):
            q, k, v = QKV[l, p], QKV[l, 6 + p], QKV[l, 12 + p]
            probs_low = PB[l, p]
            probs = probs_low.astype(F32)
            dcc = split0(HG[:, 2304 + 128 * p : 2432 + 128 * p])
            pg = dot(dcc, v, 1, 1)
            ds = (probs * (pg - jnp.sum(probs * pg, axis=-1, keepdims=True))).astype(BF)
            both = jnp.concatenate([ds[:128], ds[128:]], axis=1)
            dq = dot(both, split0(k), 1, 0) * scale
            dk = dot(ds, split0(q), 0, 0) * scale
            dv = dot(probs_low, dcc, 0, 0)
            return dq.astype(BF), dk.astype(BF), dv.astype(BF)

        for g in range(2):
            parts = [pair(3 * g + i) for i in range(3)]
            for which in range(3):
                block = jnp.concatenate([part[which] for part in parts], axis=1)
                at = 768 * which + 384 * g
                HG[:, at : at + 384] = block
                store_y(l, 2 * which + g, block)
        send_ya(l)
        for n in range(0, 768, 256):
            BIG[:, n : n + 256] = dot(HG[:, 0:2304], W[0, l, n : n + 256, 0:2304], 1, 1)
        front_back(l, 0)

    def g_at(l, n):
        return W.at[1 - l, 1, pl.ds(384 + 192 * (n // 4), 192), pl.ds(768 * (n % 4), 768)]

    def a2_copy(l, at):
        return remote(g_at(l, 4 + at), R2.at[l, at], s2s.at[l, at], s2r.at[l, at], 0, ry)

    def a3_copy(l, r4):
        return remote(g_at(l, 2 + r4), R3.at[l, r4], s3s.at[l, r4], s3r.at[l, r4], 0, rl)

    def a4_copy(l):
        return remote(g_at(l, 1), R4.at[l], s4s.at[l], s4r.at[l], 0, rh)

    def a_job(l):
        wait_item(l, AX, XR.at[l, 0])
        wait_item(l, AM, XR.at[l, 1])
        wait_item(l, AY, YR.at[l])
        for r3, r4 in ((1, 1), (1, 0), (0, 1), (0, 0)):
            h, low = flip(zh, r4), flip(zl, r3)
            xi = h * low
            rows = []
            for r2 in (1, 0):
                rows.append(jnp.concatenate([YR[l, k, h, low, flip(y, r2)] for k in range(4)], axis=1))
            lhs = jnp.concatenate(rows, axis=0)
            at = 2 * r3 + r4
            for n in range(0, 768, 256):
                res = dot(lhs, XR[l, xi, :, :, n : n + 256].reshape(512, 256), 1, 0).astype(BF)
                g_at(l, 4 + at)[:, n : n + 256] = res[:192]
                g_at(l, at)[:, n : n + 256] = res[192:]
            a2_copy(l, at).start()

    def a_stage2(l):
        for r3, r4 in ((1, 1), (1, 0), (0, 1), (0, 0)):
            at = 2 * r3 + r4
            a2_copy(l, at).wait_recv()
            g = g_at(l, at)
            g[...] = (g[...].astype(F32) + R2[l, at].astype(F32)).astype(BF)
            if r3 == 1:
                a3_copy(l, r4).start()

    def a_stage3(l):
        for r4 in (1, 0):
            a3_copy(l, r4).wait_recv()
            g = g_at(l, r4)
            g[...] = (g[...].astype(F32) + R3[l, r4].astype(F32)).astype(BF)
            if r4 == 1:
                a4_copy(l).start()

    def a_stage4(l):
        a4_copy(l).wait_recv()
        gi_o[l] = g_at(l, 0)[...].astype(F32) + R4[l].astype(F32)

    def a_sent(l):
        for at in range(4):
            a2_copy(l, at).wait_send()
        for r4 in range(2):
            a3_copy(l, r4).wait_send()
        a4_copy(l).wait_send()

    def f_at(l, which, q):
        return W.at[1 - l, 1, pl.ds(0, 384), pl.ds(pl.multiple_of(768 * (2 * which + q), 768), 768)]

    def f_half(l, q, half):
        return f_at(l, s, q).at[pl.ds(pl.multiple_of(192 * half, 192), 192), :]

    def f1_copy(l, q):
        return remote(f_at(l, other, q), RC.at[l, q], f1s.at[l, q], f1r.at[l, q], other, r)

    def f2_copy(l, q):
        return remote(f_half(l, q, 1 - x), RX.at[l, q], f2s.at[l, q], f2r.at[l, q], s, rx)

    def f3_copy(l):
        return remote(f_half(l, 1, x), RH.at[l], f3s.at[l], f3r.at[l], s, rh)

    def f_job(l):
        wait_share(0, l, FN)
        wait_share(1, l, BG)
        wait_share(2, l, SR)

        for q in (1, 0):
            c = 4 * flip(zh, q) + 2 * zl + y
            cols = pl.ds(pl.multiple_of(384 * c, 384), 384)

            def source(k, carry):
                stats = jnp.concatenate([SR[l, k]] * 16, axis=0).T
                mu, rs, m1, m2 = (stats[:, i : i + 1] for i in range(4))
                gain = gff[l : l + 1, cols]
                h = dot(FN[l, k], W[1, l, :, cols], 1, 0)
                phi = 0.5 + 0.5 * lax.erf(h * (0.5**0.5))
                xh = (h * phi - mu) * rs
                rows = pl.ds(pl.multiple_of(128 * k, 128), 128)
                FI[rows, :] = (xh * gain).astype(BF)
                ig = dot(BG[l, k], WO[l, cols, :], 1, 1)
                da = rs * (ig * gain - m1 - xh * m2)
                slope = phi + h * (jnp.exp(-0.5 * h * h) * 0.3989422804014327)
                FG[rows, :] = (slope * da).astype(BF)
                return carry

            lax.fori_loop(0, 4, source, 0)
            for which, (a, b) in enumerate(((FI, BG), (FG, FN))):
                out = f_at(l, which, q)
                for n in range(0, 768, 256):
                    out[:, n : n + 256] = dot(a[...], b[l, :, :, n : n + 256].reshape(512, 256), 0, 0).astype(BF)
            f1_copy(l, q).start()

    def f_stage1(l):
        for q in (1, 0):
            f1_copy(l, q).wait_recv()
            g = f_at(l, s, q)
            g[...] = (g[...].astype(F32) + RC[l, q].astype(F32)).astype(BF)
            f2_copy(l, q).start()

    def f_stage2(l):
        for q in (1, 0):
            f2_copy(l, q).wait_recv()
            g = f_half(l, q, x)
            g[...] = (g[...].astype(F32) + RX[l, q].astype(F32)).astype(BF)
            if q == 1:
                f3_copy(l).start()

    def o_copy(l):
        return remote(RX.at[l, 1, :, pl.ds(0, 384)], ORCV.at[l], tss.at[2 + l], tsr.at[2 + l], other, r)

    def f_stage3(l):
        f3_copy(l).wait_recv()
        g = f_half(l, 0, x)

        def final(lo, hi):
            return g[:, lo:hi].astype(F32) + RH[l, :, lo:hi].astype(F32)

        @pl.when(s == 0)
        def _():
            RX[l, 1, :, 0:384] = final(384, 768).astype(BF)
            o_copy(l).start()
            go_o[l] = final(0, 384)

        @pl.when(s == 1)
        def _():
            gi_o[l] = final(0, 768)

    def f_sent(l):
        for q in range(2):
            f1_copy(l, q).wait_send()
            f2_copy(l, q).wait_send()
        f3_copy(l).wait_send()

        @pl.when(s == 0)
        def _():
            o_copy(l).wait_send()

    def gain_stage(k):
        to = ((other, r), (s, rx), (s, ry), (s, rl), (s, rh))[k]
        return remote(GS.at[k], GR.at[k], gss.at[k], gsr.at[k], *to)

    def gain_step(k):
        gain_stage(k).wait_recv()
        if k == 4:
            gain_o[...] = GS[4] + GR[4]
        else:
            GS[k + 1] = GS[k] + GR[k]
            gain_stage(k + 1).start()

    def on0(*steps):
        @pl.when(s == 0)
        def _():
            for step in steps:
                step()

    cot_in.wait()
    share(1, 1, BG)
    UP[...] = BG[1, kf].astype(F32)
    tok_in.wait()
    ST[0] = XS[0, 0].astype(F32)
    GS[0, 14:16, :] = jnp.zeros((2, 768), F32)

    attention_forward(0)
    feed_forward(0)
    attention_forward(1)
    feed_forward(1)
    lay_cp = remote(lay_o.at[me, :], lay_o.at[me, :], tss.at[0], tsr.at[0], other, r)
    lay_cp.start()

    feed_backward(1)
    attention_backward(1)
    BG[0, kf] = UP[...].astype(BF)
    share(1, 0, BG)
    f_job(1)
    on0(lambda: a_job(1))
    f_stage1(1)
    feed_backward(0)
    attention_backward(0)
    inp_o[me, :] = UP[...].astype(BF)
    inp_cp = remote(inp_o.at[me, :], inp_o.at[me, :], tss.at[1], tsr.at[1], other, r)
    inp_cp.start()
    gain_stage(0).start()
    f_stage2(1)
    on0(lambda: a_stage2(1))
    gain_step(0)
    f_job(0)
    gain_step(1)
    on0(lambda: a_job(0))
    f_stage1(0)
    gain_step(2)
    f_stage3(1)
    on0(lambda: a_stage3(1))
    gain_step(3)
    gain_step(4)
    f_stage2(0)
    on0(lambda: a_stage4(1), lambda: a_stage2(0))
    f_stage3(0)
    on0(lambda: a_stage3(0), lambda: a_stage4(0))

    @pl.when(s == 1)
    def _():
        for l in (1, 0):
            o_copy(l).wait_recv()
            go_o[l] = ORCV[l].astype(F32)

    for l in range(2):
        f_sent(l)
        on0(lambda: a_sent(l))
    for k in range(5):
        gain_stage(k).wait_send()
    other_half = pl.ds(pl.multiple_of(other * 128, 128), 128)
    remote(lay_o.at[other_half, :], lay_o.at[other_half, :], tss.at[0], tsr.at[0], other, r).wait_recv()
    remote(inp_o.at[other_half, :], inp_o.at[other_half, :], tss.at[1], tsr.at[1], other, r).wait_recv()
    lay_cp.wait_send()
    inp_cp.wait_send()
    for cond, cp in pending:
        if cond is None:
            cp.wait_send()
        else:
            pl.when(cond)(cp.wait_send)


def hand_over(lay, inp, gi, go, gains, lay_o, inp_o, gi_o, go_o, front_o, mixer_o, feed_o):
    lay_o[...] = lay[...]
    inp_o[...] = inp[...]
    gi_o[...] = gi[...]
    go_o[...] = go[...]
    for l in range(2):
        front_o[l] = gains[2 * l : 2 * l + 2, :]
        for i in range(4):
            feed_o[l : l + 1, 768 * i : 768 * i + 768] = gains[6 + 4 * l + i : 7 + 4 * l + i, :]
    mixer_o[...] = gains[4:6, :]


def fused(tokens, segment_ids, in_proj, out_proj, front_gain, mixer_gain, feed_gain, cotangent):
    vm = pl.BlockSpec(memory_space=pltpu.VMEM)
    hbm = pl.BlockSpec(memory_space=pl.ANY)
    dma = pltpu.SemaphoreType.DMA
    outs = pl.pallas_call(
        body,
        out_shape=(
            jax.ShapeDtypeStruct((256, 768), BF),
            jax.ShapeDtypeStruct((256, 768), BF),
            jax.ShapeDtypeStruct((2, 192, 768), F32),
            jax.ShapeDtypeStruct((2, 192, 384), F32),
            jax.ShapeDtypeStruct((16, 768), F32),
        ),
        in_specs=[hbm, vm, hbm, hbm, vm, vm, vm, hbm],
        out_specs=(vm, vm, vm, vm, vm),
        scratch_shapes=[
            pltpu.VMEM((2, 2, 768, 3072), BF),
            pltpu.VMEM((2, 3072, 768), BF),
            pltpu.VMEM((2, 2, 128, 768), BF),
            pltpu.VMEM((2, 2, 2, 2, 2, 192, 128), BF),
            pltpu.VMEM((2, 2, 4, 128, 768), BF),
            pltpu.VMEM((2, 4, 2, 2, 2, 192, 128), BF),
            pltpu.VMEM((2, 4, 192, 768), BF),
            pltpu.VMEM((2, 2, 192, 768), BF),
            pltpu.VMEM((2, 192, 768), BF),
            pltpu.VMEM((2, 4, 128, 768), BF),
            pltpu.VMEM((2, 4, 128, 768), BF),
            pltpu.VMEM((2, 4, 8, 128), F32),
            pltpu.VMEM((512, 384), BF),
            pltpu.VMEM((512, 384), BF),
            pltpu.VMEM((2, 2, 384, 768), BF),
            pltpu.VMEM((2, 2, 192, 768), BF),
            pltpu.VMEM((2, 192, 768), BF),
            pltpu.VMEM((2, 18, 128, 128), BF),
            pltpu.VMEM((2, 6, 256, 128), BF),
            pltpu.VMEM((2, 128, 768), F32),
            pltpu.VMEM((4, 128, 768), F32),
            pltpu.VMEM((128, 768), F32),
            pltpu.VMEM((2, 128, 3072), BF),
            pltpu.VMEM((2, 128, 3072), BF),
            pltpu.VMEM((2, 128, 128), F32),
            pltpu.VMEM((128, 3072), F32),
            pltpu.VMEM((128, 3072), BF),
            pltpu.VMEM((2, 192, 384), BF),
            pltpu.VMEM((5, 16, 768), F32),
            pltpu.VMEM((5, 16, 768), F32),
            dma((2, 2, 4)),
            dma((2, 4)),
            dma((2,)),
            dma((2, 3, 2)),
            dma((2, 3, 4)),
            dma((2, 4)),
            dma((2, 4)),
            dma((2, 2)),
            dma((2, 2)),
            dma((2,)),
            dma((2,)),
            dma((2, 3, 3)),
            dma((2, 3, 4)),
            dma((2, 2)),
            dma((2, 2)),
            dma((2, 2)),
            dma((2, 2)),
            dma((2,)),
            dma((2,)),
            dma((5,)),
            dma((5,)),
            dma((4,)),
            dma((4,)),
            dma((2,)),
        ],
        compiler_params=pltpu.CompilerParams(
            collective_id=0, has_side_effects=True, vmem_limit_bytes=63 * 2**20
        ),
        name="layers",
    )(
        tokens,
        segment_ids.reshape(2, SEQ),
        in_proj,
        out_proj,
        front_gain,
        mixer_gain,
        feed_gain,
        cotangent,
    )
    layer_out, input_grad, in_turned, out_grad, front, mixer, feed = pl.pallas_call(
        hand_over,
        out_shape=(
            jax.ShapeDtypeStruct((256, 768), BF),
            jax.ShapeDtypeStruct((256, 768), BF),
            jax.ShapeDtypeStruct((2, 192, 768), F32),
            jax.ShapeDtypeStruct((2, 192, 384), F32),
            jax.ShapeDtypeStruct((2, 2, 768), F32),
            jax.ShapeDtypeStruct((2, 768), F32),
            jax.ShapeDtypeStruct((2, 3072), F32),
        ),
        in_specs=[vm] * 5,
        out_specs=(vm,) * 7,
        name="hand_over",
    )(*outs)
    return layer_out, input_grad, jnp.swapaxes(in_turned, 1, 2)[None], out_grad, front, mixer, feed


def passed_along(array, axis, by):
    devices = lax.axis_size(axis)
    pairs = [(i, i + by) for i in range(devices) if 0 <= i + by < devices]
    return lax.ppermute(array, axis, pairs)


def layer_norm(values, gain):
    centered = values - jnp.mean(values, axis=-1, keepdims=True)
    spread = jnp.mean(centered * centered, axis=-1, keepdims=True)
    return centered * lax.rsqrt(spread + EPSILON) * gain


def gelu_exact(values):
    return jax.nn.gelu(values, approximate=False)


def visible(segment, seq_count):
    segment_grid = segment.reshape(seq_count, SEQ)
    position = jnp.arange(SEQ)
    causal = position[:, None] >= position[None, :]
    same_doc = segment_grid[:, :, None] == segment_grid[:, None, :]
    return jnp.logical_and(causal[None], same_doc)


def attention_forward(stream, segment, weight, gain_in, gain_mid):
    model_width = stream.shape[1]
    seq_count = stream.shape[0] // SEQ
    head_count = model_width // HEAD_DIM
    normed = layer_norm(stream, gain_in).astype(jnp.bfloat16)
    projected = jnp.dot(
        normed, weight[:, : 3 * model_width], preferred_element_type=jnp.float32
    ).astype(jnp.bfloat16)
    shaped = projected.reshape(seq_count, SEQ, 3, head_count, HEAD_DIM)
    queries = shaped[:, :, 0]
    key_rows = shaped[:, :, 1]
    value_rows = shaped[:, :, 2]
    scores = jnp.einsum(
        "bqhd,bkhd->bhqk", queries, key_rows, preferred_element_type=jnp.float32
    ) * HEAD_DIM ** (-0.5)
    allowed = visible(segment, seq_count)
    scores = jnp.where(allowed[:, None], scores, -1e30)
    row_peak = jnp.max(scores, axis=-1, keepdims=True)
    weights = jnp.exp(scores - row_peak)
    attention = weights / jnp.sum(weights, axis=-1, keepdims=True)
    attention_low = attention.astype(jnp.bfloat16)
    context = jnp.einsum(
        "bhqk,bkhd->bqhd", attention_low, value_rows, preferred_element_type=jnp.float32
    )
    context = context.reshape(-1, model_width)
    inner_normed = layer_norm(context, gain_mid).astype(jnp.bfloat16)
    branch = jnp.dot(
        inner_normed, weight[:, 3 * model_width :], preferred_element_type=jnp.float32
    ).astype(jnp.bfloat16)
    return (
        branch,
        (normed, queries, key_rows, value_rows, attention, attention_low, context, inner_normed),
    )


def attention_backward(stream, segment, weight, gain_in, gain_mid, upstream):
    model_width = stream.shape[1]
    seq_count = stream.shape[0] // SEQ
    head_count = model_width // HEAD_DIM
    scale = HEAD_DIM ** (-0.5)
    branch, kept = attention_forward(stream, segment, weight, gain_in, gain_mid)
    normed, queries, key_rows, value_rows, attention, attention_low, context, inner_normed = kept
    branch_grad = upstream.astype(jnp.bfloat16)
    out_weight_grad = jnp.einsum(
        "tc,td->cd", inner_normed, branch_grad, preferred_element_type=jnp.float32
    )
    inner_grad = jnp.einsum(
        "td,cd->tc", branch_grad, weight[:, 3 * model_width :], preferred_element_type=jnp.float32
    )
    unused_value, mid_pull = jax.vjp(layer_norm, context, gain_mid)
    context_grad, mid_gain_grad = mid_pull(inner_grad)
    context_low = context_grad.astype(jnp.bfloat16).reshape(seq_count, SEQ, head_count, HEAD_DIM)
    prob_grad = jnp.einsum(
        "bqhd,bkhd->bhqk", context_low, value_rows, preferred_element_type=jnp.float32
    )
    value_grad = jnp.einsum(
        "bhqk,bqhd->bkhd", attention_low, context_low, preferred_element_type=jnp.float32
    )
    score_grad = attention * (prob_grad - jnp.sum(attention * prob_grad, axis=-1, keepdims=True))
    score_low = score_grad.astype(jnp.bfloat16)
    query_grad = (
        jnp.einsum("bhqk,bkhd->bqhd", score_low, key_rows, preferred_element_type=jnp.float32)
        * scale
    )
    key_grad = (
        jnp.einsum("bhqk,bqhd->bkhd", score_low, queries, preferred_element_type=jnp.float32)
        * scale
    )
    projected_grad = jnp.stack([query_grad, key_grad, value_grad], axis=2).astype(jnp.bfloat16)
    projected_grad = projected_grad.reshape(-1, 3 * model_width)
    in_weight_grad = jnp.einsum(
        "tc,td->cd", normed, projected_grad, preferred_element_type=jnp.float32
    )
    normed_grad = jnp.einsum(
        "td,cd->tc",
        projected_grad,
        weight[:, : 3 * model_width],
        preferred_element_type=jnp.float32,
    )
    unused_front, front_pull = jax.vjp(layer_norm, stream, gain_in)
    stream_grad, front_gain_grad = front_pull(normed_grad)
    weight_grad = jnp.concatenate([in_weight_grad, out_weight_grad], axis=1)
    return (stream_grad.astype(jnp.bfloat16), weight_grad, front_gain_grad, mid_gain_grad)


def feed_forward(stream, weight_in, weight_out, gain_in, gain_mid):
    normed = layer_norm(stream, gain_in).astype(jnp.bfloat16)
    hidden = jnp.dot(normed, weight_in, preferred_element_type=jnp.float32)
    activated = gelu_exact(hidden)
    inner_normed = layer_norm(activated, gain_mid).astype(jnp.bfloat16)
    branch = jnp.dot(inner_normed, weight_out, preferred_element_type=jnp.float32).astype(
        jnp.bfloat16
    )
    return (branch, (normed, hidden, activated, inner_normed))


def feed_backward(stream, weight_in, weight_out, gain_in, gain_mid, upstream):
    branch, kept = feed_forward(stream, weight_in, weight_out, gain_in, gain_mid)
    normed, hidden, activated, inner_normed = kept
    branch_grad = upstream.astype(jnp.bfloat16)
    out_weight_grad = jnp.einsum(
        "tc,td->cd", inner_normed, branch_grad, preferred_element_type=jnp.float32
    )
    inner_grad = jnp.einsum(
        "td,cd->tc", branch_grad, weight_out, preferred_element_type=jnp.float32
    )
    unused_value, mid_pull = jax.vjp(layer_norm, activated, gain_mid)
    act_grad, mid_gain_grad = mid_pull(inner_grad)
    unused_act, gelu_pull = jax.vjp(gelu_exact, hidden)
    hidden_grad = gelu_pull(act_grad)[0].astype(jnp.bfloat16)
    in_weight_grad = jnp.einsum(
        "tc,td->cd", normed, hidden_grad, preferred_element_type=jnp.float32
    )
    normed_grad = jnp.einsum(
        "td,cd->tc", hidden_grad, weight_in, preferred_element_type=jnp.float32
    )
    unused_front, front_pull = jax.vjp(layer_norm, stream, gain_in)
    stream_grad, front_gain_grad = front_pull(normed_grad)
    return (
        stream_grad.astype(jnp.bfloat16),
        in_weight_grad,
        out_weight_grad,
        front_gain_grad,
        mid_gain_grad,
    )


def accumulate(store, label, value):
    if label in store:
        store[label] = store[label] + value
    else:
        store[label] = value


def generic(tokens, segment_ids, in_proj, out_proj, front_gain, mixer_gain, feed_gain, cotangent):
    own_section = lax.axis_index("section")
    own_weights = in_proj[0]
    layer_total = own_weights.shape[0]
    model_width = front_gain.shape[2]
    hidden_width = feed_gain.shape[1]
    in_store = {}
    out_store = {}
    front_store = {}
    mixer_store = {}
    feed_store = {}

    def run_forward(sublayer, layer_index, stream, segment):
        if sublayer == 0:
            return attention_forward(
                stream,
                segment,
                own_weights[layer_index],
                front_gain[layer_index, 0],
                mixer_gain[layer_index],
            )[0]
        return feed_forward(
            stream,
            own_weights[layer_index],
            out_proj[layer_index],
            front_gain[layer_index, 1],
            feed_gain[layer_index],
        )[0]

    def resting_grads(stream):
        return (
            jnp.zeros(stream.shape, jnp.bfloat16),
            jnp.zeros(own_weights.shape[1:], jnp.float32),
            jnp.zeros(out_proj.shape[1:], jnp.float32),
            jnp.zeros((model_width,), jnp.float32),
            jnp.zeros((model_width,), jnp.float32),
            jnp.zeros((hidden_width,), jnp.float32),
        )

    def run_backward(sublayer, layer_index, stream, segment, upstream):
        if sublayer == 0:
            stream_grad, weight_grad, front_grad, mid_grad = attention_backward(
                stream,
                segment,
                own_weights[layer_index],
                front_gain[layer_index, 0],
                mixer_gain[layer_index],
                upstream,
            )
            return (
                stream_grad,
                weight_grad,
                jnp.zeros(out_proj.shape[1:], jnp.float32),
                front_grad,
                mid_grad,
                jnp.zeros((hidden_width,), jnp.float32),
            )
        stream_grad, in_grad, out_grad, front_grad, mid_grad = feed_backward(
            stream,
            own_weights[layer_index],
            out_proj[layer_index],
            front_gain[layer_index, 1],
            feed_gain[layer_index],
            upstream,
        )
        return (
            stream_grad,
            in_grad,
            out_grad,
            front_grad,
            jnp.zeros((model_width,), jnp.float32),
            mid_grad,
        )

    stream = tokens.astype(jnp.float32)
    upstream = cotangent.astype(jnp.float32)
    kept_streams = []
    for layer_index in range(layer_total):
        for sublayer in (0, 1):
            kept_streams.append(stream)

            def active_forward(stream_in):
                return run_forward(sublayer, layer_index, stream_in, segment_ids)

            def resting_forward(stream_in):
                return jnp.zeros(stream_in.shape, jnp.bfloat16)

            own_branch = lax.cond(own_section == sublayer, active_forward, resting_forward, stream)
            if sublayer == 0:
                received = passed_along(own_branch, "section", 1)
            else:
                received = passed_along(own_branch, "section", -1)
            stream = stream + jnp.where(own_section == sublayer, own_branch, received).astype(
                jnp.float32
            )
    for position in reversed(range(2 * layer_total)):
        layer_index, sublayer = divmod(position, 2)

        def active_backward(operand):
            return run_backward(sublayer, layer_index, operand[0], segment_ids, operand[1])

        def resting_backward(operand):
            return resting_grads(operand[0])

        grads = lax.cond(
            own_section == sublayer,
            active_backward,
            resting_backward,
            (kept_streams[position], upstream),
        )
        own_grad = grads[0]
        accumulate(in_store, layer_index, grads[1])
        accumulate(out_store, layer_index, grads[2])
        accumulate(front_store, (layer_index, sublayer), grads[3])
        accumulate(mixer_store, layer_index, grads[4])
        accumulate(feed_store, layer_index, grads[5])
        if sublayer == 0:
            received = passed_along(own_grad, "section", 1)
        else:
            received = passed_along(own_grad, "section", -1)
        upstream = upstream + jnp.where(own_section == sublayer, own_grad, received).astype(
            jnp.float32
        )
    in_total = jnp.stack([in_store[layer_index] for layer_index in range(layer_total)])
    out_total = jnp.stack([out_store[layer_index] for layer_index in range(layer_total)])
    front_total = jnp.stack(
        [
            jnp.stack([front_store[layer_index, 0], front_store[layer_index, 1]])
            for layer_index in range(layer_total)
        ]
    )
    mixer_total = jnp.stack([mixer_store[layer_index] for layer_index in range(layer_total)])
    feed_total = jnp.stack([feed_store[layer_index] for layer_index in range(layer_total)])
    first_grad = lax.psum_scatter(in_total[None], "rows", scatter_dimension=3, tiled=True)
    partial_sum = lax.psum_scatter(
        out_total.astype(jnp.bfloat16), "section", scatter_dimension=2, tiled=True
    ).astype(jnp.float32)
    second_grad = lax.psum_scatter(partial_sum, "rows", scatter_dimension=1, tiled=True)
    gain_totals = lax.psum((front_total, mixer_total, feed_total), ("section", "rows"))
    return (
        stream.astype(jnp.bfloat16),
        upstream.astype(jnp.bfloat16),
        first_grad,
        second_grad,
        gain_totals[0],
        gain_totals[1],
        gain_totals[2],
    )


def solution(mesh):
    local = fused if mesh.shape["rows"] == 16 and mesh.shape["section"] == 2 else generic
    return jax.shard_map(
        local,
        mesh=mesh,
        in_specs=(
            P("rows", None),
            P("rows"),
            P("section", None, None, None),
            P(),
            P(),
            P(),
            P(),
            P("rows", None),
        ),
        out_specs=(
            P("rows", None),
            P("rows", None),
            P("section", None, None, "rows"),
            P(None, "rows", "section"),
            P(),
            P(),
            P(),
        ),
        check_vma=False,
    )
```

```python
import jax
import jax.numpy as jnp
from jax import lax
from jax.experimental import pallas as pl
from jax.experimental.pallas import tpu as pltpu
from jax.sharding import PartitionSpec as P

HEAD_DIM = 64
SEQ = 128
EPSILON = 1e-05
MESH = pl.DeviceIdType.MESH
BF = jnp.bfloat16
F32 = jnp.float32


def dot(a, b, ca, cb):
    return lax.dot_general(a, b, (((ca,), (cb,)), ((), ())), preferred_element_type=F32)


def fold(v):
    parts = [v[:, i : i + 128] for i in range(0, v.shape[1], 128)]
    total = parts[0]
    for part in parts[1:]:
        total = total + part
    return total


def hat(v):
    centered = v - jnp.mean(v, axis=-1, keepdims=True)
    rs = lax.rsqrt(jnp.mean(centered * centered, axis=-1, keepdims=True) + EPSILON)
    return centered * rs, rs


def hat_back(xh, rs, dxh):
    m1 = jnp.mean(dxh, axis=-1, keepdims=True)
    m2 = jnp.mean(dxh * xh, axis=-1, keepdims=True)
    return rs * (dxh - m1 - xh * m2)


def flip(bit, by):
    return 1 - bit if by else bit


AX, AM, AY = range(3)


def body(
    tok, seg, in_hbm, out_hbm, gf, gm, gff, cot,
    lay_o, inp_o, gi_o, go_o, gain_o,
    W, WO, XS, YS, XR, YR, R2, R3, R4, FN, BG, SR, FG, RC, RX, RH,
    QKV, PB, CTX, ST, UP, XH, GP, RSB, BIG, HG, ORCV, LB, GI, GO, GS, GR,
    wsem, wsend, wosem, isend, irecv, s2s, s2r, s3s, s3r, s4s, s4r,
    fsend, frecv, f1s, f1r, f2s, f2r, f3s, f3r, gss, gsr, tss, tsr, tksem, osem,
):
    s = lax.axis_index("section")
    r = lax.axis_index("rows")
    x = lax.rem(r, 2)
    y = lax.rem(r // 2, 2)
    zl = lax.rem(r // 4, 2)
    zh = r // 8
    dx, dy, dl, dh = 1 - 2 * x, 2 - 4 * y, 4 - 8 * zl, 8 - 16 * zh
    rx, ry, rl, rh, rd = r + dx, r + dy, r + dl, r + dh, r + dy + dl
    other = 1 - s
    pending = []

    def remote(src, dst, ssem, rsem, sec, row):
        return pltpu.make_async_remote_copy(
            src_ref=src, dst_ref=dst, send_sem=ssem, recv_sem=rsem, device_id=(sec, row), device_id_type=MESH
        )

    me = pl.ds(pl.multiple_of(s * 128, 128), 128)
    kf = 2 * y + zl
    tok_in = pltpu.make_async_copy(tok.at[me, :], XS.at[0, 0], tksem.at[0])
    cot_in = pltpu.make_async_copy(cot.at[me, :], BG.at[1, kf], tksem.at[1])
    tok_in.start()
    cot_in.start()
    for l in range(2):
        for j in range(4):
            cols = pl.ds(768 * j, 768)
            pltpu.make_async_copy(in_hbm.at[0, l, :, cols], W.at[s, l, :, cols], wsem.at[s, l, j]).start()
    wo = [pltpu.make_async_copy(out_hbm.at[l], WO.at[l], wosem.at[l]) for l in range(2)]
    wo[0].start()
    wo[1].start()

    barrier = pltpu.get_barrier_semaphore()
    peers = [(other, r), (0, rx), (1, rx), (s, ry), (s, rl), (s, rd), (s, rh)]
    for peer in peers:
        pl.semaphore_signal(barrier, inc=1, device_id=peer, device_id_type=MESH)
    pl.semaphore_wait(barrier, len(peers))

    for l in range(2):
        for j in range(4):
            cols = pl.ds(768 * j, 768)
            cp = remote(in_hbm.at[0, l, :, cols], W.at[s, l, :, cols], wsend.at[l, j], wsem.at[s, l, j], other, r)
            cp.start()
            pending.append((None, cp))

    def wait_w(sec, l, j):
        cols = pl.ds(768 * j, 768)
        pltpu.make_async_copy(in_hbm.at[0, l, :, cols], W.at[sec, l, :, cols], wsem.at[sec, l, j]).wait()

    ka = 2 * x + s

    def exchange(item, l, own, far, dst):
        @pl.when(s == 0)
        def _():
            pltpu.make_async_copy(own, dst.at[ka], irecv.at[l, item, ka]).start()

        cp_own = remote(own, dst.at[ka], isend.at[l, item, 0], irecv.at[l, item, ka], 0, r)
        cp_far = remote(far, dst.at[ka], isend.at[l, item, 1], irecv.at[l, item, ka], 0, rx)
        cp_far.start()
        pl.when(s == 1)(cp_own.start)
        pending.append((None, cp_far))
        pending.append((s == 1, cp_own))

    def wait_item(l, item, dst):
        for k in range(4):
            pltpu.make_async_copy(dst.at[k], dst.at[k], irecv.at[l, item, k]).wait()

    def send_normed(l):
        exchange(AX, l, XS.at[0, l], XS.at[0, l], XR.at[l, 0])

    def send_mixer(l):
        exchange(AM, l, XS.at[1, l], XS.at[1, l], XR.at[l, 1])

    def send_ya(l):
        exchange(AY, l, YS.at[l, :, :, :, x], YS.at[l, :, :, :, 1 - x], YR.at[l])

    def store_y(l, c, block):
        turned = block.T
        YS[l, c // 4, (c // 2) % 2, c % 2, 0] = turned[:192]
        YS[l, c // 4, (c // 2) % 2, c % 2, 1] = turned[192:]


    def share(item, l, buf):
        for p, row in enumerate((ry, rl, rd)):
            cp = remote(buf.at[l, kf], buf.at[l, kf], fsend.at[l, item, p], frecv.at[l, item, kf], s, row)
            cp.start()
            pending.append((None, cp))

    lane = lax.broadcasted_iota(jnp.int32, (1, 128), 1)
    mk0 = jnp.where(lane < 64, 1.0, 0.0).astype(BF)
    mk1 = jnp.where(lane < 64, 0.0, 1.0).astype(BF)

    def allowed():
        ids = jnp.broadcast_to(seg[pl.ds(s, 1), :], (128, 128))
        row = lax.broadcasted_iota(jnp.int32, (128, 128), 0)
        col = lax.broadcasted_iota(jnp.int32, (128, 128), 1)
        one = jnp.logical_and(ids == ids.T, row >= col)
        return jnp.concatenate([one, one], axis=0)

    def split0(v):
        return jnp.concatenate([v * mk0, v * mk1], axis=0)

    scale = HEAD_DIM ** (-0.5)
    width = 3072.0

    def attention_forward(l):
        stream = ST[2 * l]
        xh, rs = hat(stream)
        XS[0, l] = (xh * gf[l, 0:1, :]).astype(BF)
        send_normed(l)
        for j in range(3):
            wait_w(0, l, j)
            for i in range(2):
                c = 768 * j + 384 * i
                part = dot(XS[0, l], W[0, l, :, c : c + 384], 1, 0).astype(BF)
                for p in range(3):
                    QKV[l, c // 128 + p] = part[:, 128 * p : 128 * p + 128]
        visible = allowed()

        def pair(p):
            q, k, v = QKV[l, p], QKV[l, 6 + p], QKV[l, 12 + p]
            scores = dot(split0(q), k, 1, 1) * scale
            scores = jnp.where(visible, scores, -1e30)
            e = jnp.exp(scores - jnp.max(scores, axis=-1, keepdims=True))
            probs = e * (1.0 / jnp.sum(e, axis=-1, keepdims=True))
            low = probs.astype(BF)
            PB[l, p] = low
            both = jnp.concatenate([low[:128], low[128:]], axis=1)
            return dot(both, split0(v), 1, 0)

        for p in range(6):
            CTX[l, :, 128 * p : 128 * p + 128] = pair(p)
        xh, rs = hat(CTX[l])
        XS[1, l] = (xh * gm[l : l + 1, :]).astype(BF)
        send_mixer(l)
        wait_w(0, l, 3)
        branch = dot(XS[1, l], W[0, l, :, 2304:], 1, 0).astype(BF)
        ST[2 * l + 1] = stream + branch.astype(F32)

    def feed_forward(l):
        stream = ST[2 * l + 1]
        xh, rs = hat(stream)
        FN[l, kf] = (xh * gf[l, 1:2, :]).astype(BF)
        share(0, l, FN)

        def hidden(j, total):
            for i in range(2):
                c = pl.ds(pl.multiple_of(768 * j + 384 * i, 384), 384)
                h = dot(FN[l, kf], W[1, l, :, c], 1, 0)
                phi = 0.5 + 0.5 * lax.erf(h * (0.5**0.5))
                act = h * phi
                BIG[:, c] = act
                GP[l, :, c] = (phi + h * (jnp.exp(-0.5 * h * h) * 0.3989422804014327)).astype(BF)
                total = total + fold(act)
            return total

        total = jnp.zeros((128, 128), F32)
        for j in range(4):
            wait_w(1, l, j)
            total = hidden(j, total)
        mu = jnp.sum(total, axis=-1, keepdims=True) / width

        def spread(c, acc):
            cen = BIG[:, pl.ds(pl.multiple_of(384 * c, 384), 384)] - mu
            return acc + fold(cen * cen)

        acc = lax.fori_loop(0, 8, spread, jnp.zeros((128, 128), F32))
        rs = lax.rsqrt(jnp.sum(acc, axis=-1, keepdims=True) / width + EPSILON)
        RSB[l] = jnp.where(lane == 0, mu, rs)

        def scaled(c, carry):
            cols = pl.ds(pl.multiple_of(384 * c, 384), 384)
            xh = (BIG[:, cols] - mu) * rs
            XH[l, :, cols] = xh.astype(BF)
            HG[:, cols] = (xh * gff[l : l + 1, cols]).astype(BF)
            return carry

        lax.fori_loop(0, 8, scaled, 0)
        wo[l].wait()
        for n in range(0, 768, 256):
            branch = dot(HG[...], WO[l, :, n : n + 256], 1, 0).astype(BF)
            out = stream[:, n : n + 256] + branch.astype(F32)
            if l == 0:
                ST[2, :, n : n + 256] = out
            else:
                LB[0, :, n : n + 256] = out.astype(BF)

    def feed_backward(l):
        def first(c, carry):
            a1, a2 = carry
            for i in range(2):
                at = 384 * (2 * c + i)
                cols = pl.ds(pl.multiple_of(at, 384), 384)
                ig = dot(BG[l, kf], WO[l, cols, :], 1, 1)
                xh = XH[l, :, cols].astype(F32)
                GS[0, pl.ds(6 + 4 * l + c, 1), 384 * i : 384 * i + 384] = jnp.sum(ig * xh, axis=0, keepdims=True)
                dxh = ig * gff[l : l + 1, cols]
                BIG[:, cols] = dxh
                a1 = a1 + fold(dxh)
                a2 = a2 + fold(dxh * xh)
            return a1, a2

        zero = jnp.zeros((128, 128), F32)
        a1, a2 = lax.fori_loop(0, 4, first, (zero, zero))
        m1 = jnp.sum(a1, axis=-1, keepdims=True) / width
        m2 = jnp.sum(a2, axis=-1, keepdims=True) / width
        kept = RSB[l]
        rs = kept[:, 1:2]
        stats = jnp.where(lane < 2, kept, jnp.where(lane == 2, m1, m2))
        SR[l, kf] = stats.T[0:8]
        share(2, l, SR)

        def second(c, carry):
            cols = pl.ds(pl.multiple_of(384 * c, 384), 384)
            da = rs * (BIG[:, cols] - m1 - XH[l, :, cols].astype(F32) * m2)
            HG[:, cols] = (GP[l, :, cols].astype(F32) * da).astype(BF)
            return carry

        lax.fori_loop(0, 8, second, 0)
        for n in range(0, 768, 256):
            BIG[:, n : n + 256] = dot(HG[...], W[1, l, n : n + 256, :], 1, 1)
        front_back(l, 1)

    def front_back(l, sub):
        ng = BIG[:, 0:768]
        xh, rs = hat(ST[2 * l + sub])
        GS[0, 2 * l + sub : 2 * l + sub + 1, :] = jnp.sum(ng * xh, axis=0, keepdims=True)
        UP[...] = UP[...] + hat_back(xh, rs, ng * gf[l, sub : sub + 1, :]).astype(BF).astype(F32)

    def attention_backward(l):
        low = UP[...].astype(BF)
        for i in range(2):
            store_y(l, 6 + i, low[:, 384 * i : 384 * i + 384])
        for n in range(0, 768, 256):
            BIG[:, n : n + 256] = dot(low, W[0, l, n : n + 256, 2304:], 1, 1)
        ig = BIG[:, 0:768]
        xh, rs = hat(CTX[l])
        GS[0, 4 + l : 5 + l, :] = jnp.sum(ig * xh, axis=0, keepdims=True)
        dctx = hat_back(xh, rs, ig * gm[l : l + 1, :]).astype(BF)
        HG[:, 2304:] = dctx

        def pair(p):
            q, k, v = QKV[l, p], QKV[l, 6 + p], QKV[l, 12 + p]
            probs_low = PB[l, p]
            probs = probs_low.astype(F32)
            dcc = split0(HG[:, 2304 + 128 * p : 2432 + 128 * p])
            pg = dot(dcc, v, 1, 1)
            ds = (probs * (pg - jnp.sum(probs * pg, axis=-1, keepdims=True))).astype(BF)
            both = jnp.concatenate([ds[:128], ds[128:]], axis=1)
            dq = dot(both, split0(k), 1, 0) * scale
            dk = dot(ds, split0(q), 0, 0) * scale
            dv = dot(probs_low, dcc, 0, 0)
            return dq.astype(BF), dk.astype(BF), dv.astype(BF)

        for g in range(2):
            parts = [pair(3 * g + i) for i in range(3)]
            for which in range(3):
                block = jnp.concatenate([part[which] for part in parts], axis=1)
                at = 768 * which + 384 * g
                HG[:, at : at + 384] = block
                store_y(l, 2 * which + g, block)
        send_ya(l)
        for n in range(0, 768, 256):
            BIG[:, n : n + 256] = dot(HG[:, 0:2304], W[0, l, n : n + 256, 0:2304], 1, 1)
        front_back(l, 0)

    def g_at(l, n):
        return W.at[1 - l, 1, pl.ds(384 + 192 * (n // 4), 192), pl.ds(768 * (n % 4), 768)]

    def piece(b2, b3, r4):
        return 4 * b2 + 2 * b3 + 1 if r4 else 2 * b2 + 4 * b3

    def a2_copy(l, b3, r4):
        at = 2 * b3 + r4
        src = g_at(l, piece(1, b3, r4))
        return remote(src, R2.at[l, at], s2s.at[l, at], s2r.at[l, at], 0, ry if r4 else rl)

    def a3_copy(l, r4):
        src = g_at(l, piece(0, 1, r4))
        return remote(src, R3.at[l, r4], s3s.at[l, r4], s3r.at[l, r4], 0, rl if r4 else ry)

    def a4_copy(l):
        return remote(g_at(l, 1), R4.at[l], s4s.at[l], s4r.at[l], 0, rh)

    def a_job(l):
        wait_item(l, AX, XR.at[l, 0])
        wait_item(l, AM, XR.at[l, 1])
        wait_item(l, AY, YR.at[l])
        for r4, r3 in ((1, 1), (1, 0), (0, 1), (0, 0)):
            h, low = flip(zh, r4), flip(zl, r3)
            xi = h * low
            rows = []
            for r2 in (1, 0):
                rows.append(jnp.concatenate([YR[l, k, h, low, flip(y, r2)] for k in range(4)], axis=1))
            lhs = jnp.concatenate(rows, axis=0)
            for n in range(0, 768, 256):
                res = dot(lhs, XR[l, xi, :, :, n : n + 256].reshape(512, 256), 1, 0).astype(BF)
                g_at(l, 4 + 2 * r3 + r4)[:, n : n + 256] = res[:192]
                g_at(l, 2 * r3 + r4)[:, n : n + 256] = res[192:]
            if r4 == 1:
                a2_copy(l, r3, 1).start()
            elif r3 == 1:
                a2_copy(l, 1, 0).start()
                a2_copy(l, 0, 0).start()

    def a_stage2(l, b3, r4):
        a2_copy(l, b3, r4).wait_recv()
        g = g_at(l, piece(0, b3, r4))
        g[...] = (g[...].astype(F32) + R2[l, 2 * b3 + r4].astype(F32)).astype(BF)
        if b3 == 1:
            a3_copy(l, r4).start()

    def a_stage3(l, r4):
        a3_copy(l, r4).wait_recv()
        g = g_at(l, r4)
        g[...] = (g[...].astype(F32) + R3[l, r4].astype(F32)).astype(BF)
        if r4 == 1:
            a4_copy(l).start()

    def a_stage4(l):
        a4_copy(l).wait_recv()
        GI[l] = g_at(l, 0)[...].astype(F32) + R4[l].astype(F32)
        gi_copy(l).start()

    def a_sent(l):
        for b3 in range(2):
            for r4 in range(2):
                a2_copy(l, b3, r4).wait_send()
        for r4 in range(2):
            a3_copy(l, r4).wait_send()
        a4_copy(l).wait_send()

    def f_at(l, which, q):
        return W.at[l, 1, pl.ds(0, 384), pl.ds(pl.multiple_of(768 * (2 * which + q), 768), 768)]

    def f_half(l, q, half):
        return f_at(l, s, q).at[pl.ds(pl.multiple_of(192 * half, 192), 192), :]

    def f1_copy(l, q):
        return remote(f_at(l, other, q), RC.at[l, q], f1s.at[l, q], f1r.at[l, q], other, r)

    def f2_copy(l, q):
        return remote(f_half(l, q, 1 - x), RX.at[l, q], f2s.at[l, q], f2r.at[l, q], s, rx)

    def f3_copy(l):
        return remote(f_half(l, 1, x), RH.at[l], f3s.at[l], f3r.at[l], s, rh)

    def f_job(l):
        def source(i, carry):
            along_y, along_z = i // 2, lax.rem(i, 2)
            k = 2 * (y + along_y - 2 * y * along_y) + zl + along_z - 2 * zl * along_z

            @pl.when(i > 0)
            def _():
                for item, buf in enumerate((FN, BG, SR)):
                    pltpu.make_async_copy(buf.at[l, k], buf.at[l, k], frecv.at[l, item, k]).wait()

            stats = jnp.concatenate([SR[l, k]] * 16, axis=0).T
            mu, rs, m1, m2 = (stats[:, n : n + 1] for n in range(4))
            for q in (1, 0):
                c = 4 * flip(zh, q) + 2 * zl + y
                cols = pl.ds(pl.multiple_of(384 * c, 384), 384)
                gain = gff[l : l + 1, cols]
                h = dot(FN[l, k], W[1, l, :, cols], 1, 0)
                phi = 0.5 + 0.5 * lax.erf(h * (0.5**0.5))
                xh = (h * phi - mu) * rs
                to = pl.ds(pl.multiple_of(768 * k + 384 * q, 384), 384)
                HG[:, to] = (xh * gain).astype(BF)
                ig = dot(BG[l, k], WO[l, cols, :], 1, 1)
                da = rs * (ig * gain - m1 - xh * m2)
                slope = phi + h * (jnp.exp(-0.5 * h * h) * 0.3989422804014327)
                FG[:, to] = (slope * da).astype(BF)
            return carry

        lax.fori_loop(0, 4, source, 0)
        for q in (1, 0):
            for which, (a, b) in enumerate(((HG, BG), (FG, FN))):
                out = f_at(l, which, q)
                lhs = jnp.concatenate([a[:, 768 * k + 384 * q : 768 * k + 384 * q + 384] for k in range(4)], axis=0)
                for n in range(0, 768, 256):
                    out[:, n : n + 256] = dot(lhs, b[l, :, :, n : n + 256].reshape(512, 256), 0, 0).astype(BF)
            f1_copy(l, q).start()

    def f_stage1(l, q):
        f1_copy(l, q).wait_recv()
        g = f_at(l, s, q)
        g[...] = (g[...].astype(F32) + RC[l, q].astype(F32)).astype(BF)
        f2_copy(l, q).start()

    def f_stage2(l, q):
        f2_copy(l, q).wait_recv()
        g = f_half(l, q, x)
        g[...] = (g[...].astype(F32) + RX[l, q].astype(F32)).astype(BF)
        if q == 1:
            f3_copy(l).start()

    def gi_copy(l):
        return pltpu.make_async_copy(GI.at[l], gi_o.at[l], osem.at[l])

    def go_copy(l):
        return pltpu.make_async_copy(GO.at[l], go_o.at[l], osem.at[2 + l])

    def rows_copies(n, out):
        own = pltpu.make_async_copy(LB.at[n], out.at[me, :], osem.at[4 + n])
        return own, remote(LB.at[n], out.at[me, :], tss.at[n], tsr.at[n], other, r)

    def rows_out(n, out):
        for copy in rows_copies(n, out):
            copy.start()

    def rows_done(n, out):
        own, away = rows_copies(n, out)
        own.wait()
        away.wait()

    def o_copy(l):
        return remote(RX.at[l, 1, :, pl.ds(0, 384)], ORCV.at[l], tss.at[2 + l], tsr.at[2 + l], other, r)

    def f_stage3(l):
        f3_copy(l).wait_recv()
        g = f_half(l, 0, x)

        def final(lo, hi):
            return g[:, lo:hi].astype(F32) + RH[l, :, lo:hi].astype(F32)

        @pl.when(s == 0)
        def _():
            RX[l, 1, :, 0:384] = final(384, 768).astype(BF)
            o_copy(l).start()
            GO[l] = final(0, 384)
            go_copy(l).start()

        @pl.when(s == 1)
        def _():
            GI[l] = final(0, 768)
            gi_copy(l).start()

    def f_sent(l):
        for q in range(2):
            f1_copy(l, q).wait_send()
            f2_copy(l, q).wait_send()
        f3_copy(l).wait_send()

        @pl.when(s == 0)
        def _():
            o_copy(l).wait_send()

    def gain_stage(k):
        to = ((other, r), (s, rx), (s, ry), (s, rl), (s, rh))[k]
        return remote(GS.at[k], GR.at[k], gss.at[k], gsr.at[k], *to)

    def gain_step(k):
        gain_stage(k).wait_recv()
        if k == 4:
            GR[4] = GS[4] + GR[4]
            pltpu.make_async_copy(GR.at[4], gain_o, osem.at[6]).start()
        else:
            GS[k + 1] = GS[k] + GR[k]
            gain_stage(k + 1).start()

    def on0(*steps):
        @pl.when(s == 0)
        def _():
            for step in steps:
                step()

    cot_in.wait()
    share(1, 1, BG)
    UP[...] = BG[1, kf].astype(F32)
    tok_in.wait()
    ST[0] = XS[0, 0].astype(F32)
    GS[0, 14:16, :] = jnp.zeros((2, 768), F32)

    attention_forward(0)
    feed_forward(0)
    attention_forward(1)
    feed_forward(1)
    rows_out(0, lay_o)

    feed_backward(1)
    attention_backward(1)
    BG[0, kf] = UP[...].astype(BF)
    share(1, 0, BG)
    f_job(1)
    on0(lambda: a_job(1))
    f_stage1(1, 1)
    feed_backward(0)
    on0(lambda: a_stage2(1, 1, 1))
    f_stage2(1, 1)
    attention_backward(0)
    LB[1] = UP[...].astype(BF)
    rows_out(1, inp_o)
    on0(lambda: a_stage2(1, 1, 0), lambda: a_stage2(1, 0, 1))
    f_job(0)
    on0(lambda: a_stage3(1, 1))
    f_stage1(0, 1)
    f_stage1(1, 0)
    on0(lambda: a_job(0))
    gain_stage(0).start()
    f_stage1(0, 0)
    on0(lambda: a_stage2(0, 1, 1), lambda: a_stage2(1, 0, 0))
    f_stage2(0, 1)
    on0(lambda: a_stage2(0, 1, 0), lambda: a_stage2(0, 0, 1))
    gain_step(0)
    on0(lambda: a_stage3(0, 1))
    f_stage2(0, 0)
    f_stage2(1, 0)
    on0(lambda: a_stage2(0, 0, 0))
    gain_step(1)
    on0(lambda: a_stage3(1, 0))
    gain_step(2)
    f_stage3(1)
    f_stage3(0)
    gain_step(3)
    on0(lambda: a_stage3(0, 0), lambda: a_stage4(1), lambda: a_stage4(0))
    gain_step(4)

    @pl.when(s == 1)
    def _():
        for l in (1, 0):
            o_copy(l).wait_recv()
            GO[l] = ORCV[l].astype(F32)
            go_copy(l).start()

    for l in range(2):
        f_sent(l)
        on0(lambda: a_sent(l))
        gi_copy(l).wait()
        go_copy(l).wait()
    for k in range(5):
        gain_stage(k).wait_send()
    pltpu.make_async_copy(GR.at[4], gain_o, osem.at[6]).wait()
    rows_done(0, lay_o)
    rows_done(1, inp_o)
    for cond, cp in pending:
        if cond is None:
            cp.wait_send()
        else:
            pl.when(cond)(cp.wait_send)


def hand_over(lay, inp, gi, go, gains, lay_o, inp_o, gi_o, go_o, front_o, mixer_o, feed_o):
    lay_o[...] = lay[...]
    inp_o[...] = inp[...]
    gi_o[...] = gi[...]
    go_o[...] = go[...]
    for l in range(2):
        front_o[l] = gains[2 * l : 2 * l + 2, :]
        for i in range(4):
            feed_o[l : l + 1, 768 * i : 768 * i + 768] = gains[6 + 4 * l + i : 7 + 4 * l + i, :]
    mixer_o[...] = gains[4:6, :]


def fused(tokens, segment_ids, in_proj, out_proj, front_gain, mixer_gain, feed_gain, cotangent):
    vm = pl.BlockSpec(memory_space=pltpu.VMEM)
    hbm = pl.BlockSpec(memory_space=pl.ANY)
    dma = pltpu.SemaphoreType.DMA
    outs = pl.pallas_call(
        body,
        out_shape=(
            jax.ShapeDtypeStruct((256, 768), BF),
            jax.ShapeDtypeStruct((256, 768), BF),
            jax.ShapeDtypeStruct((2, 192, 768), F32),
            jax.ShapeDtypeStruct((2, 192, 384), F32),
            jax.ShapeDtypeStruct((16, 768), F32),
        ),
        in_specs=[hbm, vm, hbm, hbm, vm, vm, vm, hbm],
        out_specs=(hbm,) * 5,
        scratch_shapes=[
            pltpu.VMEM((2, 2, 768, 3072), BF),
            pltpu.VMEM((2, 3072, 768), BF),
            pltpu.VMEM((2, 2, 128, 768), BF),
            pltpu.VMEM((2, 2, 2, 2, 2, 192, 128), BF),
            pltpu.VMEM((2, 2, 4, 128, 768), BF),
            pltpu.VMEM((2, 4, 2, 2, 2, 192, 128), BF),
            pltpu.VMEM((2, 4, 192, 768), BF),
            pltpu.VMEM((2, 2, 192, 768), BF),
            pltpu.VMEM((2, 192, 768), BF),
            pltpu.VMEM((2, 4, 128, 768), BF),
            pltpu.VMEM((2, 4, 128, 768), BF),
            pltpu.VMEM((2, 4, 8, 128), F32),
            pltpu.VMEM((128, 3072), BF),
            pltpu.VMEM((2, 2, 384, 768), BF),
            pltpu.VMEM((2, 2, 192, 768), BF),
            pltpu.VMEM((2, 192, 768), BF),
            pltpu.VMEM((2, 18, 128, 128), BF),
            pltpu.VMEM((2, 6, 256, 128), BF),
            pltpu.VMEM((2, 128, 768), F32),
            pltpu.VMEM((4, 128, 768), F32),
            pltpu.VMEM((128, 768), F32),
            pltpu.VMEM((2, 128, 3072), BF),
            pltpu.VMEM((2, 128, 3072), BF),
            pltpu.VMEM((2, 128, 128), F32),
            pltpu.VMEM((128, 3072), F32),
            pltpu.VMEM((128, 3072), BF),
            pltpu.VMEM((2, 192, 384), BF),
            pltpu.VMEM((2, 128, 768), BF),
            pltpu.VMEM((2, 192, 768), F32),
            pltpu.VMEM((2, 192, 384), F32),
            pltpu.VMEM((5, 16, 768), F32),
            pltpu.VMEM((5, 16, 768), F32),
            dma((2, 2, 4)),
            dma((2, 4)),
            dma((2,)),
            dma((2, 3, 2)),
            dma((2, 3, 4)),
            dma((2, 4)),
            dma((2, 4)),
            dma((2, 2)),
            dma((2, 2)),
            dma((2,)),
            dma((2,)),
            dma((2, 3, 3)),
            dma((2, 3, 4)),
            dma((2, 2)),
            dma((2, 2)),
            dma((2, 2)),
            dma((2, 2)),
            dma((2,)),
            dma((2,)),
            dma((5,)),
            dma((5,)),
            dma((4,)),
            dma((4,)),
            dma((2,)),
            dma((7,)),
        ],
        compiler_params=pltpu.CompilerParams(
            collective_id=0, has_side_effects=True, vmem_limit_bytes=63 * 2**20
        ),
        name="layers",
    )(
        tokens,
        segment_ids.reshape(2, SEQ),
        in_proj,
        out_proj,
        front_gain,
        mixer_gain,
        feed_gain,
        cotangent,
    )
    layer_out, input_grad, in_turned, out_grad, front, mixer, feed = pl.pallas_call(
        hand_over,
        out_shape=(
            jax.ShapeDtypeStruct((256, 768), BF),
            jax.ShapeDtypeStruct((256, 768), BF),
            jax.ShapeDtypeStruct((2, 192, 768), F32),
            jax.ShapeDtypeStruct((2, 192, 384), F32),
            jax.ShapeDtypeStruct((2, 2, 768), F32),
            jax.ShapeDtypeStruct((2, 768), F32),
            jax.ShapeDtypeStruct((2, 3072), F32),
        ),
        in_specs=[vm] * 5,
        out_specs=(vm,) * 7,
        name="hand_over",
    )(*outs)
    return layer_out, input_grad, jnp.swapaxes(in_turned, 1, 2)[None], out_grad, front, mixer, feed


def passed_along(array, axis, by):
    devices = lax.axis_size(axis)
    pairs = [(i, i + by) for i in range(devices) if 0 <= i + by < devices]
    return lax.ppermute(array, axis, pairs)


def layer_norm(values, gain):
    centered = values - jnp.mean(values, axis=-1, keepdims=True)
    spread = jnp.mean(centered * centered, axis=-1, keepdims=True)
    return centered * lax.rsqrt(spread + EPSILON) * gain


def gelu_exact(values):
    return jax.nn.gelu(values, approximate=False)


def visible(segment, seq_count):
    segment_grid = segment.reshape(seq_count, SEQ)
    position = jnp.arange(SEQ)
    causal = position[:, None] >= position[None, :]
    same_doc = segment_grid[:, :, None] == segment_grid[:, None, :]
    return jnp.logical_and(causal[None], same_doc)


def attention_forward(stream, segment, weight, gain_in, gain_mid):
    model_width = stream.shape[1]
    seq_count = stream.shape[0] // SEQ
    head_count = model_width // HEAD_DIM
    normed = layer_norm(stream, gain_in).astype(jnp.bfloat16)
    projected = jnp.dot(
        normed, weight[:, : 3 * model_width], preferred_element_type=jnp.float32
    ).astype(jnp.bfloat16)
    shaped = projected.reshape(seq_count, SEQ, 3, head_count, HEAD_DIM)
    queries = shaped[:, :, 0]
    key_rows = shaped[:, :, 1]
    value_rows = shaped[:, :, 2]
    scores = jnp.einsum(
        "bqhd,bkhd->bhqk", queries, key_rows, preferred_element_type=jnp.float32
    ) * HEAD_DIM ** (-0.5)
    allowed = visible(segment, seq_count)
    scores = jnp.where(allowed[:, None], scores, -1e30)
    row_peak = jnp.max(scores, axis=-1, keepdims=True)
    weights = jnp.exp(scores - row_peak)
    attention = weights / jnp.sum(weights, axis=-1, keepdims=True)
    attention_low = attention.astype(jnp.bfloat16)
    context = jnp.einsum(
        "bhqk,bkhd->bqhd", attention_low, value_rows, preferred_element_type=jnp.float32
    )
    context = context.reshape(-1, model_width)
    inner_normed = layer_norm(context, gain_mid).astype(jnp.bfloat16)
    branch = jnp.dot(
        inner_normed, weight[:, 3 * model_width :], preferred_element_type=jnp.float32
    ).astype(jnp.bfloat16)
    return (
        branch,
        (normed, queries, key_rows, value_rows, attention, attention_low, context, inner_normed),
    )


def attention_backward(stream, segment, weight, gain_in, gain_mid, upstream):
    model_width = stream.shape[1]
    seq_count = stream.shape[0] // SEQ
    head_count = model_width // HEAD_DIM
    scale = HEAD_DIM ** (-0.5)
    branch, kept = attention_forward(stream, segment, weight, gain_in, gain_mid)
    normed, queries, key_rows, value_rows, attention, attention_low, context, inner_normed = kept
    branch_grad = upstream.astype(jnp.bfloat16)
    out_weight_grad = jnp.einsum(
        "tc,td->cd", inner_normed, branch_grad, preferred_element_type=jnp.float32
    )
    inner_grad = jnp.einsum(
        "td,cd->tc", branch_grad, weight[:, 3 * model_width :], preferred_element_type=jnp.float32
    )
    unused_value, mid_pull = jax.vjp(layer_norm, context, gain_mid)
    context_grad, mid_gain_grad = mid_pull(inner_grad)
    context_low = context_grad.astype(jnp.bfloat16).reshape(seq_count, SEQ, head_count, HEAD_DIM)
    prob_grad = jnp.einsum(
        "bqhd,bkhd->bhqk", context_low, value_rows, preferred_element_type=jnp.float32
    )
    value_grad = jnp.einsum(
        "bhqk,bqhd->bkhd", attention_low, context_low, preferred_element_type=jnp.float32
    )
    score_grad = attention * (prob_grad - jnp.sum(attention * prob_grad, axis=-1, keepdims=True))
    score_low = score_grad.astype(jnp.bfloat16)
    query_grad = (
        jnp.einsum("bhqk,bkhd->bqhd", score_low, key_rows, preferred_element_type=jnp.float32)
        * scale
    )
    key_grad = (
        jnp.einsum("bhqk,bqhd->bkhd", score_low, queries, preferred_element_type=jnp.float32)
        * scale
    )
    projected_grad = jnp.stack([query_grad, key_grad, value_grad], axis=2).astype(jnp.bfloat16)
    projected_grad = projected_grad.reshape(-1, 3 * model_width)
    in_weight_grad = jnp.einsum(
        "tc,td->cd", normed, projected_grad, preferred_element_type=jnp.float32
    )
    normed_grad = jnp.einsum(
        "td,cd->tc",
        projected_grad,
        weight[:, : 3 * model_width],
        preferred_element_type=jnp.float32,
    )
    unused_front, front_pull = jax.vjp(layer_norm, stream, gain_in)
    stream_grad, front_gain_grad = front_pull(normed_grad)
    weight_grad = jnp.concatenate([in_weight_grad, out_weight_grad], axis=1)
    return (stream_grad.astype(jnp.bfloat16), weight_grad, front_gain_grad, mid_gain_grad)


def feed_forward(stream, weight_in, weight_out, gain_in, gain_mid):
    normed = layer_norm(stream, gain_in).astype(jnp.bfloat16)
    hidden = jnp.dot(normed, weight_in, preferred_element_type=jnp.float32)
    activated = gelu_exact(hidden)
    inner_normed = layer_norm(activated, gain_mid).astype(jnp.bfloat16)
    branch = jnp.dot(inner_normed, weight_out, preferred_element_type=jnp.float32).astype(
        jnp.bfloat16
    )
    return (branch, (normed, hidden, activated, inner_normed))


def feed_backward(stream, weight_in, weight_out, gain_in, gain_mid, upstream):
    branch, kept = feed_forward(stream, weight_in, weight_out, gain_in, gain_mid)
    normed, hidden, activated, inner_normed = kept
    branch_grad = upstream.astype(jnp.bfloat16)
    out_weight_grad = jnp.einsum(
        "tc,td->cd", inner_normed, branch_grad, preferred_element_type=jnp.float32
    )
    inner_grad = jnp.einsum(
        "td,cd->tc", branch_grad, weight_out, preferred_element_type=jnp.float32
    )
    unused_value, mid_pull = jax.vjp(layer_norm, activated, gain_mid)
    act_grad, mid_gain_grad = mid_pull(inner_grad)
    unused_act, gelu_pull = jax.vjp(gelu_exact, hidden)
    hidden_grad = gelu_pull(act_grad)[0].astype(jnp.bfloat16)
    in_weight_grad = jnp.einsum(
        "tc,td->cd", normed, hidden_grad, preferred_element_type=jnp.float32
    )
    normed_grad = jnp.einsum(
        "td,cd->tc", hidden_grad, weight_in, preferred_element_type=jnp.float32
    )
    unused_front, front_pull = jax.vjp(layer_norm, stream, gain_in)
    stream_grad, front_gain_grad = front_pull(normed_grad)
    return (
        stream_grad.astype(jnp.bfloat16),
        in_weight_grad,
        out_weight_grad,
        front_gain_grad,
        mid_gain_grad,
    )


def accumulate(store, label, value):
    if label in store:
        store[label] = store[label] + value
    else:
        store[label] = value


def generic(tokens, segment_ids, in_proj, out_proj, front_gain, mixer_gain, feed_gain, cotangent):
    own_section = lax.axis_index("section")
    own_weights = in_proj[0]
    layer_total = own_weights.shape[0]
    model_width = front_gain.shape[2]
    hidden_width = feed_gain.shape[1]
    in_store = {}
    out_store = {}
    front_store = {}
    mixer_store = {}
    feed_store = {}

    def run_forward(sublayer, layer_index, stream, segment):
        if sublayer == 0:
            return attention_forward(
                stream,
                segment,
                own_weights[layer_index],
                front_gain[layer_index, 0],
                mixer_gain[layer_index],
            )[0]
        return feed_forward(
            stream,
            own_weights[layer_index],
            out_proj[layer_index],
            front_gain[layer_index, 1],
            feed_gain[layer_index],
        )[0]

    def resting_grads(stream):
        return (
            jnp.zeros(stream.shape, jnp.bfloat16),
            jnp.zeros(own_weights.shape[1:], jnp.float32),
            jnp.zeros(out_proj.shape[1:], jnp.float32),
            jnp.zeros((model_width,), jnp.float32),
            jnp.zeros((model_width,), jnp.float32),
            jnp.zeros((hidden_width,), jnp.float32),
        )

    def run_backward(sublayer, layer_index, stream, segment, upstream):
        if sublayer == 0:
            stream_grad, weight_grad, front_grad, mid_grad = attention_backward(
                stream,
                segment,
                own_weights[layer_index],
                front_gain[layer_index, 0],
                mixer_gain[layer_index],
                upstream,
            )
            return (
                stream_grad,
                weight_grad,
                jnp.zeros(out_proj.shape[1:], jnp.float32),
                front_grad,
                mid_grad,
                jnp.zeros((hidden_width,), jnp.float32),
            )
        stream_grad, in_grad, out_grad, front_grad, mid_grad = feed_backward(
            stream,
            own_weights[layer_index],
            out_proj[layer_index],
            front_gain[layer_index, 1],
            feed_gain[layer_index],
            upstream,
        )
        return (
            stream_grad,
            in_grad,
            out_grad,
            front_grad,
            jnp.zeros((model_width,), jnp.float32),
            mid_grad,
        )

    stream = tokens.astype(jnp.float32)
    upstream = cotangent.astype(jnp.float32)
    kept_streams = []
    for layer_index in range(layer_total):
        for sublayer in (0, 1):
            kept_streams.append(stream)

            def active_forward(stream_in):
                return run_forward(sublayer, layer_index, stream_in, segment_ids)

            def resting_forward(stream_in):
                return jnp.zeros(stream_in.shape, jnp.bfloat16)

            own_branch = lax.cond(own_section == sublayer, active_forward, resting_forward, stream)
            if sublayer == 0:
                received = passed_along(own_branch, "section", 1)
            else:
                received = passed_along(own_branch, "section", -1)
            stream = stream + jnp.where(own_section == sublayer, own_branch, received).astype(
                jnp.float32
            )
    for position in reversed(range(2 * layer_total)):
        layer_index, sublayer = divmod(position, 2)

        def active_backward(operand):
            return run_backward(sublayer, layer_index, operand[0], segment_ids, operand[1])

        def resting_backward(operand):
            return resting_grads(operand[0])

        grads = lax.cond(
            own_section == sublayer,
            active_backward,
            resting_backward,
            (kept_streams[position], upstream),
        )
        own_grad = grads[0]
        accumulate(in_store, layer_index, grads[1])
        accumulate(out_store, layer_index, grads[2])
        accumulate(front_store, (layer_index, sublayer), grads[3])
        accumulate(mixer_store, layer_index, grads[4])
        accumulate(feed_store, layer_index, grads[5])
        if sublayer == 0:
            received = passed_along(own_grad, "section", 1)
        else:
            received = passed_along(own_grad, "section", -1)
        upstream = upstream + jnp.where(own_section == sublayer, own_grad, received).astype(
            jnp.float32
        )
    in_total = jnp.stack([in_store[layer_index] for layer_index in range(layer_total)])
    out_total = jnp.stack([out_store[layer_index] for layer_index in range(layer_total)])
    front_total = jnp.stack(
        [
            jnp.stack([front_store[layer_index, 0], front_store[layer_index, 1]])
            for layer_index in range(layer_total)
        ]
    )
    mixer_total = jnp.stack([mixer_store[layer_index] for layer_index in range(layer_total)])
    feed_total = jnp.stack([feed_store[layer_index] for layer_index in range(layer_total)])
    first_grad = lax.psum_scatter(in_total[None], "rows", scatter_dimension=3, tiled=True)
    partial_sum = lax.psum_scatter(
        out_total.astype(jnp.bfloat16), "section", scatter_dimension=2, tiled=True
    ).astype(jnp.float32)
    second_grad = lax.psum_scatter(partial_sum, "rows", scatter_dimension=1, tiled=True)
    gain_totals = lax.psum((front_total, mixer_total, feed_total), ("section", "rows"))
    return (
        stream.astype(jnp.bfloat16),
        upstream.astype(jnp.bfloat16),
        first_grad,
        second_grad,
        gain_totals[0],
        gain_totals[1],
        gain_totals[2],
    )


def solution(mesh):
    local = fused if mesh.shape["rows"] == 16 and mesh.shape["section"] == 2 else generic
    return jax.shard_map(
        local,
        mesh=mesh,
        in_specs=(
            P("rows", None),
            P("rows"),
            P("section", None, None, None),
            P(),
            P(),
            P(),
            P(),
            P("rows", None),
        ),
        out_specs=(
            P("rows", None),
            P("rows", None),
            P("section", None, None, "rows"),
            P(None, "rows", "section"),
            P(),
            P(),
            P(),
        ),
        check_vma=False,
    )
```

```python
import jax
import jax.numpy as jnp
from jax import lax
from jax.experimental import pallas as pl
from jax.experimental.pallas import tpu as pltpu
from jax.sharding import PartitionSpec as P

HEAD_DIM = 64
SEQ = 128
EPSILON = 1e-05
MESH = pl.DeviceIdType.MESH
BF = jnp.bfloat16
F32 = jnp.float32


def dot(a, b, ca, cb):
    return lax.dot_general(a, b, (((ca,), (cb,)), ((), ())), preferred_element_type=F32)


def fold(v):
    parts = [v[:, i : i + 128] for i in range(0, v.shape[1], 128)]
    total = parts[0]
    for part in parts[1:]:
        total = total + part
    return total


def hat(v):
    centered = v - jnp.mean(v, axis=-1, keepdims=True)
    rs = lax.rsqrt(jnp.mean(centered * centered, axis=-1, keepdims=True) + EPSILON)
    return centered * rs, rs


def hat_back(xh, rs, dxh):
    m1 = jnp.mean(dxh, axis=-1, keepdims=True)
    m2 = jnp.mean(dxh * xh, axis=-1, keepdims=True)
    return rs * (dxh - m1 - xh * m2)


def flip(bit, by):
    return 1 - bit if by else bit


AX, AM, AY = range(3)


def body(
    tok, seg, in_hbm, out_hbm, gf, gm, gff, cot,
    lay_o, inp_o, gi_o, go_o, gain_o,
    W, WO, XS, YS, XR, YR, R2, R3, R4, FN, BG, SR, FG, RC, RX, RH,
    QKV, PB, CTX, ST, UP, XH, GP, RSB, BIG, HG, ORCV, LB, GI, GO, GS, GR,
    wsem, wsend, wosem, isend, irecv, s2s, s2r, s3s, s3r, s4s, s4r,
    fsend, frecv, f1s, f1r, f2s, f2r, f3s, f3r, gss, gsr, tss, tsr, tksem, osem,
):
    s = lax.axis_index("section")
    r = lax.axis_index("rows")
    x = lax.rem(r, 2)
    y = lax.rem(r // 2, 2)
    zl = lax.rem(r // 4, 2)
    zh = r // 8
    dx, dy, dl, dh = 1 - 2 * x, 2 - 4 * y, 4 - 8 * zl, 8 - 16 * zh
    rx, ry, rl, rh = r + dx, r + dy, r + dl, r + dh
    share_bit, share_row, across_row = (zh, zl), (rh, rl), (r + dy + dh, r + dy + dl)
    rest_bit, rest_row = (zl, zh), (rl, rh)
    other = 1 - s
    pending = []

    def remote(src, dst, ssem, rsem, sec, row):
        return pltpu.make_async_remote_copy(
            src_ref=src, dst_ref=dst, send_sem=ssem, recv_sem=rsem, device_id=(sec, row), device_id_type=MESH
        )

    me = pl.ds(pl.multiple_of(s * 128, 128), 128)
    kf = [2 * y + bit for bit in share_bit]
    tok_in = pltpu.make_async_copy(tok.at[me, :], XS.at[0, 0], tksem.at[0])
    cot_in = pltpu.make_async_copy(cot.at[me, :], BG.at[1, kf[1]], tksem.at[1])
    tok_in.start()
    cot_in.start()
    for l in range(2):
        for j in range(4):
            cols = pl.ds(768 * j, 768)
            pltpu.make_async_copy(in_hbm.at[0, l, :, cols], W.at[s, l, :, cols], wsem.at[s, l, j]).start()
    wo = [pltpu.make_async_copy(out_hbm.at[l], WO.at[l], wosem.at[l]) for l in range(2)]
    wo[0].start()
    wo[1].start()

    barrier = pltpu.get_barrier_semaphore()
    peers = [(other, r), (0, rx), (1, rx), (s, ry), (s, rl), (s, rh), (s, across_row[0]), (s, across_row[1])]
    for peer in peers:
        pl.semaphore_signal(barrier, inc=1, device_id=peer, device_id_type=MESH)
    pl.semaphore_wait(barrier, len(peers))

    for l in range(2):
        for j in range(4):
            cols = pl.ds(768 * j, 768)
            cp = remote(in_hbm.at[0, l, :, cols], W.at[s, l, :, cols], wsend.at[l, j], wsem.at[s, l, j], other, r)
            cp.start()
            pending.append((None, cp))

    def wait_w(sec, l, j):
        cols = pl.ds(768 * j, 768)
        pltpu.make_async_copy(in_hbm.at[0, l, :, cols], W.at[sec, l, :, cols], wsem.at[sec, l, j]).wait()

    ka = 2 * x + s

    def exchange(item, l, own, far, dst):
        @pl.when(s == 0)
        def _():
            pltpu.make_async_copy(own, dst.at[ka], irecv.at[l, item, ka]).start()

        cp_own = remote(own, dst.at[ka], isend.at[l, item, 0], irecv.at[l, item, ka], 0, r)
        cp_far = remote(far, dst.at[ka], isend.at[l, item, 1], irecv.at[l, item, ka], 0, rx)
        cp_far.start()
        pl.when(s == 1)(cp_own.start)
        pending.append((None, cp_far))
        pending.append((s == 1, cp_own))

    def wait_item(l, item, dst):
        for k in range(4):
            pltpu.make_async_copy(dst.at[k], dst.at[k], irecv.at[l, item, k]).wait()

    def send_normed(l):
        exchange(AX, l, XS.at[0, l], XS.at[0, l], XR.at[l, 0])

    def send_mixer(l):
        exchange(AM, l, XS.at[1, l], XS.at[1, l], XR.at[l, 1])

    def send_ya(l):
        exchange(AY, l, YS.at[l, :, :, :, x], YS.at[l, :, :, :, 1 - x], YR.at[l])

    def store_y(l, c, block):
        turned = block.T
        YS[l, c // 4, (c // 2) % 2, c % 2, 0] = turned[:192]
        YS[l, c // 4, (c // 2) % 2, c % 2, 1] = turned[192:]


    def share(item, l, buf):
        for p, row in enumerate((ry, share_row[l], across_row[l])):
            own = buf.at[l, kf[l]]
            cp = remote(own, own, fsend.at[l, item, p], frecv.at[l, item, kf[l]], s, row)
            cp.start()
            pending.append((None, cp))

    lane = lax.broadcasted_iota(jnp.int32, (1, 128), 1)
    mk0 = jnp.where(lane < 64, 1.0, 0.0).astype(BF)
    mk1 = jnp.where(lane < 64, 0.0, 1.0).astype(BF)

    def allowed():
        ids = jnp.broadcast_to(seg[pl.ds(s, 1), :], (128, 128))
        row = lax.broadcasted_iota(jnp.int32, (128, 128), 0)
        col = lax.broadcasted_iota(jnp.int32, (128, 128), 1)
        one = jnp.logical_and(ids == ids.T, row >= col)
        return jnp.concatenate([one, one], axis=0)

    def split0(v):
        return jnp.concatenate([v * mk0, v * mk1], axis=0)

    scale = HEAD_DIM ** (-0.5)
    width = 3072.0

    def attention_forward(l):
        stream = ST[2 * l]
        xh, rs = hat(stream)
        XS[0, l] = (xh * gf[l, 0:1, :]).astype(BF)
        send_normed(l)
        for j in range(3):
            wait_w(0, l, j)
            for i in range(2):
                c = 768 * j + 384 * i
                part = dot(XS[0, l], W[0, l, :, c : c + 384], 1, 0).astype(BF)
                for p in range(3):
                    QKV[l, c // 128 + p] = part[:, 128 * p : 128 * p + 128]
        visible = allowed()

        def pair(p):
            q, k, v = QKV[l, p], QKV[l, 6 + p], QKV[l, 12 + p]
            scores = dot(split0(q), k, 1, 1) * scale
            scores = jnp.where(visible, scores, -1e30)
            e = jnp.exp(scores - jnp.max(scores, axis=-1, keepdims=True))
            probs = e * (1.0 / jnp.sum(e, axis=-1, keepdims=True))
            low = probs.astype(BF)
            PB[l, p] = low
            both = jnp.concatenate([low[:128], low[128:]], axis=1)
            return dot(both, split0(v), 1, 0)

        for p in range(6):
            CTX[l, :, 128 * p : 128 * p + 128] = pair(p)
        xh, rs = hat(CTX[l])
        XS[1, l] = (xh * gm[l : l + 1, :]).astype(BF)
        send_mixer(l)
        wait_w(0, l, 3)
        branch = dot(XS[1, l], W[0, l, :, 2304:], 1, 0).astype(BF)
        ST[2 * l + 1] = stream + branch.astype(F32)

    def feed_forward(l):
        stream = ST[2 * l + 1]
        xh, rs = hat(stream)
        FN[l, kf[l]] = (xh * gf[l, 1:2, :]).astype(BF)
        share(0, l, FN)

        def hidden(j, total):
            for i in range(2):
                c = pl.ds(pl.multiple_of(768 * j + 384 * i, 384), 384)
                h = dot(FN[l, kf[l]], W[1, l, :, c], 1, 0)
                phi = 0.5 + 0.5 * lax.erf(h * (0.5**0.5))
                act = h * phi
                BIG[:, c] = act
                GP[l, :, c] = (phi + h * (jnp.exp(-0.5 * h * h) * 0.3989422804014327)).astype(BF)
                total = total + fold(act)
            return total

        total = jnp.zeros((128, 128), F32)
        for j in range(4):
            wait_w(1, l, j)
            total = hidden(j, total)
        mu = jnp.sum(total, axis=-1, keepdims=True) / width

        def spread(c, acc):
            cen = BIG[:, pl.ds(pl.multiple_of(384 * c, 384), 384)] - mu
            return acc + fold(cen * cen)

        acc = lax.fori_loop(0, 8, spread, jnp.zeros((128, 128), F32))
        rs = lax.rsqrt(jnp.sum(acc, axis=-1, keepdims=True) / width + EPSILON)
        RSB[l] = jnp.where(lane == 0, mu, rs)

        def scaled(c, carry):
            cols = pl.ds(pl.multiple_of(384 * c, 384), 384)
            xh = (BIG[:, cols] - mu) * rs
            XH[l, :, cols] = xh.astype(BF)
            HG[:, cols] = (xh * gff[l : l + 1, cols]).astype(BF)
            return carry

        lax.fori_loop(0, 8, scaled, 0)
        wo[l].wait()
        for n in range(0, 768, 256):
            branch = dot(HG[...], WO[l, :, n : n + 256], 1, 0).astype(BF)
            out = stream[:, n : n + 256] + branch.astype(F32)
            if l == 0:
                ST[2, :, n : n + 256] = out
            else:
                LB[0, :, n : n + 256] = out.astype(BF)

    held = {}

    def feed_backward_0(l):
        def first(c, carry):
            a1, a2 = carry
            for i in range(2):
                at = 384 * (2 * c + i)
                cols = pl.ds(pl.multiple_of(at, 384), 384)
                ig = dot(BG[l, kf[l]], WO[l, cols, :], 1, 1)
                xh = XH[l, :, cols].astype(F32)
                GS[0, pl.ds(6 + 4 * l + c, 1), 384 * i : 384 * i + 384] = jnp.sum(ig * xh, axis=0, keepdims=True)
                dxh = ig * gff[l : l + 1, cols]
                BIG[:, cols] = dxh
                a1 = a1 + fold(dxh)
                a2 = a2 + fold(dxh * xh)
            return a1, a2

        zero = jnp.zeros((128, 128), F32)
        a1, a2 = lax.fori_loop(0, 4, first, (zero, zero))
        m1 = jnp.sum(a1, axis=-1, keepdims=True) / width
        m2 = jnp.sum(a2, axis=-1, keepdims=True) / width
        kept = RSB[l]
        rs = kept[:, 1:2]
        stats = jnp.where(lane < 2, kept, jnp.where(lane == 2, m1, m2))
        SR[l, kf[l]] = stats.T[0:8]
        share(2, l, SR)
        held[l] = m1, m2, rs

    def feed_backward_1(l):
        m1, m2, rs = held[l]

        def second(c, carry):
            cols = pl.ds(pl.multiple_of(384 * c, 384), 384)
            da = rs * (BIG[:, cols] - m1 - XH[l, :, cols].astype(F32) * m2)
            HG[:, cols] = (GP[l, :, cols].astype(F32) * da).astype(BF)
            return carry

        lax.fori_loop(0, 8, second, 0)
        for n in range(0, 768, 256):
            BIG[:, n : n + 256] = dot(HG[...], W[1, l, n : n + 256, :], 1, 1)
        front_back(l, 1)

    def front_back(l, sub):
        ng = BIG[:, 0:768]
        xh, rs = hat(ST[2 * l + sub])
        GS[0, 2 * l + sub : 2 * l + sub + 1, :] = jnp.sum(ng * xh, axis=0, keepdims=True)
        UP[...] = UP[...] + hat_back(xh, rs, ng * gf[l, sub : sub + 1, :]).astype(BF).astype(F32)

    def attention_pair_back(l, p):
        q, k, v = QKV[l, p], QKV[l, 6 + p], QKV[l, 12 + p]
        probs_low = PB[l, p]
        probs = probs_low.astype(F32)
        dcc = split0(HG[:, 2304 + 128 * p : 2432 + 128 * p])
        pg = dot(dcc, v, 1, 1)
        ds = (probs * (pg - jnp.sum(probs * pg, axis=-1, keepdims=True))).astype(BF)
        both = jnp.concatenate([ds[:128], ds[128:]], axis=1)
        dq = dot(both, split0(k), 1, 0) * scale
        dk = dot(ds, split0(q), 0, 0) * scale
        dv = dot(probs_low, dcc, 0, 0)
        return dq.astype(BF), dk.astype(BF), dv.astype(BF)

    def attention_group_back(l, g):
        parts = [attention_pair_back(l, 3 * g + i) for i in range(3)]
        for which in range(3):
            block = jnp.concatenate([part[which] for part in parts], axis=1)
            at = 768 * which + 384 * g
            HG[:, at : at + 384] = block
            store_y(l, 2 * which + g, block)

    def attention_backward_0(l):
        low = UP[...].astype(BF)
        for i in range(2):
            store_y(l, 6 + i, low[:, 384 * i : 384 * i + 384])
        for n in range(0, 768, 256):
            BIG[:, n : n + 256] = dot(low, W[0, l, n : n + 256, 2304:], 1, 1)
        ig = BIG[:, 0:768]
        xh, rs = hat(CTX[l])
        GS[0, 4 + l : 5 + l, :] = jnp.sum(ig * xh, axis=0, keepdims=True)
        dctx = hat_back(xh, rs, ig * gm[l : l + 1, :]).astype(BF)
        HG[:, 2304:] = dctx
        attention_group_back(l, 0)

    def attention_backward_1(l):
        attention_group_back(l, 1)
        send_ya(l)

    def attention_backward_2(l):
        for n in range(0, 768, 256):
            BIG[:, n : n + 256] = dot(HG[:, 0:2304], W[0, l, n : n + 256, 0:2304], 1, 1)
        front_back(l, 0)

    def g_at(l, n):
        return W.at[1 - l, 1, pl.ds(384 + 192 * (n // 4), 192), pl.ds(768 * (n % 4), 768)]

    def piece(b2, b3, r4):
        return 4 * b2 + 2 * b3 + 1 if r4 else 2 * b2 + 4 * b3

    def a2_copy(l, b3, r4):
        at = 2 * b3 + r4
        src = g_at(l, piece(1, b3, r4))
        return remote(src, R2.at[l, at], s2s.at[l, at], s2r.at[l, at], 0, ry if r4 else rl)

    def a3_copy(l, r4):
        src = g_at(l, piece(0, 1, r4))
        return remote(src, R3.at[l, r4], s3s.at[l, r4], s3r.at[l, r4], 0, rl if r4 else ry)

    def a4_copy(l):
        return remote(g_at(l, 1), R4.at[l], s4s.at[l], s4r.at[l], 0, rh)

    def a_job(l):
        wait_item(l, AX, XR.at[l, 0])
        wait_item(l, AM, XR.at[l, 1])
        wait_item(l, AY, YR.at[l])
        for r4, r3 in ((1, 1), (1, 0), (0, 1), (0, 0)):
            h, low = flip(zh, r4), flip(zl, r3)
            xi = h * low
            rows = []
            for r2 in (1, 0):
                rows.append(jnp.concatenate([YR[l, k, h, low, flip(y, r2)] for k in range(4)], axis=1))
            lhs = jnp.concatenate(rows, axis=0)
            for n in range(0, 768, 256):
                res = dot(lhs, XR[l, xi, :, :, n : n + 256].reshape(512, 256), 1, 0).astype(BF)
                g_at(l, 4 + 2 * r3 + r4)[:, n : n + 256] = res[:192]
                g_at(l, 2 * r3 + r4)[:, n : n + 256] = res[192:]
            if r4 == 1:
                a2_copy(l, r3, 1).start()
            elif r3 == 1:
                a2_copy(l, 1, 0).start()
                a2_copy(l, 0, 0).start()

    def a_stage2(l, b3, r4):
        a2_copy(l, b3, r4).wait_recv()
        g = g_at(l, piece(0, b3, r4))
        g[...] = (g[...].astype(F32) + R2[l, 2 * b3 + r4].astype(F32)).astype(BF)
        if b3 == 1:
            a3_copy(l, r4).start()

    def a_stage3(l, r4):
        a3_copy(l, r4).wait_recv()
        g = g_at(l, r4)
        g[...] = (g[...].astype(F32) + R3[l, r4].astype(F32)).astype(BF)
        if r4 == 1:
            a4_copy(l).start()

    def a_stage4(l):
        a4_copy(l).wait_recv()
        GI[l] = g_at(l, 0)[...].astype(F32) + R4[l].astype(F32)
        gi_copy(l).start()

    def a_sent(l):
        for b3 in range(2):
            for r4 in range(2):
                a2_copy(l, b3, r4).wait_send()
        for r4 in range(2):
            a3_copy(l, r4).wait_send()
        a4_copy(l).wait_send()

    def f_at(l, which, q):
        return W.at[l, 1, pl.ds(0, 384), pl.ds(pl.multiple_of(768 * (2 * which + q), 768), 768)]

    def f_rows(half, chunk=None):
        if chunk is None:
            return pl.ds(pl.multiple_of(192 * half, 192), 192)
        return pl.ds(pl.multiple_of(192 * half + 96 * chunk, 96), 96)

    def f1_copy(l, q):
        return remote(f_at(l, other, q), RC.at[l, q], f1s.at[l, q], f1r.at[l, q], other, r)

    def f_step(step):
        return (0, None, pl.ds(0, 192)) if step == 0 else (1, step - 1, pl.ds(96 * (step - 1), 96))

    def f2_copy(l, step):
        q, chunk, rows = f_step(step)
        src = f_at(l, s, q).at[f_rows(1 - x, chunk), :]
        return remote(src, RX.at[l, q, rows, :], f2s.at[l, step], f2r.at[l, step], s, rx)

    def f3_copy(l, chunk):
        src = f_at(l, s, 1).at[f_rows(x, chunk), :]
        return remote(src, RH.at[l, pl.ds(96 * chunk, 96), :], f3s.at[l, chunk], f3r.at[l, chunk], s, rest_row[l])

    def f_job(l):
        def source(i, carry):
            along_y, along_z = i // 2, lax.rem(i, 2)
            bit = share_bit[l]
            k = 2 * (y + along_y - 2 * y * along_y) + bit + along_z - 2 * bit * along_z

            @pl.when(i > 0)
            def _():
                for item, buf in enumerate((FN, BG, SR)):
                    pltpu.make_async_copy(buf.at[l, k], buf.at[l, k], frecv.at[l, item, k]).wait()

            stats = jnp.concatenate([SR[l, k]] * 16, axis=0).T
            mu, rs, m1, m2 = (stats[:, n : n + 1] for n in range(4))
            for q in (1, 0):
                rest = flip(rest_bit[l], q)
                c = (4 * rest + 2 * zl if l == 1 else 4 * zh + 2 * rest) + y
                cols = pl.ds(pl.multiple_of(384 * c, 384), 384)
                gain = gff[l : l + 1, cols]
                h = dot(FN[l, k], W[1, l, :, cols], 1, 0)
                phi = 0.5 + 0.5 * lax.erf(h * (0.5**0.5))
                xh = (h * phi - mu) * rs
                to = pl.ds(pl.multiple_of(768 * k + 384 * q, 384), 384)
                HG[:, to] = (xh * gain).astype(BF)
                ig = dot(BG[l, k], WO[l, cols, :], 1, 1)
                da = rs * (ig * gain - m1 - xh * m2)
                slope = phi + h * (jnp.exp(-0.5 * h * h) * 0.3989422804014327)
                FG[:, to] = (slope * da).astype(BF)
            return carry

        lax.fori_loop(0, 4, source, 0)
        for q in (1, 0):
            for which, (a, b) in enumerate(((HG, BG), (FG, FN))):
                out = f_at(l, which, q)
                lhs = jnp.concatenate([a[:, 768 * k + 384 * q : 768 * k + 384 * q + 384] for k in range(4)], axis=0)
                for n in range(0, 768, 256):
                    out[:, n : n + 256] = dot(lhs, b[l, :, :, n : n + 256].reshape(512, 256), 0, 0).astype(BF)
            f1_copy(l, q).start()

    def f_stage1(l, q):
        f1_copy(l, q).wait_recv()
        g, got = f_at(l, s, q), RC.at[l, q]

        def add(rows):
            g[rows, :] = (g[rows, :].astype(F32) + got[rows, :].astype(F32)).astype(BF)

        for step in (1, 2) if q else (0,):
            add(f_rows(1 - x, f_step(step)[1]))
            f2_copy(l, step).start()
        add(f_rows(x))

    def f_stage2(l, step):
        f2_copy(l, step).wait_recv()
        q, chunk, rows = f_step(step)
        g = f_at(l, s, q).at[f_rows(x, chunk), :]
        g[...] = (g[...].astype(F32) + RX[l, q, rows, :].astype(F32)).astype(BF)
        if q == 1:
            f3_copy(l, chunk).start()

    def gi_copy(l):
        return pltpu.make_async_copy(GI.at[l], gi_o.at[l], osem.at[l])

    def go_copy(l):
        return pltpu.make_async_copy(GO.at[l], go_o.at[l], osem.at[2 + l])

    def rows_copies(n, out):
        own = pltpu.make_async_copy(LB.at[n], out.at[me, :], osem.at[4 + n])
        return own, remote(LB.at[n], out.at[me, :], tss.at[n], tsr.at[n], other, r)

    def rows_out(n, out):
        for copy in rows_copies(n, out):
            copy.start()

    def rows_done(n, out):
        own, away = rows_copies(n, out)
        own.wait()
        away.wait()

    def o_copy(l):
        return remote(RX.at[l, 1, :, pl.ds(0, 384)], ORCV.at[l], tss.at[2 + l], tsr.at[2 + l], other, r)

    def f_stage3(l):
        f3_copy(l, 0).wait_recv()
        f3_copy(l, 1).wait_recv()
        g = f_at(l, s, 0).at[f_rows(x), :]

        def final(lo, hi):
            return g[:, lo:hi].astype(F32) + RH[l, :, lo:hi].astype(F32)

        @pl.when(s == 0)
        def _():
            RX[l, 1, :, 0:384] = final(384, 768).astype(BF)
            o_copy(l).start()
            GO[l] = final(0, 384)
            go_copy(l).start()

        @pl.when(s == 1)
        def _():
            GI[l] = final(0, 768)
            gi_copy(l).start()

    def f_sent(l):
        for q in range(2):
            f1_copy(l, q).wait_send()
            f3_copy(l, q).wait_send()
        for step in range(3):
            f2_copy(l, step).wait_send()

        @pl.when(s == 0)
        def _():
            o_copy(l).wait_send()

    def gain_stage(k):
        to = ((other, r), (s, rl), (s, ry), (s, rh), (s, rx))[k]
        return remote(GS.at[k], GR.at[k], gss.at[k], gsr.at[k], *to)

    def gain_step(k):
        gain_stage(k).wait_recv()
        if k == 4:
            GR[4] = GS[4] + GR[4]
            pltpu.make_async_copy(GR.at[4], gain_o, osem.at[6]).start()
        else:
            GS[k + 1] = GS[k] + GR[k]
            gain_stage(k + 1).start()

    def on0(*steps):
        @pl.when(s == 0)
        def _():
            for step in steps:
                step()

    cot_in.wait()
    share(1, 1, BG)
    UP[...] = BG[1, kf[1]].astype(F32)
    tok_in.wait()
    ST[0] = XS[0, 0].astype(F32)
    GS[0, 14:16, :] = jnp.zeros((2, 768), F32)

    attention_forward(0)
    feed_forward(0)
    attention_forward(1)
    feed_forward(1)
    rows_out(0, lay_o)

    feed_backward_0(1)
    feed_backward_1(1)
    attention_backward_0(1)
    attention_backward_1(1)
    attention_backward_2(1)
    BG[0, kf[0]] = UP[...].astype(BF)
    share(1, 0, BG)
    f_job(1)
    feed_backward_0(0)
    f_stage1(1, 1)
    on0(lambda: a_job(1))
    feed_backward_1(0)
    attention_backward_0(0)
    attention_backward_1(0)
    attention_backward_2(0)
    LB[1] = UP[...].astype(BF)
    rows_out(1, inp_o)
    f_stage2(1, 1)
    on0(lambda: a_stage2(1, 1, 1))
    f_stage2(1, 2)
    gain_stage(0).start()
    gain_step(0)
    f_job(0)
    f_stage1(1, 0)
    on0(lambda: a_job(0))
    gain_step(1)
    on0(lambda: a_stage2(1, 1, 0), lambda: a_stage2(1, 0, 1))
    f_stage1(0, 1)
    on0(lambda: a_stage2(1, 0, 0), lambda: a_stage2(0, 1, 1), lambda: a_stage3(1, 1))
    f_stage1(0, 0)
    on0(lambda: a_stage2(0, 1, 0), lambda: a_stage2(0, 0, 1), lambda: a_stage2(0, 0, 0))
    gain_step(2)
    f_stage2(0, 1)
    f_stage2(1, 0)
    f_stage2(0, 2)
    on0(lambda: a_stage3(0, 1))
    gain_step(3)
    on0(lambda: a_stage3(0, 0), lambda: a_stage3(1, 0))
    f_stage2(0, 0)
    on0(lambda: a_stage4(1))
    gain_step(4)
    f_stage3(1)
    f_stage3(0)
    on0(lambda: a_stage4(0))

    @pl.when(s == 1)
    def _():
        for l in (1, 0):
            o_copy(l).wait_recv()
            GO[l] = ORCV[l].astype(F32)
            go_copy(l).start()

    for l in range(2):
        f_sent(l)
        on0(lambda: a_sent(l))
        gi_copy(l).wait()
        go_copy(l).wait()
    for k in range(5):
        gain_stage(k).wait_send()
    pltpu.make_async_copy(GR.at[4], gain_o, osem.at[6]).wait()
    rows_done(0, lay_o)
    rows_done(1, inp_o)
    for cond, cp in pending:
        if cond is None:
            cp.wait_send()
        else:
            pl.when(cond)(cp.wait_send)


def hand_over(lay, inp, gi, go, gains, lay_o, inp_o, gi_o, go_o, front_o, mixer_o, feed_o):
    lay_o[...] = lay[...]
    inp_o[...] = inp[...]
    gi_o[...] = gi[...]
    go_o[...] = go[...]
    for l in range(2):
        front_o[l] = gains[2 * l : 2 * l + 2, :]
        for i in range(4):
            feed_o[l : l + 1, 768 * i : 768 * i + 768] = gains[6 + 4 * l + i : 7 + 4 * l + i, :]
    mixer_o[...] = gains[4:6, :]


def fused(tokens, segment_ids, in_proj, out_proj, front_gain, mixer_gain, feed_gain, cotangent):
    vm = pl.BlockSpec(memory_space=pltpu.VMEM)
    hbm = pl.BlockSpec(memory_space=pl.ANY)
    dma = pltpu.SemaphoreType.DMA
    outs = pl.pallas_call(
        body,
        out_shape=(
            jax.ShapeDtypeStruct((256, 768), BF),
            jax.ShapeDtypeStruct((256, 768), BF),
            jax.ShapeDtypeStruct((2, 192, 768), F32),
            jax.ShapeDtypeStruct((2, 192, 384), F32),
            jax.ShapeDtypeStruct((16, 768), F32),
        ),
        in_specs=[hbm, vm, hbm, hbm, vm, vm, vm, hbm],
        out_specs=(hbm,) * 5,
        scratch_shapes=[
            pltpu.VMEM((2, 2, 768, 3072), BF),
            pltpu.VMEM((2, 3072, 768), BF),
            pltpu.VMEM((2, 2, 128, 768), BF),
            pltpu.VMEM((2, 2, 2, 2, 2, 192, 128), BF),
            pltpu.VMEM((2, 2, 4, 128, 768), BF),
            pltpu.VMEM((2, 4, 2, 2, 2, 192, 128), BF),
            pltpu.VMEM((2, 4, 192, 768), BF),
            pltpu.VMEM((2, 2, 192, 768), BF),
            pltpu.VMEM((2, 192, 768), BF),
            pltpu.VMEM((2, 4, 128, 768), BF),
            pltpu.VMEM((2, 4, 128, 768), BF),
            pltpu.VMEM((2, 4, 8, 128), F32),
            pltpu.VMEM((128, 3072), BF),
            pltpu.VMEM((2, 2, 384, 768), BF),
            pltpu.VMEM((2, 2, 192, 768), BF),
            pltpu.VMEM((2, 192, 768), BF),
            pltpu.VMEM((2, 18, 128, 128), BF),
            pltpu.VMEM((2, 6, 256, 128), BF),
            pltpu.VMEM((2, 128, 768), F32),
            pltpu.VMEM((4, 128, 768), F32),
            pltpu.VMEM((128, 768), F32),
            pltpu.VMEM((2, 128, 3072), BF),
            pltpu.VMEM((2, 128, 3072), BF),
            pltpu.VMEM((2, 128, 128), F32),
            pltpu.VMEM((128, 3072), F32),
            pltpu.VMEM((128, 3072), BF),
            pltpu.VMEM((2, 192, 384), BF),
            pltpu.VMEM((2, 128, 768), BF),
            pltpu.VMEM((2, 192, 768), F32),
            pltpu.VMEM((2, 192, 384), F32),
            pltpu.VMEM((5, 16, 768), F32),
            pltpu.VMEM((5, 16, 768), F32),
            dma((2, 2, 4)),
            dma((2, 4)),
            dma((2,)),
            dma((2, 3, 2)),
            dma((2, 3, 4)),
            dma((2, 4)),
            dma((2, 4)),
            dma((2, 2)),
            dma((2, 2)),
            dma((2,)),
            dma((2,)),
            dma((2, 3, 3)),
            dma((2, 3, 4)),
            dma((2, 2)),
            dma((2, 2)),
            dma((2, 3)),
            dma((2, 3)),
            dma((2, 2)),
            dma((2, 2)),
            dma((5,)),
            dma((5,)),
            dma((4,)),
            dma((4,)),
            dma((2,)),
            dma((7,)),
        ],
        compiler_params=pltpu.CompilerParams(
            collective_id=0, has_side_effects=True, vmem_limit_bytes=63 * 2**20
        ),
        name="layers",
    )(
        tokens,
        segment_ids.reshape(2, SEQ),
        in_proj,
        out_proj,
        front_gain,
        mixer_gain,
        feed_gain,
        cotangent,
    )
    layer_out, input_grad, in_turned, out_grad, front, mixer, feed = pl.pallas_call(
        hand_over,
        out_shape=(
            jax.ShapeDtypeStruct((256, 768), BF),
            jax.ShapeDtypeStruct((256, 768), BF),
            jax.ShapeDtypeStruct((2, 192, 768), F32),
            jax.ShapeDtypeStruct((2, 192, 384), F32),
            jax.ShapeDtypeStruct((2, 2, 768), F32),
            jax.ShapeDtypeStruct((2, 768), F32),
            jax.ShapeDtypeStruct((2, 3072), F32),
        ),
        in_specs=[vm] * 5,
        out_specs=(vm,) * 7,
        name="hand_over",
    )(*outs)
    return layer_out, input_grad, jnp.swapaxes(in_turned, 1, 2)[None], out_grad, front, mixer, feed


def passed_along(array, axis, by):
    devices = lax.axis_size(axis)
    pairs = [(i, i + by) for i in range(devices) if 0 <= i + by < devices]
    return lax.ppermute(array, axis, pairs)


def layer_norm(values, gain):
    centered = values - jnp.mean(values, axis=-1, keepdims=True)
    spread = jnp.mean(centered * centered, axis=-1, keepdims=True)
    return centered * lax.rsqrt(spread + EPSILON) * gain


def gelu_exact(values):
    return jax.nn.gelu(values, approximate=False)


def visible(segment, seq_count):
    segment_grid = segment.reshape(seq_count, SEQ)
    position = jnp.arange(SEQ)
    causal = position[:, None] >= position[None, :]
    same_doc = segment_grid[:, :, None] == segment_grid[:, None, :]
    return jnp.logical_and(causal[None], same_doc)


def attention_forward(stream, segment, weight, gain_in, gain_mid):
    model_width = stream.shape[1]
    seq_count = stream.shape[0] // SEQ
    head_count = model_width // HEAD_DIM
    normed = layer_norm(stream, gain_in).astype(jnp.bfloat16)
    projected = jnp.dot(
        normed, weight[:, : 3 * model_width], preferred_element_type=jnp.float32
    ).astype(jnp.bfloat16)
    shaped = projected.reshape(seq_count, SEQ, 3, head_count, HEAD_DIM)
    queries = shaped[:, :, 0]
    key_rows = shaped[:, :, 1]
    value_rows = shaped[:, :, 2]
    scores = jnp.einsum(
        "bqhd,bkhd->bhqk", queries, key_rows, preferred_element_type=jnp.float32
    ) * HEAD_DIM ** (-0.5)
    allowed = visible(segment, seq_count)
    scores = jnp.where(allowed[:, None], scores, -1e30)
    row_peak = jnp.max(scores, axis=-1, keepdims=True)
    weights = jnp.exp(scores - row_peak)
    attention = weights / jnp.sum(weights, axis=-1, keepdims=True)
    attention_low = attention.astype(jnp.bfloat16)
    context = jnp.einsum(
        "bhqk,bkhd->bqhd", attention_low, value_rows, preferred_element_type=jnp.float32
    )
    context = context.reshape(-1, model_width)
    inner_normed = layer_norm(context, gain_mid).astype(jnp.bfloat16)
    branch = jnp.dot(
        inner_normed, weight[:, 3 * model_width :], preferred_element_type=jnp.float32
    ).astype(jnp.bfloat16)
    return (
        branch,
        (normed, queries, key_rows, value_rows, attention, attention_low, context, inner_normed),
    )


def attention_backward(stream, segment, weight, gain_in, gain_mid, upstream):
    model_width = stream.shape[1]
    seq_count = stream.shape[0] // SEQ
    head_count = model_width // HEAD_DIM
    scale = HEAD_DIM ** (-0.5)
    branch, kept = attention_forward(stream, segment, weight, gain_in, gain_mid)
    normed, queries, key_rows, value_rows, attention, attention_low, context, inner_normed = kept
    branch_grad = upstream.astype(jnp.bfloat16)
    out_weight_grad = jnp.einsum(
        "tc,td->cd", inner_normed, branch_grad, preferred_element_type=jnp.float32
    )
    inner_grad = jnp.einsum(
        "td,cd->tc", branch_grad, weight[:, 3 * model_width :], preferred_element_type=jnp.float32
    )
    unused_value, mid_pull = jax.vjp(layer_norm, context, gain_mid)
    context_grad, mid_gain_grad = mid_pull(inner_grad)
    context_low = context_grad.astype(jnp.bfloat16).reshape(seq_count, SEQ, head_count, HEAD_DIM)
    prob_grad = jnp.einsum(
        "bqhd,bkhd->bhqk", context_low, value_rows, preferred_element_type=jnp.float32
    )
    value_grad = jnp.einsum(
        "bhqk,bqhd->bkhd", attention_low, context_low, preferred_element_type=jnp.float32
    )
    score_grad = attention * (prob_grad - jnp.sum(attention * prob_grad, axis=-1, keepdims=True))
    score_low = score_grad.astype(jnp.bfloat16)
    query_grad = (
        jnp.einsum("bhqk,bkhd->bqhd", score_low, key_rows, preferred_element_type=jnp.float32)
        * scale
    )
    key_grad = (
        jnp.einsum("bhqk,bqhd->bkhd", score_low, queries, preferred_element_type=jnp.float32)
        * scale
    )
    projected_grad = jnp.stack([query_grad, key_grad, value_grad], axis=2).astype(jnp.bfloat16)
    projected_grad = projected_grad.reshape(-1, 3 * model_width)
    in_weight_grad = jnp.einsum(
        "tc,td->cd", normed, projected_grad, preferred_element_type=jnp.float32
    )
    normed_grad = jnp.einsum(
        "td,cd->tc",
        projected_grad,
        weight[:, : 3 * model_width],
        preferred_element_type=jnp.float32,
    )
    unused_front, front_pull = jax.vjp(layer_norm, stream, gain_in)
    stream_grad, front_gain_grad = front_pull(normed_grad)
    weight_grad = jnp.concatenate([in_weight_grad, out_weight_grad], axis=1)
    return (stream_grad.astype(jnp.bfloat16), weight_grad, front_gain_grad, mid_gain_grad)


def feed_forward(stream, weight_in, weight_out, gain_in, gain_mid):
    normed = layer_norm(stream, gain_in).astype(jnp.bfloat16)
    hidden = jnp.dot(normed, weight_in, preferred_element_type=jnp.float32)
    activated = gelu_exact(hidden)
    inner_normed = layer_norm(activated, gain_mid).astype(jnp.bfloat16)
    branch = jnp.dot(inner_normed, weight_out, preferred_element_type=jnp.float32).astype(
        jnp.bfloat16
    )
    return (branch, (normed, hidden, activated, inner_normed))


def feed_backward(stream, weight_in, weight_out, gain_in, gain_mid, upstream):
    branch, kept = feed_forward(stream, weight_in, weight_out, gain_in, gain_mid)
    normed, hidden, activated, inner_normed = kept
    branch_grad = upstream.astype(jnp.bfloat16)
    out_weight_grad = jnp.einsum(
        "tc,td->cd", inner_normed, branch_grad, preferred_element_type=jnp.float32
    )
    inner_grad = jnp.einsum(
        "td,cd->tc", branch_grad, weight_out, preferred_element_type=jnp.float32
    )
    unused_value, mid_pull = jax.vjp(layer_norm, activated, gain_mid)
    act_grad, mid_gain_grad = mid_pull(inner_grad)
    unused_act, gelu_pull = jax.vjp(gelu_exact, hidden)
    hidden_grad = gelu_pull(act_grad)[0].astype(jnp.bfloat16)
    in_weight_grad = jnp.einsum(
        "tc,td->cd", normed, hidden_grad, preferred_element_type=jnp.float32
    )
    normed_grad = jnp.einsum(
        "td,cd->tc", hidden_grad, weight_in, preferred_element_type=jnp.float32
    )
    unused_front, front_pull = jax.vjp(layer_norm, stream, gain_in)
    stream_grad, front_gain_grad = front_pull(normed_grad)
    return (
        stream_grad.astype(jnp.bfloat16),
        in_weight_grad,
        out_weight_grad,
        front_gain_grad,
        mid_gain_grad,
    )


def accumulate(store, label, value):
    if label in store:
        store[label] = store[label] + value
    else:
        store[label] = value


def generic(tokens, segment_ids, in_proj, out_proj, front_gain, mixer_gain, feed_gain, cotangent):
    own_section = lax.axis_index("section")
    own_weights = in_proj[0]
    layer_total = own_weights.shape[0]
    model_width = front_gain.shape[2]
    hidden_width = feed_gain.shape[1]
    in_store = {}
    out_store = {}
    front_store = {}
    mixer_store = {}
    feed_store = {}

    def run_forward(sublayer, layer_index, stream, segment):
        if sublayer == 0:
            return attention_forward(
                stream,
                segment,
                own_weights[layer_index],
                front_gain[layer_index, 0],
                mixer_gain[layer_index],
            )[0]
        return feed_forward(
            stream,
            own_weights[layer_index],
            out_proj[layer_index],
            front_gain[layer_index, 1],
            feed_gain[layer_index],
        )[0]

    def resting_grads(stream):
        return (
            jnp.zeros(stream.shape, jnp.bfloat16),
            jnp.zeros(own_weights.shape[1:], jnp.float32),
            jnp.zeros(out_proj.shape[1:], jnp.float32),
            jnp.zeros((model_width,), jnp.float32),
            jnp.zeros((model_width,), jnp.float32),
            jnp.zeros((hidden_width,), jnp.float32),
        )

    def run_backward(sublayer, layer_index, stream, segment, upstream):
        if sublayer == 0:
            stream_grad, weight_grad, front_grad, mid_grad = attention_backward(
                stream,
                segment,
                own_weights[layer_index],
                front_gain[layer_index, 0],
                mixer_gain[layer_index],
                upstream,
            )
            return (
                stream_grad,
                weight_grad,
                jnp.zeros(out_proj.shape[1:], jnp.float32),
                front_grad,
                mid_grad,
                jnp.zeros((hidden_width,), jnp.float32),
            )
        stream_grad, in_grad, out_grad, front_grad, mid_grad = feed_backward(
            stream,
            own_weights[layer_index],
            out_proj[layer_index],
            front_gain[layer_index, 1],
            feed_gain[layer_index],
            upstream,
        )
        return (
            stream_grad,
            in_grad,
            out_grad,
            front_grad,
            jnp.zeros((model_width,), jnp.float32),
            mid_grad,
        )

    stream = tokens.astype(jnp.float32)
    upstream = cotangent.astype(jnp.float32)
    kept_streams = []
    for layer_index in range(layer_total):
        for sublayer in (0, 1):
            kept_streams.append(stream)

            def active_forward(stream_in):
                return run_forward(sublayer, layer_index, stream_in, segment_ids)

            def resting_forward(stream_in):
                return jnp.zeros(stream_in.shape, jnp.bfloat16)

            own_branch = lax.cond(own_section == sublayer, active_forward, resting_forward, stream)
            if sublayer == 0:
                received = passed_along(own_branch, "section", 1)
            else:
                received = passed_along(own_branch, "section", -1)
            stream = stream + jnp.where(own_section == sublayer, own_branch, received).astype(
                jnp.float32
            )
    for position in reversed(range(2 * layer_total)):
        layer_index, sublayer = divmod(position, 2)

        def active_backward(operand):
            return run_backward(sublayer, layer_index, operand[0], segment_ids, operand[1])

        def resting_backward(operand):
            return resting_grads(operand[0])

        grads = lax.cond(
            own_section == sublayer,
            active_backward,
            resting_backward,
            (kept_streams[position], upstream),
        )
        own_grad = grads[0]
        accumulate(in_store, layer_index, grads[1])
        accumulate(out_store, layer_index, grads[2])
        accumulate(front_store, (layer_index, sublayer), grads[3])
        accumulate(mixer_store, layer_index, grads[4])
        accumulate(feed_store, layer_index, grads[5])
        if sublayer == 0:
            received = passed_along(own_grad, "section", 1)
        else:
            received = passed_along(own_grad, "section", -1)
        upstream = upstream + jnp.where(own_section == sublayer, own_grad, received).astype(
            jnp.float32
        )
    in_total = jnp.stack([in_store[layer_index] for layer_index in range(layer_total)])
    out_total = jnp.stack([out_store[layer_index] for layer_index in range(layer_total)])
    front_total = jnp.stack(
        [
            jnp.stack([front_store[layer_index, 0], front_store[layer_index, 1]])
            for layer_index in range(layer_total)
        ]
    )
    mixer_total = jnp.stack([mixer_store[layer_index] for layer_index in range(layer_total)])
    feed_total = jnp.stack([feed_store[layer_index] for layer_index in range(layer_total)])
    first_grad = lax.psum_scatter(in_total[None], "rows", scatter_dimension=3, tiled=True)
    partial_sum = lax.psum_scatter(
        out_total.astype(jnp.bfloat16), "section", scatter_dimension=2, tiled=True
    ).astype(jnp.float32)
    second_grad = lax.psum_scatter(partial_sum, "rows", scatter_dimension=1, tiled=True)
    gain_totals = lax.psum((front_total, mixer_total, feed_total), ("section", "rows"))
    return (
        stream.astype(jnp.bfloat16),
        upstream.astype(jnp.bfloat16),
        first_grad,
        second_grad,
        gain_totals[0],
        gain_totals[1],
        gain_totals[2],
    )


def solution(mesh):
    local = fused if mesh.shape["rows"] == 16 and mesh.shape["section"] == 2 else generic
    return jax.shard_map(
        local,
        mesh=mesh,
        in_specs=(
            P("rows", None),
            P("rows"),
            P("section", None, None, None),
            P(),
            P(),
            P(),
            P(),
            P("rows", None),
        ),
        out_specs=(
            P("rows", None),
            P("rows", None),
            P("section", None, None, "rows"),
            P(None, "rows", "section"),
            P(),
            P(),
            P(),
        ),
        check_vma=False,
    )
```

```python
import jax
import jax.numpy as jnp
from jax import lax
from jax.experimental import pallas as pl
from jax.experimental.pallas import tpu as pltpu
from jax.sharding import PartitionSpec as P

HEAD_DIM = 64
SEQ = 128
EPSILON = 1e-05
MESH = pl.DeviceIdType.MESH
BF = jnp.bfloat16
F32 = jnp.float32


def dot(a, b, ca, cb):
    return lax.dot_general(a, b, (((ca,), (cb,)), ((), ())), preferred_element_type=F32)


def fold(v):
    parts = [v[:, i : i + 128] for i in range(0, v.shape[1], 128)]
    total = parts[0]
    for part in parts[1:]:
        total = total + part
    return total


def hat(v):
    centered = v - jnp.mean(v, axis=-1, keepdims=True)
    rs = lax.rsqrt(jnp.mean(centered * centered, axis=-1, keepdims=True) + EPSILON)
    return centered * rs, rs


def hat_back(xh, rs, dxh):
    m1 = jnp.mean(dxh, axis=-1, keepdims=True)
    m2 = jnp.mean(dxh * xh, axis=-1, keepdims=True)
    return rs * (dxh - m1 - xh * m2)


def flip(bit, by):
    return 1 - bit if by else bit


AX, AM, AY = range(3)


def body(
    tok, seg, in_hbm, out_hbm, gf, gm, gff, cot,
    lay_o, inp_o, gi_o, go_o, gain_o,
    W, WO, XS, YS, XR, YR, R2, R3, R4, FN, BG, SR, FG, RC, RX, RH,
    QKV, PB, CTX, ST, UP, XH, GP, RSB, BIG, HG, ORCV, LB, GI, GO, GS, GR,
    wsem, wsend, wosem, isend, irecv, s2s, s2r, s3s, s3r, s4s, s4r,
    fsend, frecv, f1s, f1r, f2s, f2r, f3s, f3r, gss, gsr, tss, tsr, tksem, osem,
):
    s = lax.axis_index("section")
    r = lax.axis_index("rows")
    x = lax.rem(r, 2)
    y = lax.rem(r // 2, 2)
    zl = lax.rem(r // 4, 2)
    zh = r // 8
    dx, dy, dl, dh = 1 - 2 * x, 2 - 4 * y, 4 - 8 * zl, 8 - 16 * zh
    rx, ry, rl, rh = r + dx, r + dy, r + dl, r + dh
    share_bit, share_row, across_row = (zh, zl), (rh, rl), (r + dy + dh, r + dy + dl)
    rest_bit, rest_row = (zl, zh), (rl, rh)
    other = 1 - s
    pending = []

    def remote(src, dst, ssem, rsem, sec, row):
        return pltpu.make_async_remote_copy(
            src_ref=src, dst_ref=dst, send_sem=ssem, recv_sem=rsem, device_id=(sec, row), device_id_type=MESH
        )

    me = pl.ds(pl.multiple_of(s * 128, 128), 128)
    kf = [2 * y + bit for bit in share_bit]
    tok_in = pltpu.make_async_copy(tok.at[me, :], XS.at[0, 0], tksem.at[0])
    cot_in = pltpu.make_async_copy(cot.at[me, :], BG.at[1, kf[1]], tksem.at[1])
    tok_in.start()
    cot_in.start()
    for l in range(2):
        for j in range(4):
            cols = pl.ds(768 * j, 768)
            pltpu.make_async_copy(in_hbm.at[0, l, :, cols], W.at[s, l, :, cols], wsem.at[s, l, j]).start()
    wo = [pltpu.make_async_copy(out_hbm.at[l], WO.at[l], wosem.at[l]) for l in range(2)]
    wo[0].start()
    wo[1].start()

    barrier = pltpu.get_barrier_semaphore()
    peers = [(other, r), (0, rx), (1, rx), (s, ry), (s, rl), (s, rh), (s, across_row[0]), (s, across_row[1])]
    for peer in peers:
        pl.semaphore_signal(barrier, inc=1, device_id=peer, device_id_type=MESH)
    pl.semaphore_wait(barrier, len(peers))

    for l in range(2):
        for j in range(4):
            cols = pl.ds(768 * j, 768)
            cp = remote(in_hbm.at[0, l, :, cols], W.at[s, l, :, cols], wsend.at[l, j], wsem.at[s, l, j], other, r)
            cp.start()
            pending.append((None, cp))

    def wait_w(sec, l, j):
        cols = pl.ds(768 * j, 768)
        pltpu.make_async_copy(in_hbm.at[0, l, :, cols], W.at[sec, l, :, cols], wsem.at[sec, l, j]).wait()

    ka = 2 * x + s

    def exchange(item, l, own, far, dst):
        @pl.when(s == 0)
        def _():
            pltpu.make_async_copy(own, dst.at[ka], irecv.at[l, item, ka]).start()

        cp_own = remote(own, dst.at[ka], isend.at[l, item, 0], irecv.at[l, item, ka], 0, r)
        cp_far = remote(far, dst.at[ka], isend.at[l, item, 1], irecv.at[l, item, ka], 0, rx)
        cp_far.start()
        pl.when(s == 1)(cp_own.start)
        pending.append((None, cp_far))
        pending.append((s == 1, cp_own))

    def wait_item(l, item, dst):
        for k in range(4):
            pltpu.make_async_copy(dst.at[k], dst.at[k], irecv.at[l, item, k]).wait()

    def send_normed(l):
        exchange(AX, l, XS.at[0, l], XS.at[0, l], XR.at[l, 0])

    def send_mixer(l):
        exchange(AM, l, XS.at[1, l], XS.at[1, l], XR.at[l, 1])

    def send_ya(l):
        exchange(AY, l, YS.at[l, :, :, :, x], YS.at[l, :, :, :, 1 - x], YR.at[l])

    def store_y(l, c, block):
        turned = block.T
        YS[l, c // 4, (c // 2) % 2, c % 2, 0] = turned[:192]
        YS[l, c // 4, (c // 2) % 2, c % 2, 1] = turned[192:]


    def share(item, l, buf):
        for p, row in enumerate((ry, share_row[l], across_row[l])):
            own = buf.at[l, kf[l]]
            cp = remote(own, own, fsend.at[l, item, p], frecv.at[l, item, kf[l]], s, row)
            cp.start()
            pending.append((None, cp))

    lane = lax.broadcasted_iota(jnp.int32, (1, 128), 1)
    mk0 = jnp.where(lane < 64, 1.0, 0.0).astype(BF)
    mk1 = jnp.where(lane < 64, 0.0, 1.0).astype(BF)

    def allowed():
        ids = jnp.broadcast_to(seg[pl.ds(s, 1), :], (128, 128))
        row = lax.broadcasted_iota(jnp.int32, (128, 128), 0)
        col = lax.broadcasted_iota(jnp.int32, (128, 128), 1)
        one = jnp.logical_and(ids == ids.T, row >= col)
        return jnp.concatenate([one, one], axis=0)

    def split0(v):
        return jnp.concatenate([v * mk0, v * mk1], axis=0)

    scale = HEAD_DIM ** (-0.5)
    width = 3072.0

    def attention_forward(l):
        stream = ST[2 * l]
        xh, rs = hat(stream)
        XS[0, l] = (xh * gf[l, 0:1, :]).astype(BF)
        send_normed(l)
        for j in range(3):
            wait_w(0, l, j)
            for i in range(2):
                c = 768 * j + 384 * i
                part = dot(XS[0, l], W[0, l, :, c : c + 384], 1, 0).astype(BF)
                for p in range(3):
                    QKV[l, c // 128 + p] = part[:, 128 * p : 128 * p + 128]
        visible = allowed()

        def pair(p):
            q, k, v = QKV[l, p], QKV[l, 6 + p], QKV[l, 12 + p]
            scores = dot(split0(q), k, 1, 1) * scale
            scores = jnp.where(visible, scores, -1e30)
            e = jnp.exp(scores - jnp.max(scores, axis=-1, keepdims=True))
            probs = e * (1.0 / jnp.sum(e, axis=-1, keepdims=True))
            low = probs.astype(BF)
            PB[l, p] = low
            both = jnp.concatenate([low[:128], low[128:]], axis=1)
            return dot(both, split0(v), 1, 0)

        for p in range(6):
            CTX[l, :, 128 * p : 128 * p + 128] = pair(p)
        xh, rs = hat(CTX[l])
        XS[1, l] = (xh * gm[l : l + 1, :]).astype(BF)
        send_mixer(l)
        wait_w(0, l, 3)
        branch = dot(XS[1, l], W[0, l, :, 2304:], 1, 0).astype(BF)
        ST[2 * l + 1] = stream + branch.astype(F32)

    def feed_forward(l):
        stream = ST[2 * l + 1]
        xh, rs = hat(stream)
        FN[l, kf[l]] = (xh * gf[l, 1:2, :]).astype(BF)
        share(0, l, FN)

        def hidden(j, total):
            for i in range(2):
                c = pl.ds(pl.multiple_of(768 * j + 384 * i, 384), 384)
                h = dot(FN[l, kf[l]], W[1, l, :, c], 1, 0)
                phi = 0.5 + 0.5 * lax.erf(h * (0.5**0.5))
                act = h * phi
                BIG[:, c] = act
                GP[l, :, c] = (phi + h * (jnp.exp(-0.5 * h * h) * 0.3989422804014327)).astype(BF)
                total = total + fold(act)
            return total

        total = jnp.zeros((128, 128), F32)
        for j in range(4):
            wait_w(1, l, j)
            total = hidden(j, total)
        mu = jnp.sum(total, axis=-1, keepdims=True) / width

        def spread(c, acc):
            cen = BIG[:, pl.ds(pl.multiple_of(384 * c, 384), 384)] - mu
            return acc + fold(cen * cen)

        acc = lax.fori_loop(0, 8, spread, jnp.zeros((128, 128), F32))
        rs = lax.rsqrt(jnp.sum(acc, axis=-1, keepdims=True) / width + EPSILON)
        RSB[l] = jnp.where(lane == 0, mu, rs)

        def scaled(c, carry):
            cols = pl.ds(pl.multiple_of(384 * c, 384), 384)
            xh = (BIG[:, cols] - mu) * rs
            XH[l, :, cols] = xh.astype(BF)
            HG[:, cols] = (xh * gff[l : l + 1, cols]).astype(BF)
            return carry

        lax.fori_loop(0, 8, scaled, 0)
        wo[l].wait()
        for n in range(0, 768, 256):
            branch = dot(HG[...], WO[l, :, n : n + 256], 1, 0).astype(BF)
            out = stream[:, n : n + 256] + branch.astype(F32)
            if l == 0:
                ST[2, :, n : n + 256] = out
            else:
                LB[0, :, n : n + 256] = out.astype(BF)

    held = {}

    def feed_backward_0(l):
        def first(c, carry):
            a1, a2 = carry
            for i in range(2):
                at = 384 * (2 * c + i)
                cols = pl.ds(pl.multiple_of(at, 384), 384)
                ig = dot(BG[l, kf[l]], WO[l, cols, :], 1, 1)
                xh = XH[l, :, cols].astype(F32)
                GS[0, pl.ds(6 + 4 * l + c, 1), 384 * i : 384 * i + 384] = jnp.sum(ig * xh, axis=0, keepdims=True)
                dxh = ig * gff[l : l + 1, cols]
                BIG[:, cols] = dxh
                a1 = a1 + fold(dxh)
                a2 = a2 + fold(dxh * xh)
            return a1, a2

        zero = jnp.zeros((128, 128), F32)
        a1, a2 = lax.fori_loop(0, 4, first, (zero, zero))
        m1 = jnp.sum(a1, axis=-1, keepdims=True) / width
        m2 = jnp.sum(a2, axis=-1, keepdims=True) / width
        kept = RSB[l]
        rs = kept[:, 1:2]
        stats = jnp.where(lane < 2, kept, jnp.where(lane == 2, m1, m2))
        SR[l, kf[l]] = stats.T[0:8]
        share(2, l, SR)
        held[l] = m1, m2, rs

    def feed_backward_1(l):
        m1, m2, rs = held[l]

        def second(c, carry):
            cols = pl.ds(pl.multiple_of(384 * c, 384), 384)
            da = rs * (BIG[:, cols] - m1 - XH[l, :, cols].astype(F32) * m2)
            HG[:, cols] = (GP[l, :, cols].astype(F32) * da).astype(BF)
            return carry

        lax.fori_loop(0, 8, second, 0)
        for n in range(0, 768, 256):
            BIG[:, n : n + 256] = dot(HG[...], W[1, l, n : n + 256, :], 1, 1)
        front_back(l, 1)

    def front_back(l, sub):
        ng = BIG[:, 0:768]
        xh, rs = hat(ST[2 * l + sub])
        GS[0, 2 * l + sub : 2 * l + sub + 1, :] = jnp.sum(ng * xh, axis=0, keepdims=True)
        UP[...] = UP[...] + hat_back(xh, rs, ng * gf[l, sub : sub + 1, :]).astype(BF).astype(F32)

    def attention_pair_back(l, p):
        q, k, v = QKV[l, p], QKV[l, 6 + p], QKV[l, 12 + p]
        probs_low = PB[l, p]
        probs = probs_low.astype(F32)
        dcc = split0(HG[:, 2304 + 128 * p : 2432 + 128 * p])
        pg = dot(dcc, v, 1, 1)
        ds = (probs * (pg - jnp.sum(probs * pg, axis=-1, keepdims=True))).astype(BF)
        both = jnp.concatenate([ds[:128], ds[128:]], axis=1)
        dq = dot(both, split0(k), 1, 0) * scale
        dk = dot(ds, split0(q), 0, 0) * scale
        dv = dot(probs_low, dcc, 0, 0)
        return dq.astype(BF), dk.astype(BF), dv.astype(BF)

    def attention_group_back(l, g):
        parts = [attention_pair_back(l, 3 * g + i) for i in range(3)]
        for which in range(3):
            block = jnp.concatenate([part[which] for part in parts], axis=1)
            at = 768 * which + 384 * g
            HG[:, at : at + 384] = block
            store_y(l, 2 * which + g, block)

    def attention_backward_0(l):
        low = UP[...].astype(BF)
        for i in range(2):
            store_y(l, 6 + i, low[:, 384 * i : 384 * i + 384])
        for n in range(0, 768, 256):
            BIG[:, n : n + 256] = dot(low, W[0, l, n : n + 256, 2304:], 1, 1)
        ig = BIG[:, 0:768]
        xh, rs = hat(CTX[l])
        GS[0, 4 + l : 5 + l, :] = jnp.sum(ig * xh, axis=0, keepdims=True)
        dctx = hat_back(xh, rs, ig * gm[l : l + 1, :]).astype(BF)
        HG[:, 2304:] = dctx
        attention_group_back(l, 0)

    def attention_backward_1(l):
        attention_group_back(l, 1)
        send_ya(l)

    def attention_backward_2(l):
        for n in range(0, 768, 256):
            BIG[:, n : n + 256] = dot(HG[:, 0:2304], W[0, l, n : n + 256, 0:2304], 1, 1)
        front_back(l, 0)

    def g_at(l, n):
        return W.at[1 - l, 1, pl.ds(384 + 192 * (n // 4), 192), pl.ds(768 * (n % 4), 768)]

    def piece(b2, b3, r4):
        return 4 * b2 + 2 * b3 + 1 if r4 else 2 * b2 + 4 * b3

    def a2_copy(l, b3, r4):
        at = 2 * b3 + r4
        src = g_at(l, piece(1, b3, r4))
        return remote(src, R2.at[l, at], s2s.at[l, at], s2r.at[l, at], 0, ry if r4 else rl)

    def a3_copy(l, r4):
        src = g_at(l, piece(0, 1, r4))
        return remote(src, R3.at[l, r4], s3s.at[l, r4], s3r.at[l, r4], 0, rl if r4 else ry)

    def a4_copy(l):
        return remote(g_at(l, 1), R4.at[l], s4s.at[l], s4r.at[l], 0, rh)

    def a_job(l):
        wait_item(l, AX, XR.at[l, 0])
        wait_item(l, AM, XR.at[l, 1])
        wait_item(l, AY, YR.at[l])
        for r4, r3 in ((1, 1), (1, 0), (0, 1), (0, 0)):
            h, low = flip(zh, r4), flip(zl, r3)
            xi = h * low
            rows = []
            for r2 in (1, 0):
                rows.append(jnp.concatenate([YR[l, k, h, low, flip(y, r2)] for k in range(4)], axis=1))
            lhs = jnp.concatenate(rows, axis=0)
            for n in range(0, 768, 256):
                res = dot(lhs, XR[l, xi, :, :, n : n + 256].reshape(512, 256), 1, 0).astype(BF)
                g_at(l, 4 + 2 * r3 + r4)[:, n : n + 256] = res[:192]
                g_at(l, 2 * r3 + r4)[:, n : n + 256] = res[192:]
            if r4 == 1:
                a2_copy(l, r3, 1).start()
            elif r3 == 1:
                a2_copy(l, 1, 0).start()
                a2_copy(l, 0, 0).start()

    def a_stage2(l, b3, r4):
        a2_copy(l, b3, r4).wait_recv()
        g = g_at(l, piece(0, b3, r4))
        g[...] = (g[...].astype(F32) + R2[l, 2 * b3 + r4].astype(F32)).astype(BF)
        if b3 == 1:
            a3_copy(l, r4).start()

    def a_stage3(l, r4):
        a3_copy(l, r4).wait_recv()
        g = g_at(l, r4)
        g[...] = (g[...].astype(F32) + R3[l, r4].astype(F32)).astype(BF)
        if r4 == 1:
            a4_copy(l).start()

    def a_stage4(l):
        a4_copy(l).wait_recv()
        GI[l] = (g_at(l, 0)[...].astype(F32) + R4[l].astype(F32)).astype(BF)
        gi_copy(l).start()

    def a_sent(l):
        for b3 in range(2):
            for r4 in range(2):
                a2_copy(l, b3, r4).wait_send()
        for r4 in range(2):
            a3_copy(l, r4).wait_send()
        a4_copy(l).wait_send()

    def f_at(l, which, q):
        return W.at[l, 1, pl.ds(0, 384), pl.ds(pl.multiple_of(768 * (2 * which + q), 768), 768)]

    def f_rows(half, chunk=None):
        if chunk is None:
            return pl.ds(pl.multiple_of(192 * half, 192), 192)
        return pl.ds(pl.multiple_of(192 * half + 96 * chunk, 96), 96)

    def f1_copy(l, q):
        return remote(f_at(l, other, q), RC.at[l, q], f1s.at[l, q], f1r.at[l, q], other, r)

    def f_step(step):
        return (0, None, pl.ds(0, 192)) if step == 0 else (1, step - 1, pl.ds(96 * (step - 1), 96))

    def f2_copy(l, step):
        q, chunk, rows = f_step(step)
        src = f_at(l, s, q).at[f_rows(1 - x, chunk), :]
        return remote(src, RX.at[l, q, rows, :], f2s.at[l, step], f2r.at[l, step], s, rx)

    def f3_copy(l, chunk):
        src = f_at(l, s, 1).at[f_rows(x, chunk), :]
        return remote(src, RH.at[l, pl.ds(96 * chunk, 96), :], f3s.at[l, chunk], f3r.at[l, chunk], s, rest_row[l])

    def f_job(l):
        def source(i, carry):
            along_y, along_z = i // 2, lax.rem(i, 2)
            bit = share_bit[l]
            k = 2 * (y + along_y - 2 * y * along_y) + bit + along_z - 2 * bit * along_z

            @pl.when(i > 0)
            def _():
                for item, buf in enumerate((FN, BG, SR)):
                    pltpu.make_async_copy(buf.at[l, k], buf.at[l, k], frecv.at[l, item, k]).wait()

            stats = jnp.concatenate([SR[l, k]] * 16, axis=0).T
            mu, rs, m1, m2 = (stats[:, n : n + 1] for n in range(4))
            for q in (1, 0):
                rest = flip(rest_bit[l], q)
                c = (4 * rest + 2 * zl if l == 1 else 4 * zh + 2 * rest) + y
                cols = pl.ds(pl.multiple_of(384 * c, 384), 384)
                gain = gff[l : l + 1, cols]
                h = dot(FN[l, k], W[1, l, :, cols], 1, 0)
                phi = 0.5 + 0.5 * lax.erf(h * (0.5**0.5))
                xh = (h * phi - mu) * rs
                to = pl.ds(pl.multiple_of(768 * k + 384 * q, 384), 384)
                HG[:, to] = (xh * gain).astype(BF)
                ig = dot(BG[l, k], WO[l, cols, :], 1, 1)
                da = rs * (ig * gain - m1 - xh * m2)
                slope = phi + h * (jnp.exp(-0.5 * h * h) * 0.3989422804014327)
                FG[:, to] = (slope * da).astype(BF)
            return carry

        lax.fori_loop(0, 4, source, 0)
        for q in (1, 0):
            for which, (a, b) in enumerate(((HG, BG), (FG, FN))):
                out = f_at(l, which, q)
                lhs = jnp.concatenate([a[:, 768 * k + 384 * q : 768 * k + 384 * q + 384] for k in range(4)], axis=0)
                for n in range(0, 768, 256):
                    out[:, n : n + 256] = dot(lhs, b[l, :, :, n : n + 256].reshape(512, 256), 0, 0).astype(BF)
            f1_copy(l, q).start()

    def f_stage1(l, q):
        f1_copy(l, q).wait_recv()
        g, got = f_at(l, s, q), RC.at[l, q]

        def add(rows):
            g[rows, :] = (g[rows, :].astype(F32) + got[rows, :].astype(F32)).astype(BF)

        for step in (1, 2) if q else (0,):
            add(f_rows(1 - x, f_step(step)[1]))
            f2_copy(l, step).start()
        add(f_rows(x))

    def f_stage2(l, step):
        f2_copy(l, step).wait_recv()
        q, chunk, rows = f_step(step)
        g = f_at(l, s, q).at[f_rows(x, chunk), :]
        g[...] = (g[...].astype(F32) + RX[l, q, rows, :].astype(F32)).astype(BF)
        if q == 1:
            f3_copy(l, chunk).start()

    def gi_copy(l):
        return pltpu.make_async_copy(GI.at[l], gi_o.at[l], osem.at[l])

    def go_copy(l):
        return pltpu.make_async_copy(GO.at[l], go_o.at[l], osem.at[2 + l])

    def rows_copies(n, out):
        own = pltpu.make_async_copy(LB.at[n], out.at[me, :], osem.at[4 + n])
        return own, remote(LB.at[n], out.at[me, :], tss.at[n], tsr.at[n], other, r)

    def rows_out(n, out):
        for copy in rows_copies(n, out):
            copy.start()

    def rows_done(n, out):
        own, away = rows_copies(n, out)
        own.wait()
        away.wait()

    def o_copy(l):
        return remote(RX.at[l, 1, :, pl.ds(0, 384)], ORCV.at[l], tss.at[2 + l], tsr.at[2 + l], other, r)

    def f_stage3(l):
        f3_copy(l, 0).wait_recv()
        f3_copy(l, 1).wait_recv()
        g = f_at(l, s, 0).at[f_rows(x), :]

        def final(lo, hi):
            return g[:, lo:hi].astype(F32) + RH[l, :, lo:hi].astype(F32)

        @pl.when(s == 0)
        def _():
            RX[l, 1, :, 0:384] = final(384, 768).astype(BF)
            o_copy(l).start()
            GO[l] = final(0, 384).astype(BF)
            go_copy(l).start()

        @pl.when(s == 1)
        def _():
            GI[l] = final(0, 768).astype(BF)
            gi_copy(l).start()

    def f_sent(l):
        for q in range(2):
            f1_copy(l, q).wait_send()
            f3_copy(l, q).wait_send()
        for step in range(3):
            f2_copy(l, step).wait_send()

        @pl.when(s == 0)
        def _():
            o_copy(l).wait_send()

    def gain_stage(k):
        to = ((other, r), (s, rl), (s, ry), (s, rh), (s, rx))[k]
        return remote(GS.at[k], GR.at[k], gss.at[k], gsr.at[k], *to)

    def gain_step(k):
        gain_stage(k).wait_recv()
        if k == 4:
            GR[4] = GS[4] + GR[4]
            pltpu.make_async_copy(GR.at[4], gain_o, osem.at[6]).start()
        else:
            GS[k + 1] = GS[k] + GR[k]
            gain_stage(k + 1).start()

    def on0(*steps):
        @pl.when(s == 0)
        def _():
            for step in steps:
                step()

    def operands_sent():
        for cond, cp in pending:
            if cond is None:
                cp.wait_send()
            else:
                pl.when(cond)(cp.wait_send)
        rows_done(0, lay_o)

    cot_in.wait()
    share(1, 1, BG)
    UP[...] = BG[1, kf[1]].astype(F32)
    tok_in.wait()
    ST[0] = XS[0, 0].astype(F32)
    GS[0, 14:16, :] = jnp.zeros((2, 768), F32)

    attention_forward(0)
    feed_forward(0)
    attention_forward(1)
    feed_forward(1)
    rows_out(0, lay_o)

    feed_backward_0(1)
    feed_backward_1(1)
    attention_backward_0(1)
    attention_backward_1(1)
    attention_backward_2(1)
    BG[0, kf[0]] = UP[...].astype(BF)
    share(1, 0, BG)
    f_job(1)
    f_stage1(1, 1)
    feed_backward_0(0)
    on0(lambda: a_job(1))
    feed_backward_1(0)
    f_stage2(1, 1)
    f_stage2(1, 2)
    attention_backward_0(0)
    attention_backward_1(0)
    attention_backward_2(0)
    LB[1] = UP[...].astype(BF)
    rows_out(1, inp_o)
    on0(lambda: a_stage2(1, 1, 1))
    gain_stage(0).start()
    gain_step(0)
    on0(lambda: a_stage2(1, 1, 0))
    f_job(0)
    f_stage1(1, 0)
    on0(lambda: a_job(0))
    gain_step(1)
    on0(lambda: a_stage2(1, 0, 1))
    f_stage1(0, 1)
    on0(lambda: a_stage2(1, 0, 0), lambda: a_stage2(0, 1, 1), lambda: a_stage3(1, 1))
    f_stage1(0, 0)
    on0(lambda: a_stage2(0, 1, 0), lambda: a_stage2(0, 0, 1), lambda: a_stage2(0, 0, 0))
    gain_step(2)
    f_stage2(0, 1)
    f_stage2(1, 0)
    f_stage2(0, 2)
    on0(lambda: a_stage3(0, 1))
    gain_step(3)
    on0(lambda: a_stage3(0, 0), lambda: a_stage3(1, 0))
    operands_sent()
    f_stage2(0, 0)
    on0(lambda: a_stage4(1))
    gain_step(4)
    f_stage3(1)
    f_stage3(0)
    on0(lambda: a_stage4(0))

    @pl.when(s == 1)
    def _():
        for l in (1, 0):
            o_copy(l).wait_recv()
            pltpu.make_async_copy(ORCV.at[l], go_o.at[l], osem.at[2 + l]).start()

    for l in range(2):
        f_sent(l)
        on0(lambda: a_sent(l))
        gi_copy(l).wait()
        go_copy(l).wait()
    for k in range(5):
        gain_stage(k).wait_send()
    pltpu.make_async_copy(GR.at[4], gain_o, osem.at[6]).wait()
    rows_done(1, inp_o)


def hand_over(lay, inp, gi, go, gains, lay_o, inp_o, gi_o, go_o, front_o, mixer_o, feed_o):
    lay_o[...] = lay[...]
    inp_o[...] = inp[...]
    gi_o[...] = gi[...].astype(F32)
    go_o[...] = go[...].astype(F32)
    for l in range(2):
        front_o[l] = gains[2 * l : 2 * l + 2, :]
        for i in range(4):
            feed_o[l : l + 1, 768 * i : 768 * i + 768] = gains[6 + 4 * l + i : 7 + 4 * l + i, :]
    mixer_o[...] = gains[4:6, :]


def fused(tokens, segment_ids, in_proj, out_proj, front_gain, mixer_gain, feed_gain, cotangent):
    vm = pl.BlockSpec(memory_space=pltpu.VMEM)
    hbm = pl.BlockSpec(memory_space=pl.ANY)
    dma = pltpu.SemaphoreType.DMA
    outs = pl.pallas_call(
        body,
        out_shape=(
            jax.ShapeDtypeStruct((256, 768), BF),
            jax.ShapeDtypeStruct((256, 768), BF),
            jax.ShapeDtypeStruct((2, 192, 768), BF),
            jax.ShapeDtypeStruct((2, 192, 384), BF),
            jax.ShapeDtypeStruct((16, 768), F32),
        ),
        in_specs=[hbm, vm, hbm, hbm, vm, vm, vm, hbm],
        out_specs=(hbm,) * 5,
        scratch_shapes=[
            pltpu.VMEM((2, 2, 768, 3072), BF),
            pltpu.VMEM((2, 3072, 768), BF),
            pltpu.VMEM((2, 2, 128, 768), BF),
            pltpu.VMEM((2, 2, 2, 2, 2, 192, 128), BF),
            pltpu.VMEM((2, 2, 4, 128, 768), BF),
            pltpu.VMEM((2, 4, 2, 2, 2, 192, 128), BF),
            pltpu.VMEM((2, 4, 192, 768), BF),
            pltpu.VMEM((2, 2, 192, 768), BF),
            pltpu.VMEM((2, 192, 768), BF),
            pltpu.VMEM((2, 4, 128, 768), BF),
            pltpu.VMEM((2, 4, 128, 768), BF),
            pltpu.VMEM((2, 4, 8, 128), F32),
            pltpu.VMEM((128, 3072), BF),
            pltpu.VMEM((2, 2, 384, 768), BF),
            pltpu.VMEM((2, 2, 192, 768), BF),
            pltpu.VMEM((2, 192, 768), BF),
            pltpu.VMEM((2, 18, 128, 128), BF),
            pltpu.VMEM((2, 6, 256, 128), BF),
            pltpu.VMEM((2, 128, 768), F32),
            pltpu.VMEM((4, 128, 768), F32),
            pltpu.VMEM((128, 768), F32),
            pltpu.VMEM((2, 128, 3072), BF),
            pltpu.VMEM((2, 128, 3072), BF),
            pltpu.VMEM((2, 128, 128), F32),
            pltpu.VMEM((128, 3072), F32),
            pltpu.VMEM((128, 3072), BF),
            pltpu.VMEM((2, 192, 384), BF),
            pltpu.VMEM((2, 128, 768), BF),
            pltpu.VMEM((2, 192, 768), BF),
            pltpu.VMEM((2, 192, 384), BF),
            pltpu.VMEM((5, 16, 768), F32),
            pltpu.VMEM((5, 16, 768), F32),
            dma((2, 2, 4)),
            dma((2, 4)),
            dma((2,)),
            dma((2, 3, 2)),
            dma((2, 3, 4)),
            dma((2, 4)),
            dma((2, 4)),
            dma((2, 2)),
            dma((2, 2)),
            dma((2,)),
            dma((2,)),
            dma((2, 3, 3)),
            dma((2, 3, 4)),
            dma((2, 2)),
            dma((2, 2)),
            dma((2, 3)),
            dma((2, 3)),
            dma((2, 2)),
            dma((2, 2)),
            dma((5,)),
            dma((5,)),
            dma((4,)),
            dma((4,)),
            dma((2,)),
            dma((7,)),
        ],
        compiler_params=pltpu.CompilerParams(
            collective_id=0, has_side_effects=True, vmem_limit_bytes=63 * 2**20
        ),
        name="layers",
    )(
        tokens,
        segment_ids.reshape(2, SEQ),
        in_proj,
        out_proj,
        front_gain,
        mixer_gain,
        feed_gain,
        cotangent,
    )
    layer_out, input_grad, in_turned, out_grad, front, mixer, feed = pl.pallas_call(
        hand_over,
        out_shape=(
            jax.ShapeDtypeStruct((256, 768), BF),
            jax.ShapeDtypeStruct((256, 768), BF),
            jax.ShapeDtypeStruct((2, 192, 768), F32),
            jax.ShapeDtypeStruct((2, 192, 384), F32),
            jax.ShapeDtypeStruct((2, 2, 768), F32),
            jax.ShapeDtypeStruct((2, 768), F32),
            jax.ShapeDtypeStruct((2, 3072), F32),
        ),
        in_specs=[vm] * 5,
        out_specs=(vm,) * 7,
        name="hand_over",
    )(*outs)
    return layer_out, input_grad, jnp.swapaxes(in_turned, 1, 2)[None], out_grad, front, mixer, feed


def passed_along(array, axis, by):
    devices = lax.axis_size(axis)
    pairs = [(i, i + by) for i in range(devices) if 0 <= i + by < devices]
    return lax.ppermute(array, axis, pairs)


def layer_norm(values, gain):
    centered = values - jnp.mean(values, axis=-1, keepdims=True)
    spread = jnp.mean(centered * centered, axis=-1, keepdims=True)
    return centered * lax.rsqrt(spread + EPSILON) * gain


def gelu_exact(values):
    return jax.nn.gelu(values, approximate=False)


def visible(segment, seq_count):
    segment_grid = segment.reshape(seq_count, SEQ)
    position = jnp.arange(SEQ)
    causal = position[:, None] >= position[None, :]
    same_doc = segment_grid[:, :, None] == segment_grid[:, None, :]
    return jnp.logical_and(causal[None], same_doc)


def attention_forward(stream, segment, weight, gain_in, gain_mid):
    model_width = stream.shape[1]
    seq_count = stream.shape[0] // SEQ
    head_count = model_width // HEAD_DIM
    normed = layer_norm(stream, gain_in).astype(jnp.bfloat16)
    projected = jnp.dot(
        normed, weight[:, : 3 * model_width], preferred_element_type=jnp.float32
    ).astype(jnp.bfloat16)
    shaped = projected.reshape(seq_count, SEQ, 3, head_count, HEAD_DIM)
    queries = shaped[:, :, 0]
    key_rows = shaped[:, :, 1]
    value_rows = shaped[:, :, 2]
    scores = jnp.einsum(
        "bqhd,bkhd->bhqk", queries, key_rows, preferred_element_type=jnp.float32
    ) * HEAD_DIM ** (-0.5)
    allowed = visible(segment, seq_count)
    scores = jnp.where(allowed[:, None], scores, -1e30)
    row_peak = jnp.max(scores, axis=-1, keepdims=True)
    weights = jnp.exp(scores - row_peak)
    attention = weights / jnp.sum(weights, axis=-1, keepdims=True)
    attention_low = attention.astype(jnp.bfloat16)
    context = jnp.einsum(
        "bhqk,bkhd->bqhd", attention_low, value_rows, preferred_element_type=jnp.float32
    )
    context = context.reshape(-1, model_width)
    inner_normed = layer_norm(context, gain_mid).astype(jnp.bfloat16)
    branch = jnp.dot(
        inner_normed, weight[:, 3 * model_width :], preferred_element_type=jnp.float32
    ).astype(jnp.bfloat16)
    return (
        branch,
        (normed, queries, key_rows, value_rows, attention, attention_low, context, inner_normed),
    )


def attention_backward(stream, segment, weight, gain_in, gain_mid, upstream):
    model_width = stream.shape[1]
    seq_count = stream.shape[0] // SEQ
    head_count = model_width // HEAD_DIM
    scale = HEAD_DIM ** (-0.5)
    branch, kept = attention_forward(stream, segment, weight, gain_in, gain_mid)
    normed, queries, key_rows, value_rows, attention, attention_low, context, inner_normed = kept
    branch_grad = upstream.astype(jnp.bfloat16)
    out_weight_grad = jnp.einsum(
        "tc,td->cd", inner_normed, branch_grad, preferred_element_type=jnp.float32
    )
    inner_grad = jnp.einsum(
        "td,cd->tc", branch_grad, weight[:, 3 * model_width :], preferred_element_type=jnp.float32
    )
    unused_value, mid_pull = jax.vjp(layer_norm, context, gain_mid)
    context_grad, mid_gain_grad = mid_pull(inner_grad)
    context_low = context_grad.astype(jnp.bfloat16).reshape(seq_count, SEQ, head_count, HEAD_DIM)
    prob_grad = jnp.einsum(
        "bqhd,bkhd->bhqk", context_low, value_rows, preferred_element_type=jnp.float32
    )
    value_grad = jnp.einsum(
        "bhqk,bqhd->bkhd", attention_low, context_low, preferred_element_type=jnp.float32
    )
    score_grad = attention * (prob_grad - jnp.sum(attention * prob_grad, axis=-1, keepdims=True))
    score_low = score_grad.astype(jnp.bfloat16)
    query_grad = (
        jnp.einsum("bhqk,bkhd->bqhd", score_low, key_rows, preferred_element_type=jnp.float32)
        * scale
    )
    key_grad = (
        jnp.einsum("bhqk,bqhd->bkhd", score_low, queries, preferred_element_type=jnp.float32)
        * scale
    )
    projected_grad = jnp.stack([query_grad, key_grad, value_grad], axis=2).astype(jnp.bfloat16)
    projected_grad = projected_grad.reshape(-1, 3 * model_width)
    in_weight_grad = jnp.einsum(
        "tc,td->cd", normed, projected_grad, preferred_element_type=jnp.float32
    )
    normed_grad = jnp.einsum(
        "td,cd->tc",
        projected_grad,
        weight[:, : 3 * model_width],
        preferred_element_type=jnp.float32,
    )
    unused_front, front_pull = jax.vjp(layer_norm, stream, gain_in)
    stream_grad, front_gain_grad = front_pull(normed_grad)
    weight_grad = jnp.concatenate([in_weight_grad, out_weight_grad], axis=1)
    return (stream_grad.astype(jnp.bfloat16), weight_grad, front_gain_grad, mid_gain_grad)


def feed_forward(stream, weight_in, weight_out, gain_in, gain_mid):
    normed = layer_norm(stream, gain_in).astype(jnp.bfloat16)
    hidden = jnp.dot(normed, weight_in, preferred_element_type=jnp.float32)
    activated = gelu_exact(hidden)
    inner_normed = layer_norm(activated, gain_mid).astype(jnp.bfloat16)
    branch = jnp.dot(inner_normed, weight_out, preferred_element_type=jnp.float32).astype(
        jnp.bfloat16
    )
    return (branch, (normed, hidden, activated, inner_normed))


def feed_backward(stream, weight_in, weight_out, gain_in, gain_mid, upstream):
    branch, kept = feed_forward(stream, weight_in, weight_out, gain_in, gain_mid)
    normed, hidden, activated, inner_normed = kept
    branch_grad = upstream.astype(jnp.bfloat16)
    out_weight_grad = jnp.einsum(
        "tc,td->cd", inner_normed, branch_grad, preferred_element_type=jnp.float32
    )
    inner_grad = jnp.einsum(
        "td,cd->tc", branch_grad, weight_out, preferred_element_type=jnp.float32
    )
    unused_value, mid_pull = jax.vjp(layer_norm, activated, gain_mid)
    act_grad, mid_gain_grad = mid_pull(inner_grad)
    unused_act, gelu_pull = jax.vjp(gelu_exact, hidden)
    hidden_grad = gelu_pull(act_grad)[0].astype(jnp.bfloat16)
    in_weight_grad = jnp.einsum(
        "tc,td->cd", normed, hidden_grad, preferred_element_type=jnp.float32
    )
    normed_grad = jnp.einsum(
        "td,cd->tc", hidden_grad, weight_in, preferred_element_type=jnp.float32
    )
    unused_front, front_pull = jax.vjp(layer_norm, stream, gain_in)
    stream_grad, front_gain_grad = front_pull(normed_grad)
    return (
        stream_grad.astype(jnp.bfloat16),
        in_weight_grad,
        out_weight_grad,
        front_gain_grad,
        mid_gain_grad,
    )


def accumulate(store, label, value):
    if label in store:
        store[label] = store[label] + value
    else:
        store[label] = value


def generic(tokens, segment_ids, in_proj, out_proj, front_gain, mixer_gain, feed_gain, cotangent):
    own_section = lax.axis_index("section")
    own_weights = in_proj[0]
    layer_total = own_weights.shape[0]
    model_width = front_gain.shape[2]
    hidden_width = feed_gain.shape[1]
    in_store = {}
    out_store = {}
    front_store = {}
    mixer_store = {}
    feed_store = {}

    def run_forward(sublayer, layer_index, stream, segment):
        if sublayer == 0:
            return attention_forward(
                stream,
                segment,
                own_weights[layer_index],
                front_gain[layer_index, 0],
                mixer_gain[layer_index],
            )[0]
        return feed_forward(
            stream,
            own_weights[layer_index],
            out_proj[layer_index],
            front_gain[layer_index, 1],
            feed_gain[layer_index],
        )[0]

    def resting_grads(stream):
        return (
            jnp.zeros(stream.shape, jnp.bfloat16),
            jnp.zeros(own_weights.shape[1:], jnp.float32),
            jnp.zeros(out_proj.shape[1:], jnp.float32),
            jnp.zeros((model_width,), jnp.float32),
            jnp.zeros((model_width,), jnp.float32),
            jnp.zeros((hidden_width,), jnp.float32),
        )

    def run_backward(sublayer, layer_index, stream, segment, upstream):
        if sublayer == 0:
            stream_grad, weight_grad, front_grad, mid_grad = attention_backward(
                stream,
                segment,
                own_weights[layer_index],
                front_gain[layer_index, 0],
                mixer_gain[layer_index],
                upstream,
            )
            return (
                stream_grad,
                weight_grad,
                jnp.zeros(out_proj.shape[1:], jnp.float32),
                front_grad,
                mid_grad,
                jnp.zeros((hidden_width,), jnp.float32),
            )
        stream_grad, in_grad, out_grad, front_grad, mid_grad = feed_backward(
            stream,
            own_weights[layer_index],
            out_proj[layer_index],
            front_gain[layer_index, 1],
            feed_gain[layer_index],
            upstream,
        )
        return (
            stream_grad,
            in_grad,
            out_grad,
            front_grad,
            jnp.zeros((model_width,), jnp.float32),
            mid_grad,
        )

    stream = tokens.astype(jnp.float32)
    upstream = cotangent.astype(jnp.float32)
    kept_streams = []
    for layer_index in range(layer_total):
        for sublayer in (0, 1):
            kept_streams.append(stream)

            def active_forward(stream_in):
                return run_forward(sublayer, layer_index, stream_in, segment_ids)

            def resting_forward(stream_in):
                return jnp.zeros(stream_in.shape, jnp.bfloat16)

            own_branch = lax.cond(own_section == sublayer, active_forward, resting_forward, stream)
            if sublayer == 0:
                received = passed_along(own_branch, "section", 1)
            else:
                received = passed_along(own_branch, "section", -1)
            stream = stream + jnp.where(own_section == sublayer, own_branch, received).astype(
                jnp.float32
            )
    for position in reversed(range(2 * layer_total)):
        layer_index, sublayer = divmod(position, 2)

        def active_backward(operand):
            return run_backward(sublayer, layer_index, operand[0], segment_ids, operand[1])

        def resting_backward(operand):
            return resting_grads(operand[0])

        grads = lax.cond(
            own_section == sublayer,
            active_backward,
            resting_backward,
            (kept_streams[position], upstream),
        )
        own_grad = grads[0]
        accumulate(in_store, layer_index, grads[1])
        accumulate(out_store, layer_index, grads[2])
        accumulate(front_store, (layer_index, sublayer), grads[3])
        accumulate(mixer_store, layer_index, grads[4])
        accumulate(feed_store, layer_index, grads[5])
        if sublayer == 0:
            received = passed_along(own_grad, "section", 1)
        else:
            received = passed_along(own_grad, "section", -1)
        upstream = upstream + jnp.where(own_section == sublayer, own_grad, received).astype(
            jnp.float32
        )
    in_total = jnp.stack([in_store[layer_index] for layer_index in range(layer_total)])
    out_total = jnp.stack([out_store[layer_index] for layer_index in range(layer_total)])
    front_total = jnp.stack(
        [
            jnp.stack([front_store[layer_index, 0], front_store[layer_index, 1]])
            for layer_index in range(layer_total)
        ]
    )
    mixer_total = jnp.stack([mixer_store[layer_index] for layer_index in range(layer_total)])
    feed_total = jnp.stack([feed_store[layer_index] for layer_index in range(layer_total)])
    first_grad = lax.psum_scatter(in_total[None], "rows", scatter_dimension=3, tiled=True)
    partial_sum = lax.psum_scatter(
        out_total.astype(jnp.bfloat16), "section", scatter_dimension=2, tiled=True
    ).astype(jnp.float32)
    second_grad = lax.psum_scatter(partial_sum, "rows", scatter_dimension=1, tiled=True)
    gain_totals = lax.psum((front_total, mixer_total, feed_total), ("section", "rows"))
    return (
        stream.astype(jnp.bfloat16),
        upstream.astype(jnp.bfloat16),
        first_grad,
        second_grad,
        gain_totals[0],
        gain_totals[1],
        gain_totals[2],
    )


def solution(mesh):
    local = fused if mesh.shape["rows"] == 16 and mesh.shape["section"] == 2 else generic
    return jax.shard_map(
        local,
        mesh=mesh,
        in_specs=(
            P("rows", None),
            P("rows"),
            P("section", None, None, None),
            P(),
            P(),
            P(),
            P(),
            P("rows", None),
        ),
        out_specs=(
            P("rows", None),
            P("rows", None),
            P("section", None, None, "rows"),
            P(None, "rows", "section"),
            P(),
            P(),
            P(),
        ),
        check_vma=False,
    )
```
